32 devices in a mesh: mp: 4 (over x, core), ctx: 8 (over z, y).
Axes of the slice: x: 2, y: 2, z: 4, core: 2. Of those that a mesh axis runs over, the one named last changes fastest.
Arguments:
- queries: bfloat16 [32768, 1024], P(('mp', 'ctx')), parts along dimension 0, may hold values from -6 to 6
- key_rows: bfloat16 [32768, 1024], P(('mp', 'ctx')), parts along dimension 0, may hold values from -6 to 6
- value_rows: bfloat16 [32768, 1024], P(('mp', 'ctx')), parts along dimension 0, may hold values from -6 to 6
- conv_weight: float32 [12, 4, 1024], P('mp'), parts along dimension 0, may hold values from -3 to 3
- head_gain: float32 [4096], P('mp'), parts along dimension 0, may hold values from 0.1 to 1.9
Outputs:
- attended: bfloat16 [32768, 1024], P(('mp', 'ctx')), parts along dimension 0
The draws below stay inside these ranges and needn't reach their ends.
There are 4 independent parts, one for each index of `mp`. The reference program is written for one: setup_inputs(seed, part) draws one part's arguments, and reference() takes and returns one part's arrays. A program takes and returns all parts, laid end to end along the dimension named above; each array names one. Nothing has to cross between parts.
All inputs are finite; a program needn't handle non-finite values.
Results may differ from the reference program's by a relative error of at most 0.006.
Values may be sent and summed in bfloat16 or wider, within the bound.
No kernel may reach another device: no remote copies, remote signals or barrier semaphores. Data moves between devices by JAX's collectives and lax.ppermute only.
A program may use at most 128 MiB of HBM per device.

```python
import jax
import jax.numpy as jnp
from jax import lax

HEADS = 8
HDIM = 128
CONV = 4
TOK_DEV = 1024
HD = 1024
TOKENS = 8192
N_CTX = 8


def block_levels(stream_key, extent, cuts, low, top_value):
    loudness, own = 1.0, jax.random.fold_in(stream_key, 6)
    for dim, blocks in cuts:
        draws = jnp.exp(jax.random.uniform(jax.random.fold_in(own, dim), (blocks,), jnp.float32, low / len(cuts), top_value / len(cuts)))
        loudness = loudness * jnp.repeat(draws, extent[dim] // blocks).reshape([-1 if axis == dim else 1 for axis in range(len(extent))])
    return loudness


def bell_draw(own_key, extent, spread, bound, split=(), dtype=jnp.bfloat16):
    entries = spread * jax.random.normal(own_key, extent, jnp.float32)
    if split:
        entries = entries * block_levels(own_key, extent, split, -0.22, 0.18)
    return jnp.clip(entries, -bound, bound).astype(dtype)


def setup_inputs(seed: int = 0, part: int = 0) -> dict:
    arg_keys = jax.random.split(jax.random.key(seed), 6)
    part_keys = jax.random.split(jax.random.fold_in(arg_keys[5], part), 6)
    queries = bell_draw(part_keys[0], (TOKENS, HD), 1.0, 6.0, ((0, 8),))
    key_rows = bell_draw(part_keys[1], (TOKENS, HD), 1.0, 6.0, ((0, 8),))
    value_rows = bell_draw(part_keys[2], (TOKENS, HD), 1.0, 6.0, ((0, 8),))
    conv_weight = bell_draw(part_keys[3], (3, CONV, HD), 0.5, 3.0, (), jnp.float32)
    head_gain = jnp.clip(1.0 + 0.18 * jax.random.normal(part_keys[4], (HD,), jnp.float32), 0.1, 1.9)
    return dict(queries=queries, key_rows=key_rows, value_rows=value_rows, conv_weight=conv_weight, head_gain=head_gain)


def causal_conv(rows, taps):
    tokens_all = rows.shape[0]
    padded = jnp.concatenate([jnp.zeros((CONV - 1, rows.shape[1]), jnp.float32), rows.astype(jnp.float32)], axis=0)
    total = jnp.zeros((tokens_all, rows.shape[1]), jnp.float32)
    for tap in range(CONV):
        total = total + taps[tap][None, :] * padded[tap:tap + tokens_all]
    return total

def reference(queries, key_rows, value_rows, conv_weight, head_gain):
    query_f = (jax.nn.silu(causal_conv(queries, conv_weight[0])) * HDIM ** (-0.5)).astype(jnp.bfloat16)
    key_f = jax.nn.silu(causal_conv(key_rows, conv_weight[1])).astype(jnp.bfloat16)
    value_f = causal_conv(value_rows, conv_weight[2]).astype(jnp.bfloat16)
    query_b = query_f.reshape(N_CTX, TOK_DEV, HEADS, HDIM)
    key_b = key_f.reshape(N_CTX, TOK_DEV, HEADS, HDIM)
    value_b = value_f.reshape(N_CTX, TOK_DEV, HEADS, HDIM)
    causal = jnp.arange(TOK_DEV)[:, None] >= jnp.arange(TOK_DEV)[None, :]

    def block_step(state, pieces):
        query_p, key_p, value_p = pieces
        qq = query_p.astype(jnp.float32)
        kk = key_p.astype(jnp.float32)
        vv = value_p.astype(jnp.float32)
        scores = jnp.einsum('thd,shd->hts', qq, kk)
        scores = jnp.where(causal[None], scores, 0.0).astype(jnp.bfloat16)
        inner = jnp.einsum('hts,she->the', scores.astype(jnp.float32), vv)
        prefix = state.astype(jnp.bfloat16).astype(jnp.float32)
        cross = jnp.einsum('thd,hde->the', qq, prefix)
        local = jnp.einsum('shd,she->hde', kk, vv)
        return (state + local, inner + cross)
    start = jnp.zeros((HEADS, HDIM, HDIM), jnp.float32)
    final_state, outputs = lax.scan(block_step, start, (query_b, key_b, value_b))
    outputs = outputs.reshape(N_CTX * TOK_DEV, HEADS, HDIM)
    scale_inv = lax.rsqrt(lax.optimization_barrier(jnp.mean(outputs * outputs, axis=2, keepdims=True)) + 1e-06)
    normed = outputs * scale_inv * head_gain.reshape(HEADS, HDIM)[None]
    return normed.reshape(N_CTX * TOK_DEV, HEADS * HDIM).astype(jnp.bfloat16)
```

```python
import functools

import jax
import jax.numpy as jnp
from jax import lax
from jax.experimental import pallas as pl
from jax.experimental.pallas import tpu as pltpu
from jax.sharding import PartitionSpec as P

HDIM = 128
CONV = 4
GROUP = 4
CHUNK = 128
AUX = 32
FIX = 16
HALF_SCALE = HDIM ** (-0.5)
F32, BF16 = jnp.float32, jnp.bfloat16


def rows_iota(shape):
    return lax.broadcasted_iota(jnp.int32, shape, 0)


def dot(a, b, dims):
    return lax.dot_general(a, b, (dims, ((), ())), preferred_element_type=F32)


def conv_chunk(x_ref, cols, start, taps):
    x = x_ref[start : start + CHUNK, cols].astype(F32)
    if start:
        earlier = x_ref[start - 16 : start, cols].astype(F32)[8:16]
    else:
        earlier = jnp.zeros((8, HDIM), F32)
    x = jnp.concatenate([earlier, x], axis=0)
    x1 = pltpu.roll(x, 1, 0)
    late = taps[3:4] * x + taps[2:3] * x1
    early = taps[1:2] * x + taps[0:1] * x1
    return (late + pltpu.roll(early, 2, 0))[8:]


def silu_of_twice(half):
    return half + half * jnp.tanh(half)


def merged_rows(first16, last16):
    first = first16.astype(F32)[0:8]
    last = last16.astype(F32)[8:16]
    return jnp.where(rows_iota((8, HDIM)) < 4, first, last)


def state_kernel(m_ref, q_first, q_last, k_ref, v_ref, w_ref, kf_ref, vf_ref, msg_ref):
    tokens = k_ref.shape[0]
    for h in range(k_ref.shape[1] // HDIM):
        cols = slice(h * HDIM, (h + 1) * HDIM)
        wk = w_ref[1, :, cols] * 0.5
        wv = w_ref[2, :, cols]
        for start in range(0, tokens, CHUNK):
            kf = silu_of_twice(conv_chunk(k_ref, cols, start, wk))
            if start == 0:
                kf = jnp.where(rows_iota(kf.shape) < CONV - 1, 0.0, kf)
            kf_ref[start : start + CHUNK, cols] = kf.astype(BF16)
            vf_ref[start : start + CHUNK, cols] = conv_chunk(v_ref, cols, start, wv).astype(BF16)
        local = dot(kf_ref[:, cols], vf_ref[:, cols], ((0,), (0,)))
        msg_ref[h, 0:HDIM] = local.astype(BF16)
        mk = merged_rows(k_ref[0:16, cols], k_ref[tokens - 16 : tokens, cols])
        mv = merged_rows(v_ref[0:16, cols], v_ref[tokens - 16 : tokens, cols])
        mq = merged_rows(q_first[:, cols], q_last[:, cols])
        msg_ref[h, HDIM : HDIM + 16] = jnp.concatenate([mk, mv], axis=0).astype(BF16)
        msg_ref[h, HDIM + 16 : HDIM + 32] = jnp.concatenate([mq, mq], axis=0).astype(BF16)


def block_states(m, queries, key_rows, value_rows, conv_weight):
    tokens, width = key_rows.shape
    quarter = width // GROUP
    heads = quarter // HDIM
    last = tokens // 16 - 1
    cols = lambda j, m: (0, j ^ m[0])
    return pl.pallas_call(
        state_kernel,
        grid_spec=pltpu.PrefetchScalarGridSpec(
            num_scalar_prefetch=1,
            grid=(GROUP,),
            in_specs=[
                pl.BlockSpec((16, quarter), cols),
                pl.BlockSpec((16, quarter), lambda j, m: (last, j ^ m[0])),
                pl.BlockSpec((tokens, quarter), cols),
                pl.BlockSpec((tokens, quarter), cols),
                pl.BlockSpec((3, CONV, quarter), lambda j, m: (0, 0, j ^ m[0])),
            ],
            out_specs=[
                pl.BlockSpec((tokens, quarter), cols),
                pl.BlockSpec((tokens, quarter), cols),
                pl.BlockSpec((heads, HDIM + AUX, HDIM), lambda j, m: (j, 0, 0)),
            ],
        ),
        out_shape=[
            jax.ShapeDtypeStruct((tokens, width), BF16),
            jax.ShapeDtypeStruct((tokens, width), BF16),
            jax.ShapeDtypeStruct((GROUP * heads, HDIM + AUX, HDIM), BF16),
        ],
        compiler_params=pltpu.CompilerParams(vmem_limit_bytes=16 << 20),
        cost_estimate=pl.CostEstimate(flops=2 * tokens * width * HDIM, bytes_accessed=8 * tokens * width, transcendentals=tokens * width),
        name="block_states",
    )(m, queries, queries, key_rows, value_rows, conv_weight)


def edge_rows(own, before, taps):
    z = pltpu.roll(jnp.where(rows_iota((8, HDIM)) < 4, own, before), 3, 0)
    y = taps[3:4] * z
    for back in range(1, CONV):
        y = y + taps[3 - back : 4 - back] * pltpu.roll(z, back, 0)
    return y


def edge_only(y):
    rows = rows_iota(y.shape)
    return jnp.where((rows >= 3) & (rows < 6), y, 0.0)


def edge_kv(own, before, w_ref, cols):
    kf = silu_of_twice(edge_rows(own[0:8], before[0:8], w_ref[1, :, cols] * 0.5))
    vf = edge_rows(own[8:16], before[8:16], w_ref[2, :, cols])
    return edge_only(kf), edge_only(vf)


def gather_packets(m_ref, packets, buf):
    for j, packet in enumerate(packets):
        buf[m_ref[0] ^ j] = packet[...]


def total_kernel(has_tail, m_ref, *refs):
    packets, refs = refs[:GROUP], refs[GROUP:]
    if has_tail:
        tail_ref, refs = refs[0], refs[1:]
    w_ref, out_ref, buf = refs
    gather_packets(m_ref, packets, buf)
    for h in range(out_ref.shape[0]):
        cols = slice(h * HDIM, (h + 1) * HDIM)
        before = tail_ref[h].astype(F32) if has_tail else jnp.zeros((AUX, HDIM), F32)
        kfs, vfs = [], []
        total = jnp.zeros((HDIM, HDIM), F32)
        for t in range(GROUP):
            own = buf[t, h, HDIM:].astype(F32)
            kf, vf = edge_kv(own, before, w_ref, cols)
            kfs.append(kf)
            vfs.append(vf)
            before = own
            total = total + buf[t, h, 0:HDIM].astype(F32)
        kf = jnp.concatenate(kfs, axis=0).astype(BF16)
        vf = jnp.concatenate(vfs, axis=0).astype(BF16)
        total = total + dot(kf, vf, ((0,), (0,)))
        out_ref[h, 0:HDIM] = total.astype(BF16)
        out_ref[h, HDIM:] = buf[GROUP - 1, h, HDIM:]


def packet_specs(heads, rows):
    return [pl.BlockSpec((heads, rows, HDIM), lambda i, m: (0, 0, 0))] * GROUP


def group_total(m, packets, tail, conv_weight):
    quarter = conv_weight.shape[2] // GROUP
    heads = quarter // HDIM
    tails = [] if tail is None else [tail]
    return pl.pallas_call(
        functools.partial(total_kernel, tail is not None),
        grid_spec=pltpu.PrefetchScalarGridSpec(
            num_scalar_prefetch=1,
            grid=(1,),
            in_specs=packet_specs(heads, HDIM + AUX)
            + [pl.BlockSpec((heads, AUX, HDIM), lambda i, m: (0, 0, 0))] * len(tails)
            + [pl.BlockSpec((3, CONV, quarter), lambda i, m: (0, 0, m[0]))],
            out_specs=pl.BlockSpec((heads, HDIM + AUX, HDIM), lambda i, m: (0, 0, 0)),
            scratch_shapes=[pltpu.VMEM((GROUP, heads, HDIM + AUX, HDIM), BF16)],
        ),
        out_shape=jax.ShapeDtypeStruct((heads, HDIM + AUX, HDIM), BF16),
        compiler_params=pltpu.CompilerParams(vmem_limit_bytes=8 << 20),
        name="group_total",
    )(m, *packets, *tails, conv_weight)


def prefix_kernel(m_ref, p0, p1, p2, p3, x_ref, w_ref, gain_ref, o0, o1, o2, o3, buf, out):
    gather_packets(m_ref, (p0, p1, p2, p3), buf)
    later = (m_ref[1] > 0).astype(F32)
    heads = x_ref.shape[0]
    for h in range(heads):
        cols = slice(h * HDIM, (h + 1) * HDIM)
        gain = gain_ref[:, cols]
        prefix = x_ref[h, 0:HDIM].astype(F32) * later
        before = x_ref[h, HDIM:].astype(F32) * later
        for t in range(GROUP):
            own = buf[t, h, HDIM:].astype(F32)
            kf, vf = edge_kv(own, before, w_ref, cols)
            qf = silu_of_twice(edge_rows(own[16:24], before[16:24], w_ref[0, :, cols] * 0.5)) * HALF_SCALE
            blank = jnp.zeros((8, HDIM), F32)
            kf = jnp.concatenate([kf, blank], axis=0).astype(BF16)
            vf = jnp.concatenate([vf, blank], axis=0).astype(BF16)
            qf = jnp.concatenate([edge_only(qf), blank], axis=0).astype(BF16)
            scores = dot(qf, kf, ((1,), (1,)))
            causal = rows_iota(scores.shape) >= lax.broadcasted_iota(jnp.int32, scores.shape, 1)
            scores = jnp.where(causal, scores, 0.0).astype(BF16)
            o = dot(scores, vf, ((1,), (0,))) + dot(qf, prefix.astype(BF16), ((1,), (0,)))
            o = o * lax.rsqrt(jnp.mean(o * o, axis=1, keepdims=True) + 1e-06) * gain
            shifted = prefix + dot(kf, vf, ((0,), (0,)))
            out[t, h, 0:HDIM] = shifted.astype(BF16)
            out[t, h, HDIM:] = jnp.concatenate([pltpu.roll(o[0:8], 5, 0), blank], axis=0).astype(BF16)
            prefix = shifted + buf[t, h, 0:HDIM].astype(F32)
            before = own
    for j, o_ref in enumerate((o0, o1, o2, o3)):
        o_ref[...] = out[m_ref[0] ^ j]


def member_prefixes(m, packets, incoming, conv_weight, gain):
    quarter = conv_weight.shape[2] // GROUP
    heads = quarter // HDIM
    out = jax.ShapeDtypeStruct((heads, HDIM + FIX, HDIM), BF16)
    return pl.pallas_call(
        prefix_kernel,
        grid_spec=pltpu.PrefetchScalarGridSpec(
            num_scalar_prefetch=1,
            grid=(1,),
            in_specs=packet_specs(heads, HDIM + AUX)
            + [
                pl.BlockSpec((heads, HDIM + AUX, HDIM), lambda i, m: (0, 0, 0)),
                pl.BlockSpec((3, CONV, quarter), lambda i, m: (0, 0, m[0])),
                pl.BlockSpec((1, quarter), lambda i, m: (0, m[0])),
            ],
            out_specs=packet_specs(heads, HDIM + FIX),
            scratch_shapes=[
                pltpu.VMEM((GROUP, heads, HDIM + AUX, HDIM), BF16),
                pltpu.VMEM((GROUP, heads, HDIM + FIX, HDIM), BF16),
            ],
        ),
        out_shape=[out] * GROUP,
        compiler_params=pltpu.CompilerParams(vmem_limit_bytes=8 << 20),
        name="member_prefixes",
    )(m, *packets, incoming, conv_weight, gain)


def inner_kernel(q_ref, kf_ref, vf_ref, w_ref, qf_ref, inner_ref):
    tokens = q_ref.shape[0]
    shape = (CHUNK, CHUNK)
    causal = rows_iota(shape) >= lax.broadcasted_iota(jnp.int32, shape, 1)
    for h in range(q_ref.shape[1] // HDIM):
        cols = slice(h * HDIM, (h + 1) * HDIM)
        wq = w_ref[0, :, cols] * 0.5
        state = None
        for start in range(0, tokens, CHUNK):
            rows = slice(start, start + CHUNK)
            qf = (silu_of_twice(conv_chunk(q_ref, cols, start, wq)) * HALF_SCALE).astype(BF16)
            qf_ref[rows, cols] = qf
            kf, vf = kf_ref[rows, cols], vf_ref[rows, cols]
            scores = jnp.where(causal, dot(qf, kf, ((1,), (1,))), 0.0).astype(BF16)
            if state is None:
                inner = dot(scores, vf, ((1,), (0,)))
                state = dot(kf, vf, ((0,), (0,)))
            else:
                left = jnp.concatenate([scores, qf], axis=1)
                right = jnp.concatenate([vf, state.astype(BF16)], axis=0)
                inner = dot(left, right, ((1,), (0,)))
                if start + CHUNK < tokens:
                    state = state + dot(kf, vf, ((0,), (0,)))
            inner_ref[rows, cols] = inner


def inner_attention(queries, kf, vf, conv_weight):
    tokens, width = queries.shape
    quarter = width // GROUP
    block = pl.BlockSpec((tokens, quarter), lambda j: (0, j))
    return pl.pallas_call(
        inner_kernel,
        grid=(GROUP,),
        in_specs=[block, block, block, pl.BlockSpec((3, CONV, quarter), lambda j: (0, 0, j))],
        out_specs=[block, block],
        out_shape=[
            jax.ShapeDtypeStruct((tokens, width), BF16),
            jax.ShapeDtypeStruct((tokens, width), F32),
        ],
        compiler_params=pltpu.CompilerParams(vmem_limit_bytes=16 << 20),
        cost_estimate=pl.CostEstimate(flops=8 * tokens * width * HDIM, bytes_accessed=12 * tokens * width, transcendentals=tokens * width),
        name="inner_attention",
    )(queries, kf, vf, conv_weight)


def finish_kernel(m_ref, p0, p1, p2, p3, qf_ref, inner_ref, gain_ref, out_ref, buf):
    step = pl.program_id(0)

    @pl.when(step == 0)
    def _():
        gather_packets(m_ref, (p0, p1, p2, p3), buf)

    heads = p0.shape[0]
    for index in range(GROUP * heads):
        t, h = index // heads, index % heads
        cols = slice(index * HDIM, (index + 1) * HDIM)
        o = inner_ref[:, cols] + dot(qf_ref[:, cols], buf[t, h, 0:HDIM], ((1,), (0,)))
        o = o * lax.rsqrt(jnp.mean(o * o, axis=1, keepdims=True) + 1e-06) * gain_ref[:, cols]
        out_ref[:, cols] = o.astype(BF16)

    @pl.when(step == 0)
    def _():
        for index in range(GROUP * heads):
            t, h = index // heads, index % heads
            cols = slice(index * HDIM, (index + 1) * HDIM)
            there = rows_iota((FIX, HDIM)) < CONV - 1
            fixed = buf[t, h, HDIM:].astype(F32)
            out_ref[0:FIX, cols] = jnp.where(there, fixed, out_ref[0:FIX, cols].astype(F32)).astype(BF16)


def finish(m, prefixes, qf, inner, gain):
    tokens, width = qf.shape
    heads = width // GROUP // HDIM
    rows = tokens // 4
    block = pl.BlockSpec((rows, width), lambda i, m: (i, 0))
    return pl.pallas_call(
        finish_kernel,
        grid_spec=pltpu.PrefetchScalarGridSpec(
            num_scalar_prefetch=1,
            grid=(tokens // rows,),
            in_specs=packet_specs(heads, HDIM + FIX)
            + [block, block, pl.BlockSpec((1, width), lambda i, m: (0, 0))],
            out_specs=block,
            scratch_shapes=[pltpu.VMEM((GROUP, heads, HDIM + FIX, HDIM), BF16)],
        ),
        out_shape=jax.ShapeDtypeStruct((tokens, width), BF16),
        compiler_params=pltpu.CompilerParams(vmem_limit_bytes=16 << 20),
        name="finish",
    )(m, *prefixes, qf, inner, gain)


def swapped(value, bits):
    count = lax.axis_size("ctx")
    return lax.ppermute(value, "ctx", [(s, s ^ bits) for s in range(count)])


def to_next_group(value):
    count = lax.axis_size("ctx")
    return lax.ppermute(value, "ctx", [(s, s + GROUP) for s in range(count - GROUP)])


def body(queries, key_rows, value_rows, conv_weight, head_gain):
    width = queries.shape[1]
    heads = width // GROUP // HDIM
    groups = lax.axis_size("ctx") // GROUP
    place = lax.axis_index("ctx")
    m = jnp.stack([place % GROUP, place // GROUP]).astype(jnp.int32)
    gain = head_gain.reshape(1, width)
    kf, vf, messages = block_states(m, queries, key_rows, value_rows, conv_weight)
    packets = [messages[0:heads]]
    packets += [swapped(messages[j * heads : (j + 1) * heads], j) for j in range(1, GROUP)]
    if groups == 2:
        incoming = swapped(group_total(m, packets, None, conv_weight), GROUP)
    else:
        last = jnp.stack(packets)[m[0] ^ (GROUP - 1)][:, HDIM:]
        tail = to_next_group(last)
        total = group_total(m, packets, tail, conv_weight)[:, 0:HDIM].astype(F32)
        prefix, passed = jnp.zeros_like(total), total
        for _ in range(groups - 1):
            prefix = to_next_group(passed)
            passed = prefix + total
        incoming = jnp.concatenate([prefix.astype(BF16), tail], axis=1)
    qf, inner = inner_attention(queries, kf, vf, conv_weight)
    sends = member_prefixes(m, packets, incoming, conv_weight, gain)
    prefixes = [sends[0]] + [swapped(sends[j], j) for j in range(1, GROUP)]
    return finish(m, prefixes, qf, inner, gain)


def solution(mesh):
    return jax.shard_map(
        body,
        mesh=mesh,
        in_specs=(
            P(("mp", "ctx"), None),
            P(("mp", "ctx"), None),
            P(("mp", "ctx"), None),
            P("mp", None, None),
            P("mp"),
        ),
        out_specs=P(("mp", "ctx"), None),
        check_vma=False,
    )
```

```python
import functools

import jax
import jax.numpy as jnp
from jax import lax
from jax.experimental import pallas as pl
from jax.experimental.pallas import tpu as pltpu
from jax.sharding import PartitionSpec as P

HDIM = 128
CONV = 4
GROUP = 4
ROWS = 256
CHUNK = 256
PIECES = (3, 3, 2)
PARTS = 2
AHEAD = 2
AUX = 32
FIX = 16
SCALE = HDIM ** (-0.5)
F32, BF16 = jnp.float32, jnp.bfloat16


def rows_iota(shape):
    return lax.broadcasted_iota(jnp.int32, shape, 0)


def dot(a, b, dims):
    return lax.dot_general(a, b, (dims, ((), ())), preferred_element_type=F32)


def conv_rows(x, earlier, taps):
    x = x.astype(F32)
    earlier = jnp.zeros((8, HDIM), F32) if earlier is None else earlier.astype(F32)[8:16]
    x = jnp.concatenate([earlier, x], axis=0)
    x1 = pltpu.roll(x, 1, 0)
    late = taps[3:4] * x + taps[2:3] * x1
    early = taps[1:2] * x + taps[0:1] * x1
    return (late + pltpu.roll(early, 2, 0))[8:]


def silu_of_twice(half):
    return half + half * jnp.tanh(half)


def merged_rows(first16, last16):
    first = first16.astype(F32)[0:8]
    last = last16.astype(F32)[8:16]
    return jnp.where(rows_iota((8, HDIM)) < 4, first, last)


def state_kernel(m_ref, q_hbm, k_hbm, v_hbm, w_hbm, kf_ref, vf_ref, msg_ref, k_buf, v_buf, edge, w_ref, k_sem, v_sem, sem):
    heads, tokens = k_buf.shape[0:2]

    def fetch(source, target, semaphore, h):
        cols = pl.ds(pl.multiple_of(h * HDIM, HDIM), HDIM)
        return pltpu.make_async_copy(source.at[:, cols], target.at[h], semaphore.at[h])

    small = [
        pltpu.make_async_copy(w_hbm, w_ref, sem.at[0]),
        pltpu.make_async_copy(q_hbm.at[0:16], edge.at[0], sem.at[1]),
        pltpu.make_async_copy(q_hbm.at[tokens - 16 : tokens], edge.at[1], sem.at[2]),
    ]
    small[0].start()
    for h in range(AHEAD):
        fetch(k_hbm, k_buf, k_sem, h).start()
        fetch(v_hbm, v_buf, v_sem, h).start()
    small[1].start()
    small[2].start()
    for copy in small:
        copy.wait()

    def one_head(h, carry):
        @pl.when(h + AHEAD < heads)
        def _():
            fetch(k_hbm, k_buf, k_sem, h + AHEAD).start()
            fetch(v_hbm, v_buf, v_sem, h + AHEAD).start()

        fetch(k_hbm, k_buf, k_sem, h).wait()
        fetch(v_hbm, v_buf, v_sem, h).wait()
        cols = pl.ds(pl.multiple_of(h * HDIM, HDIM), HDIM)
        wk = w_ref[1, :, cols] * 0.5
        wv = w_ref[2, :, cols]
        local = jnp.zeros((HDIM, HDIM), F32)
        for start in range(0, tokens, ROWS):
            rows = slice(start, start + ROWS)
            above = slice(start - 16, start)
            kf = silu_of_twice(conv_rows(k_buf[h, rows], k_buf[h, above] if start else None, wk))
            if start == 0:
                kf = jnp.where(rows_iota(kf.shape) < CONV - 1, 0.0, kf)
            kf = kf.astype(BF16)
            vf = conv_rows(v_buf[h, rows], v_buf[h, above] if start else None, wv).astype(BF16)
            kf_ref[h, rows] = kf
            vf_ref[h, rows] = vf
            local = local + dot(kf, vf, ((0,), (0,)))
        per = heads // GROUP
        place = (lax.div(h, per) ^ m_ref[0]) * per + lax.rem(h, per)
        msg_ref[place, 0:HDIM] = local.astype(BF16)
        mk = merged_rows(k_buf[h, 0:16], k_buf[h, tokens - 16 : tokens])
        mv = merged_rows(v_buf[h, 0:16], v_buf[h, tokens - 16 : tokens])
        mq = merged_rows(edge[0, :, cols], edge[1, :, cols])
        msg_ref[place, HDIM : HDIM + 16] = jnp.concatenate([mk, mv], axis=0).astype(BF16)
        msg_ref[place, HDIM + 16 : HDIM + 32] = jnp.concatenate([mq, mq], axis=0).astype(BF16)
        return carry

    lax.fori_loop(0, heads, one_head, 0)


VMEM = pl.BlockSpec(memory_space=pltpu.VMEM)
SMEM = pl.BlockSpec(memory_space=pltpu.SMEM)
HBM = pl.BlockSpec(memory_space=pltpu.HBM)


def block_states(m, queries, key_rows, value_rows, conv_weight):
    tokens, width = key_rows.shape
    heads = width // HDIM
    features = jax.ShapeDtypeStruct((heads, tokens, HDIM), BF16)
    arrays = [pltpu.with_memory_space_constraint(a, pltpu.HBM) for a in (queries, key_rows, value_rows, conv_weight)]
    return pl.pallas_call(
        state_kernel,
        in_specs=[SMEM, HBM, HBM, HBM, HBM],
        out_specs=[VMEM] * 3,
        out_shape=[features, features, jax.ShapeDtypeStruct((heads, HDIM + AUX, HDIM), BF16)],
        scratch_shapes=[
            pltpu.VMEM((heads, tokens, HDIM), BF16),
            pltpu.VMEM((heads, tokens, HDIM), BF16),
            pltpu.VMEM((2, 16, width), BF16),
            pltpu.VMEM(conv_weight.shape, F32),
            pltpu.SemaphoreType.DMA((heads,)),
            pltpu.SemaphoreType.DMA((heads,)),
            pltpu.SemaphoreType.DMA((3,)),
        ],
        compiler_params=pltpu.CompilerParams(vmem_limit_bytes=24 << 20),
        cost_estimate=pl.CostEstimate(flops=2 * tokens * width * HDIM, bytes_accessed=8 * tokens * width, transcendentals=tokens * width),
        name="block_states",
    )(m, *arrays)


def edge_rows(own, before, taps):
    z = pltpu.roll(jnp.where(rows_iota((8, HDIM)) < 4, own, before), 3, 0)
    y = taps[3:4] * z
    for back in range(1, CONV):
        y = y + taps[3 - back : 4 - back] * pltpu.roll(z, back, 0)
    return y


def edge_only(y):
    rows = rows_iota(y.shape)
    return jnp.where((rows >= 3) & (rows < 6), y, 0.0)


def edge_kv(own, before, w_ref, cols):
    kf = silu_of_twice(edge_rows(own[0:8], before[0:8], w_ref[1, :, cols] * 0.5))
    vf = edge_rows(own[8:16], before[8:16], w_ref[2, :, cols])
    return edge_only(kf), edge_only(vf)


def gather_packets(m_ref, packets, buf):
    for j, packet in enumerate(packets):
        buf[m_ref[0] ^ j] = packet[...]


def total_kernel(has_tail, m_ref, *refs):
    packets, refs = refs[:GROUP], refs[GROUP:]
    if has_tail:
        tail_ref, refs = refs[0], refs[1:]
    w_ref, out_ref, buf = refs
    gather_packets(m_ref, packets, buf)
    for h in range(out_ref.shape[0]):
        cols = slice(h * HDIM, (h + 1) * HDIM)
        before = tail_ref[h].astype(F32) if has_tail else jnp.zeros((AUX, HDIM), F32)
        kfs, vfs = [], []
        total = jnp.zeros((HDIM, HDIM), F32)
        for t in range(GROUP):
            own = buf[t, h, HDIM:].astype(F32)
            kf, vf = edge_kv(own, before, w_ref, cols)
            kfs.append(kf)
            vfs.append(vf)
            before = own
            total = total + buf[t, h, 0:HDIM].astype(F32)
        kf = jnp.concatenate(kfs, axis=0).astype(BF16)
        vf = jnp.concatenate(vfs, axis=0).astype(BF16)
        total = total + dot(kf, vf, ((0,), (0,)))
        out_ref[h, 0:HDIM] = total.astype(BF16)
        out_ref[h, HDIM:] = buf[GROUP - 1, h, HDIM:]


def packet_specs(heads, rows):
    return [pl.BlockSpec((heads, rows, HDIM), lambda i, m: (0, 0, 0))] * GROUP


def group_total(m, packets, tail, conv_weight):
    quarter = conv_weight.shape[2] // GROUP
    heads = quarter // HDIM
    tails = [] if tail is None else [tail]
    return pl.pallas_call(
        functools.partial(total_kernel, tail is not None),
        grid_spec=pltpu.PrefetchScalarGridSpec(
            num_scalar_prefetch=1,
            grid=(1,),
            in_specs=packet_specs(heads, HDIM + AUX)
            + [pl.BlockSpec((heads, AUX, HDIM), lambda i, m: (0, 0, 0))] * len(tails)
            + [pl.BlockSpec((3, CONV, quarter), lambda i, m: (0, 0, m[0]))],
            out_specs=pl.BlockSpec((heads, HDIM + AUX, HDIM), lambda i, m: (0, 0, 0)),
            scratch_shapes=[pltpu.VMEM((GROUP, heads, HDIM + AUX, HDIM), BF16)],
        ),
        out_shape=jax.ShapeDtypeStruct((heads, HDIM + AUX, HDIM), BF16),
        compiler_params=pltpu.CompilerParams(vmem_limit_bytes=8 << 20),
        name="group_total",
    )(m, *packets, *tails, conv_weight)


def prefix_kernel(m_ref, p0, p1, p2, p3, x_ref, w_ref, gain_ref, o0, o1, o2, o3, buf, out):
    gather_packets(m_ref, (p0, p1, p2, p3), buf)
    later = (m_ref[1] > 0).astype(F32)
    heads = x_ref.shape[0]
    for h in range(heads):
        cols = slice(h * HDIM, (h + 1) * HDIM)
        gain = gain_ref[:, cols]
        prefix = x_ref[h, 0:HDIM].astype(F32) * later
        before = x_ref[h, HDIM:].astype(F32) * later
        for t in range(GROUP):
            own = buf[t, h, HDIM:].astype(F32)
            kf, vf = edge_kv(own, before, w_ref, cols)
            qf = silu_of_twice(edge_rows(own[16:24], before[16:24], w_ref[0, :, cols] * 0.5)) * SCALE
            blank = jnp.zeros((8, HDIM), F32)
            kf = jnp.concatenate([kf, blank], axis=0).astype(BF16)
            vf = jnp.concatenate([vf, blank], axis=0).astype(BF16)
            qf = jnp.concatenate([edge_only(qf), blank], axis=0).astype(BF16)
            scores = dot(qf, kf, ((1,), (1,)))
            causal = rows_iota(scores.shape) >= lax.broadcasted_iota(jnp.int32, scores.shape, 1)
            scores = jnp.where(causal, scores, 0.0).astype(BF16)
            o = dot(scores, vf, ((1,), (0,))) + dot(qf, prefix.astype(BF16), ((1,), (0,)))
            o = o * lax.rsqrt(jnp.mean(o * o, axis=1, keepdims=True) + 1e-06) * gain
            shifted = prefix + dot(kf, vf, ((0,), (0,)))
            out[t, h, 0:HDIM] = shifted.astype(BF16)
            out[t, h, HDIM:] = jnp.concatenate([pltpu.roll(o[0:8], 5, 0), blank], axis=0).astype(BF16)
            prefix = shifted + buf[t, h, 0:HDIM].astype(F32)
            before = own
    for j, o_ref in enumerate((o0, o1, o2, o3)):
        o_ref[...] = out[m_ref[0] ^ j]


def member_prefixes(m, packets, incoming, conv_weight, gain):
    quarter = conv_weight.shape[2] // GROUP
    heads = quarter // HDIM
    out = jax.ShapeDtypeStruct((heads, HDIM + FIX, HDIM), BF16)
    return pl.pallas_call(
        prefix_kernel,
        grid_spec=pltpu.PrefetchScalarGridSpec(
            num_scalar_prefetch=1,
            grid=(1,),
            in_specs=packet_specs(heads, HDIM + AUX)
            + [
                pl.BlockSpec((heads, HDIM + AUX, HDIM), lambda i, m: (0, 0, 0)),
                pl.BlockSpec((3, CONV, quarter), lambda i, m: (0, 0, m[0])),
                pl.BlockSpec((1, quarter), lambda i, m: (0, m[0])),
            ],
            out_specs=packet_specs(heads, HDIM + FIX),
            scratch_shapes=[
                pltpu.VMEM((GROUP, heads, HDIM + AUX, HDIM), BF16),
                pltpu.VMEM((GROUP, heads, HDIM + FIX, HDIM), BF16),
            ],
        ),
        out_shape=[out] * GROUP,
        compiler_params=pltpu.CompilerParams(vmem_limit_bytes=8 << 20),
        name="member_prefixes",
    )(m, *packets, incoming, conv_weight, gain)


def inner_kernel(first, q_ref, kf_ref, vf_ref, w_ref, qf_ref, inner_ref):
    heads, tokens = qf_ref.shape[0:2]
    shape = (CHUNK, CHUNK)
    causal = rows_iota(shape) >= lax.broadcasted_iota(jnp.int32, shape, 1)
    for h in range(heads):
        cols = slice((first + h) * HDIM, (first + h + 1) * HDIM)
        wq = w_ref[0, :, cols] * 0.5
        state = None
        for start in range(0, tokens, CHUNK):
            rows = slice(start, start + CHUNK)
            above = q_ref[start - 16 : start, cols] if start else None
            qf = (silu_of_twice(conv_rows(q_ref[rows, cols], above, wq)) * SCALE).astype(BF16)
            qf_ref[h, rows] = qf
            kf, vf = kf_ref[first + h, rows], vf_ref[first + h, rows]
            scores = jnp.where(causal, dot(qf, kf, ((1,), (1,))), 0.0).astype(BF16)
            inner = dot(scores, vf, ((1,), (0,)))
            if state is not None:
                inner = inner + dot(qf, state.astype(BF16), ((1,), (0,)))
            inner_ref[h, rows] = inner
            if start + CHUNK < tokens:
                new = dot(kf, vf, ((0,), (0,)))
                state = new if state is None else state + new


def inner_attention(first, count, queries, kf, vf, conv_weight):
    heads, tokens = kf.shape[0:2]
    return pl.pallas_call(
        functools.partial(inner_kernel, first),
        in_specs=[VMEM] * 4,
        out_specs=[VMEM] * 2,
        out_shape=[
            jax.ShapeDtypeStruct((count, tokens, HDIM), BF16),
            jax.ShapeDtypeStruct((count, tokens, HDIM), F32),
        ],
        compiler_params=pltpu.CompilerParams(vmem_limit_bytes=24 << 20),
        cost_estimate=pl.CostEstimate(
            flops=8 * count * tokens * HDIM * HDIM,
            bytes_accessed=12 * tokens * count * HDIM,
            transcendentals=tokens * count * HDIM,
        ),
        name="inner_attention",
    )(queries, kf, vf, conv_weight)


def finish_kernel(pieces, m_ref, p0, p1, p2, p3, *refs):
    qf_refs, inner_refs, refs = refs[0:pieces], refs[pieces : 2 * pieces], refs[2 * pieces :]
    gain_ref, out_hbm, buf, out_buf, sem = refs
    gather_packets(m_ref, (p0, p1, p2, p3), buf)
    heads = p0.shape[0]
    tokens = qf_refs[0].shape[1]
    part = tokens // sem.shape[0]

    def send(c):
        rows = slice(c * part, (c + 1) * part)
        return pltpu.make_async_copy(out_buf.at[rows], out_hbm.at[rows], sem.at[c])

    for c in range(sem.shape[0]):
        rows = slice(c * part, (c + 1) * part)
        index = 0
        for qf_ref, inner_ref in zip(qf_refs, inner_refs):
            for i in range(qf_ref.shape[0]):
                t, h = index // heads, index % heads
                cols = slice(index * HDIM, (index + 1) * HDIM)
                o = inner_ref[i, rows] + dot(qf_ref[i, rows], buf[t, h, 0:HDIM], ((1,), (0,)))
                o = o * lax.rsqrt(jnp.mean(o * o, axis=1, keepdims=True) + 1e-06) * gain_ref[:, cols]
                if c == 0:
                    fixed = buf[t, h, HDIM:].astype(F32)
                    there = rows_iota((FIX, HDIM)) < CONV - 1
                    o = jnp.concatenate([jnp.where(there, fixed, o[0:FIX]), o[FIX:]], axis=0)
                out_buf[rows, cols] = o.astype(BF16)
                index += 1
        send(c).start()
    for c in range(sem.shape[0]):
        send(c).wait()


def finish(m, prefixes, qfs, inners, gain):
    tokens = qfs[0].shape[1]
    width = gain.shape[1]
    heads = width // GROUP // HDIM
    return pl.pallas_call(
        functools.partial(finish_kernel, len(qfs)),
        in_specs=[SMEM] + [VMEM] * (GROUP + 2 * len(qfs) + 1),
        out_specs=HBM,
        out_shape=jax.ShapeDtypeStruct((tokens, width), BF16),
        scratch_shapes=[
            pltpu.VMEM((GROUP, heads, HDIM + FIX, HDIM), BF16),
            pltpu.VMEM((tokens, width), BF16),
            pltpu.SemaphoreType.DMA((PARTS,)),
        ],
        compiler_params=pltpu.CompilerParams(vmem_limit_bytes=24 << 20),
        name="finish",
    )(m, *prefixes, *qfs, *inners, gain)


def swapped(value, bits):
    count = lax.axis_size("ctx")
    return lax.ppermute(value, "ctx", [(s, s ^ bits) for s in range(count)])


def to_next_group(value):
    count = lax.axis_size("ctx")
    return lax.ppermute(value, "ctx", [(s, s + GROUP) for s in range(count - GROUP)])


def body(queries, key_rows, value_rows, conv_weight, head_gain):
    width = queries.shape[1]
    heads = width // GROUP // HDIM
    groups = lax.axis_size("ctx") // GROUP
    place = lax.axis_index("ctx")
    m = jnp.stack([place % GROUP, place // GROUP]).astype(jnp.int32)
    gain = head_gain.reshape(1, width)
    kf, vf, messages = block_states(m, queries, key_rows, value_rows, conv_weight)
    bounds = [0]
    for piece in PIECES:
        bounds.append(bounds[-1] + piece * (width // HDIM) // 8)
    qfs, inners = [], []

    def beside(piece, arrays):
        first, end = bounds[piece : piece + 2]
        qf, inner = inner_attention(first, end - first, queries, kf, vf, conv_weight)
        arrays, qf, inner = lax.optimization_barrier((arrays, qf, inner))
        qfs.append(qf)
        inners.append(inner)
        return arrays

    packets = [messages[0:heads]]
    packets += [swapped(messages[j * heads : (j + 1) * heads], j) for j in range(1, GROUP)]
    packets = beside(0, packets)
    if groups == 2:
        incoming = swapped(group_total(m, packets, None, conv_weight), GROUP)
    else:
        last = jnp.stack(packets)[m[0] ^ (GROUP - 1)][:, HDIM:]
        tail = to_next_group(last)
        total = group_total(m, packets, tail, conv_weight)[:, 0:HDIM].astype(F32)
        prefix, passed = jnp.zeros_like(total), total
        for _ in range(groups - 1):
            prefix = to_next_group(passed)
            passed = prefix + total
        incoming = jnp.concatenate([prefix.astype(BF16), tail], axis=1)
    incoming = beside(1, incoming)
    sends = member_prefixes(m, packets, incoming, conv_weight, gain)
    prefixes = [sends[0]] + [swapped(sends[j], j) for j in range(1, GROUP)]
    prefixes = beside(2, prefixes)
    return finish(m, prefixes, qfs, inners, gain)


def solution(mesh):
    return jax.shard_map(
        body,
        mesh=mesh,
        in_specs=(
            P(("mp", "ctx"), None),
            P(("mp", "ctx"), None),
            P(("mp", "ctx"), None),
            P("mp", None, None),
            P("mp"),
        ),
        out_specs=P(("mp", "ctx"), None),
        check_vma=False,
    )
```

```python
import functools

import jax
import jax.numpy as jnp
from jax import lax
from jax.experimental import pallas as pl
from jax.experimental.pallas import tpu as pltpu
from jax.sharding import PartitionSpec as P

HDIM = 128
CONV = 4
GROUP = 4
ROWS = 256
CHUNK = 256
PIECES = (3, 3, 2)
PARTS = 8
PAIR = 2
AUX = 32
TAIL = 16
FIX = 16
SCALE = HDIM ** (-0.5)
F32, BF16 = jnp.float32, jnp.bfloat16


def rows_iota(shape):
    return lax.broadcasted_iota(jnp.int32, shape, 0)


def dot(a, b, dims):
    return lax.dot_general(a, b, (dims, ((), ())), preferred_element_type=F32)


def conv_rows(x, earlier, taps):
    x = x.astype(F32)
    earlier = jnp.zeros((8, HDIM), F32) if earlier is None else earlier.astype(F32)[8:16]
    x = jnp.concatenate([earlier, x], axis=0)
    x1 = pltpu.roll(x, 1, 0)
    late = taps[3:4] * x + taps[2:3] * x1
    early = taps[1:2] * x + taps[0:1] * x1
    return (late + pltpu.roll(early, 2, 0))[8:]


def silu_of_twice(half):
    return half + half * jnp.tanh(half)


def merged_rows(first16, last16):
    first = first16.astype(F32)[0:8]
    last = last16.astype(F32)[8:16]
    return jnp.where(rows_iota((8, HDIM)) < 4, first, last)


def conv_from(wide, rows, taps):
    at = lambda back: wide[rows.start + 8 - back : rows.stop + 8 - back]
    return (taps[3:4] * at(0) + taps[2:3] * at(1)) + (taps[1:2] * at(2) + taps[0:1] * at(3))


def state_kernel(m_ref, q_hbm, k_hbm, v_hbm, w_hbm, kf_ref, vf_ref, msg_ref, k_buf, v_buf, wide, edge, w_ref, k_sem, v_sem, sem):
    heads, tokens = k_buf.shape[0:2]

    def fetch(source, target, semaphore, h):
        cols = pl.ds(pl.multiple_of(h * HDIM, HDIM), HDIM)
        return pltpu.make_async_copy(source.at[:, cols], target.at[h], semaphore.at[h])

    def fetch_pair(first):
        for source, target, semaphore in ((k_hbm, k_buf, k_sem), (v_hbm, v_buf, v_sem)):
            for u in range(PAIR):
                fetch(source, target, semaphore, first + u).start()

    small = [
        pltpu.make_async_copy(w_hbm, w_ref, sem.at[0]),
        pltpu.make_async_copy(q_hbm.at[0:16], edge.at[0], sem.at[1]),
        pltpu.make_async_copy(q_hbm.at[tokens - 16 : tokens], edge.at[1], sem.at[2]),
    ]
    small[0].start()
    fetch_pair(0)
    small[1].start()
    small[2].start()
    for u in range(PAIR):
        for a in range(2):
            wide[u, a, 0:8] = jnp.zeros((8, HDIM), F32)
    small[0].wait()

    def some_heads(i, carry):
        first = i * PAIR

        @pl.when(first + PAIR < heads)
        def _():
            fetch_pair(first + PAIR)

        for u in range(PAIR):
            fetch(k_hbm, k_buf, k_sem, first + u).wait()
        for u in range(PAIR):
            h = first + u
            wk = w_ref[1, :, pl.ds(pl.multiple_of(h * HDIM, HDIM), HDIM)] * 0.5
            for start in range(0, tokens, ROWS):
                rows = slice(start, start + ROWS)
                wide[u, 0, start + 8 : start + 8 + ROWS] = k_buf[h, rows].astype(F32)
                kf = silu_of_twice(conv_from(wide.at[u, 0], rows, wk))
                if start == 0:
                    kf = jnp.where(rows_iota(kf.shape) < CONV - 1, 0.0, kf)
                kf_ref[h, rows] = kf.astype(BF16)
        for u in range(PAIR):
            fetch(v_hbm, v_buf, v_sem, first + u).wait()
        for u in range(PAIR):
            h = first + u
            cols = pl.ds(pl.multiple_of(h * HDIM, HDIM), HDIM)
            wv = w_ref[2, :, cols]
            local = jnp.zeros((HDIM, HDIM), F32)
            for start in range(0, tokens, ROWS):
                rows = slice(start, start + ROWS)
                wide[u, 1, start + 8 : start + 8 + ROWS] = v_buf[h, rows].astype(F32)
                vf = conv_from(wide.at[u, 1], rows, wv).astype(BF16)
                vf_ref[h, rows] = vf
                local = local + dot(kf_ref[h, rows], vf, ((0,), (0,)))
            per = heads // GROUP
            place = (lax.div(h, per) ^ m_ref[0]) * per + lax.rem(h, per)
            msg_ref[place, 0:HDIM] = local.astype(BF16)
            mk = merged_rows(k_buf[h, 0:16], k_buf[h, tokens - 16 : tokens])
            mv = merged_rows(v_buf[h, 0:16], v_buf[h, tokens - 16 : tokens])
            msg_ref[place, HDIM : HDIM + 16] = jnp.concatenate([mk, mv], axis=0).astype(BF16)
        return carry

    lax.fori_loop(0, heads // PAIR, some_heads, 0)
    small[1].wait()
    small[2].wait()
    for h in range(heads):
        cols = slice(h * HDIM, (h + 1) * HDIM)
        per = heads // GROUP
        place = (h // per ^ m_ref[0]) * per + h % per
        mq = merged_rows(edge[0, :, cols], edge[1, :, cols])
        msg_ref[place, HDIM + 16 : HDIM + 32] = jnp.concatenate([mq, mq], axis=0).astype(BF16)


VMEM = pl.BlockSpec(memory_space=pltpu.VMEM)
SMEM = pl.BlockSpec(memory_space=pltpu.SMEM)
HBM = pl.BlockSpec(memory_space=pltpu.HBM)


def block_states(m, queries, key_rows, value_rows, conv_weight):
    tokens, width = key_rows.shape
    heads = width // HDIM
    features = jax.ShapeDtypeStruct((heads, tokens, HDIM), BF16)
    arrays = [pltpu.with_memory_space_constraint(a, pltpu.HBM) for a in (queries, key_rows, value_rows, conv_weight)]
    return pl.pallas_call(
        state_kernel,
        in_specs=[SMEM, HBM, HBM, HBM, HBM],
        out_specs=[VMEM] * 3,
        out_shape=[features, features, jax.ShapeDtypeStruct((heads, HDIM + AUX, HDIM), BF16)],
        scratch_shapes=[
            pltpu.VMEM((heads, tokens, HDIM), BF16),
            pltpu.VMEM((heads, tokens, HDIM), BF16),
            pltpu.VMEM((PAIR, 2, tokens + 8, HDIM), F32),
            pltpu.VMEM((2, 16, width), BF16),
            pltpu.VMEM(conv_weight.shape, F32),
            pltpu.SemaphoreType.DMA((heads,)),
            pltpu.SemaphoreType.DMA((heads,)),
            pltpu.SemaphoreType.DMA((3,)),
        ],
        compiler_params=pltpu.CompilerParams(vmem_limit_bytes=24 << 20),
        cost_estimate=pl.CostEstimate(flops=2 * tokens * width * HDIM, bytes_accessed=8 * tokens * width, transcendentals=tokens * width),
        name="block_states",
    )(m, *arrays)


def edge_rows(own, before, taps):
    z = pltpu.roll(jnp.where(rows_iota((8, HDIM)) < 4, own, before), 3, 0)
    y = taps[3:4] * z
    for back in range(1, CONV):
        y = y + taps[3 - back : 4 - back] * pltpu.roll(z, back, 0)
    return y


def edge_only(y):
    rows = rows_iota(y.shape)
    return jnp.where((rows >= 3) & (rows < 6), y, 0.0)


def edge_kv(own, before, w_ref, cols):
    kf = silu_of_twice(edge_rows(own[0:8], before[0:8], w_ref[1, :, cols] * 0.5))
    vf = edge_rows(own[8:16], before[8:16], w_ref[2, :, cols])
    return edge_only(kf), edge_only(vf)


def gather_packets(m_ref, packets, buf):
    for j, packet in enumerate(packets):
        buf[m_ref[0] ^ j] = packet[...]


def gather_edges(m_ref, packets, buf):
    for j, packet in enumerate(packets):
        buf[m_ref[0] ^ j] = packet[:, HDIM:]


def total_kernel(has_tail, m_ref, *refs):
    packets, refs = refs[:GROUP], refs[GROUP:]
    if has_tail:
        tail_ref, refs = refs[0], refs[1:]
    w_ref, out_ref, buf = refs
    gather_edges(m_ref, packets, buf)
    for h in range(out_ref.shape[0]):
        cols = slice(h * HDIM, (h + 1) * HDIM)
        before = tail_ref[h].astype(F32) if has_tail else jnp.zeros((AUX, HDIM), F32)
        kfs, vfs = [], []
        total = sum(packet[h, 0:HDIM].astype(F32) for packet in packets)
        for t in range(GROUP):
            own = buf[t, h].astype(F32)
            kf, vf = edge_kv(own, before, w_ref, cols)
            kfs.append(kf)
            vfs.append(vf)
            before = own
        kf = jnp.concatenate(kfs, axis=0).astype(BF16)
        vf = jnp.concatenate(vfs, axis=0).astype(BF16)
        total = total + dot(kf, vf, ((0,), (0,)))
        out_ref[h, 0:HDIM] = total.astype(BF16)
        out_ref[h, HDIM:] = pack_tail(before).astype(BF16)


def pack_tail(raw):
    k = jnp.where(rows_iota((8, HDIM)) < 4, pltpu.roll(raw[16:24], 3, 0), raw[0:8])
    return jnp.concatenate([k, raw[8:16]], axis=0)


def unpack_tail(tail):
    q = pltpu.roll(tail[0:8], 5, 0)
    return jnp.concatenate([tail, q, q], axis=0)


def whole(a):
    return pl.BlockSpec(a.shape, lambda i, m: (0,) * len(a.shape))


def packet_specs(heads, rows):
    return [pl.BlockSpec((heads, rows, HDIM), lambda i, m: (0, 0, 0))] * GROUP


def group_total(m, packets, tail, conv_weight):
    quarter = conv_weight.shape[2] // GROUP
    heads = quarter // HDIM
    tails = [] if tail is None else [tail]
    return pl.pallas_call(
        functools.partial(total_kernel, tail is not None),
        grid_spec=pltpu.PrefetchScalarGridSpec(
            num_scalar_prefetch=1,
            grid=(1,),
            in_specs=packet_specs(heads, HDIM + AUX)
            + [pl.BlockSpec((heads, AUX, HDIM), lambda i, m: (0, 0, 0))] * len(tails)
            + [pl.BlockSpec((3, CONV, quarter), lambda i, m: (0, 0, m[0]))],
            out_specs=pl.BlockSpec((heads, HDIM + TAIL, HDIM), lambda i, m: (0, 0, 0)),
            scratch_shapes=[pltpu.VMEM((GROUP, heads, AUX, HDIM), BF16)],
        ),
        out_shape=jax.ShapeDtypeStruct((heads, HDIM + TAIL, HDIM), BF16),
        compiler_params=pltpu.CompilerParams(vmem_limit_bytes=8 << 20),
        name="group_total",
    )(m, *packets, *tails, conv_weight)


def edge_features(own, before, w_ref, cols):
    kf, vf = edge_kv(own, before, w_ref, cols)
    qf = silu_of_twice(edge_rows(own[16:24], before[16:24], w_ref[0, :, cols] * 0.5)) * SCALE
    blank = jnp.zeros((8, HDIM), F32)
    qf, kf, vf = (jnp.concatenate([a, blank], axis=0).astype(BF16) for a in (edge_only(qf), kf, vf))
    scores = dot(qf, kf, ((1,), (1,)))
    causal = rows_iota(scores.shape) >= lax.broadcasted_iota(jnp.int32, scores.shape, 1)
    scores = jnp.where(causal, scores, 0.0).astype(BF16)
    return qf, dot(scores, vf, ((1,), (0,))), dot(kf, vf, ((0,), (0,)))


def edges_kernel(m_ref, p0, p1, p2, p3, w_ref, qf_ref, inner_ref, before_ref, with_ref, first_ref, buf):
    gather_packets(m_ref, (p0, p1, p2, p3), buf)
    for h in range(p0.shape[0]):
        cols = slice(h * HDIM, (h + 1) * HDIM)
        first_ref[h] = buf[0, h, HDIM:]
        state = buf[0, h, 0:HDIM].astype(F32)
        for t in range(1, GROUP):
            own, before = buf[t, h, HDIM:].astype(F32), buf[t - 1, h, HDIM:].astype(F32)
            qf, inner, first = edge_features(own, before, w_ref, cols)
            qf_ref[t - 1, h] = qf
            inner_ref[t - 1, h] = inner
            before_ref[t - 1, h] = state
            state = state + first
            with_ref[t - 1, h] = state
            state = state + buf[t, h, 0:HDIM].astype(F32)


def member_edges(m, packets, conv_weight):
    quarter = conv_weight.shape[2] // GROUP
    heads = quarter // HDIM
    shapes = [
        jax.ShapeDtypeStruct((GROUP - 1, heads, 16, HDIM), BF16),
        jax.ShapeDtypeStruct((GROUP - 1, heads, 16, HDIM), F32),
        jax.ShapeDtypeStruct((GROUP - 1, heads, HDIM, HDIM), F32),
        jax.ShapeDtypeStruct((GROUP - 1, heads, HDIM, HDIM), F32),
        jax.ShapeDtypeStruct((heads, AUX, HDIM), BF16),
    ]
    return pl.pallas_call(
        edges_kernel,
        grid_spec=pltpu.PrefetchScalarGridSpec(
            num_scalar_prefetch=1,
            grid=(1,),
            in_specs=packet_specs(heads, HDIM + AUX) + [pl.BlockSpec((3, CONV, quarter), lambda i, m: (0, 0, m[0]))],
            out_specs=[whole(s) for s in shapes],
            scratch_shapes=[pltpu.VMEM((GROUP, heads, HDIM + AUX, HDIM), BF16)],
        ),
        out_shape=shapes,
        compiler_params=pltpu.CompilerParams(vmem_limit_bytes=8 << 20),
        name="member_edges",
    )(m, *packets, conv_weight)


def prefix_kernel(m_ref, qf_ref, inner_ref, before_ref, with_ref, first_ref, x_ref, w_ref, gain_ref, o0, o1, o2, o3, out):
    later = (m_ref[1] > 0).astype(F32)
    blank = jnp.zeros((8, HDIM), F32)
    for h in range(x_ref.shape[0]):
        cols = slice(h * HDIM, (h + 1) * HDIM)
        base = x_ref[h, 0:HDIM].astype(F32) * later
        tail = unpack_tail(x_ref[h, HDIM:].astype(F32) * later)
        qf, inner, first = edge_features(first_ref[h].astype(F32), tail, w_ref, cols)
        prefix = base
        base = base + first
        shifted = base
        for t in range(GROUP):
            if t:
                qf, inner = qf_ref[t - 1, h], inner_ref[t - 1, h]
                prefix = base + before_ref[t - 1, h]
                shifted = base + with_ref[t - 1, h]
            o = inner + dot(qf, prefix.astype(BF16), ((1,), (0,)))
            o = o * lax.rsqrt(jnp.mean(o * o, axis=1, keepdims=True) + 1e-06) * gain_ref[:, cols]
            out[t, h, 0:HDIM] = shifted.astype(BF16)
            out[t, h, HDIM:] = jnp.concatenate([pltpu.roll(o[0:8], 5, 0), blank], axis=0).astype(BF16)
    for j, o_ref in enumerate((o0, o1, o2, o3)):
        o_ref[...] = out[m_ref[0] ^ j]


def member_prefixes(m, edges, incoming, conv_weight, gain):
    quarter = conv_weight.shape[2] // GROUP
    heads = quarter // HDIM
    out = jax.ShapeDtypeStruct((heads, HDIM + FIX, HDIM), BF16)
    return pl.pallas_call(
        prefix_kernel,
        grid_spec=pltpu.PrefetchScalarGridSpec(
            num_scalar_prefetch=1,
            grid=(1,),
            in_specs=[whole(a) for a in edges]
            + [
                whole(incoming),
                pl.BlockSpec((3, CONV, quarter), lambda i, m: (0, 0, m[0])),
                pl.BlockSpec((1, quarter), lambda i, m: (0, m[0])),
            ],
            out_specs=packet_specs(heads, HDIM + FIX),
            scratch_shapes=[pltpu.VMEM((GROUP, heads, HDIM + FIX, HDIM), BF16)],
        ),
        out_shape=[out] * GROUP,
        compiler_params=pltpu.CompilerParams(vmem_limit_bytes=8 << 20),
        name="member_prefixes",
    )(m, *edges, incoming, conv_weight, gain)


def inner_kernel(first, q_ref, kf_ref, vf_ref, w_ref, qf_ref, inner_ref):
    heads, tokens = qf_ref.shape[0:2]
    shape = (CHUNK, CHUNK)
    causal = rows_iota(shape) >= lax.broadcasted_iota(jnp.int32, shape, 1)
    for h in range(heads):
        cols = slice((first + h) * HDIM, (first + h + 1) * HDIM)
        wq = w_ref[0, :, cols] * 0.5
        state = None
        for start in range(0, tokens, CHUNK):
            rows = slice(start, start + CHUNK)
            above = q_ref[start - 16 : start, cols] if start else None
            qf = (silu_of_twice(conv_rows(q_ref[rows, cols], above, wq)) * SCALE).astype(BF16)
            qf_ref[h, rows] = qf
            kf, vf = kf_ref[first + h, rows], vf_ref[first + h, rows]
            scores = jnp.where(causal, dot(qf, kf, ((1,), (1,))), 0.0).astype(BF16)
            inner = dot(scores, vf, ((1,), (0,)))
            if state is not None:
                inner = inner + dot(qf, state.astype(BF16), ((1,), (0,)))
            inner_ref[h, rows] = inner
            if start + CHUNK < tokens:
                new = dot(kf, vf, ((0,), (0,)))
                state = new if state is None else state + new


def inner_attention(first, count, queries, kf, vf, conv_weight):
    heads, tokens = kf.shape[0:2]
    return pl.pallas_call(
        functools.partial(inner_kernel, first),
        in_specs=[VMEM] * 4,
        out_specs=[VMEM] * 2,
        out_shape=[
            jax.ShapeDtypeStruct((count, tokens, HDIM), BF16),
            jax.ShapeDtypeStruct((count, tokens, HDIM), F32),
        ],
        compiler_params=pltpu.CompilerParams(vmem_limit_bytes=24 << 20),
        cost_estimate=pl.CostEstimate(
            flops=8 * count * tokens * HDIM * HDIM,
            bytes_accessed=12 * tokens * count * HDIM,
            transcendentals=tokens * count * HDIM,
        ),
        name="inner_attention",
    )(queries, kf, vf, conv_weight)


def finish_kernel(pieces, m_ref, p0, p1, p2, p3, *refs):
    qf_refs, inner_refs, refs = refs[0:pieces], refs[pieces : 2 * pieces], refs[2 * pieces :]
    gain_ref, out_hbm, buf, out_buf, sem = refs
    gather_packets(m_ref, (p0, p1, p2, p3), buf)
    heads = p0.shape[0]
    tokens = qf_refs[0].shape[1]
    part = tokens // sem.shape[0]

    def send(c):
        rows = slice(c * part, (c + 1) * part)
        return pltpu.make_async_copy(out_buf.at[rows], out_hbm.at[rows], sem.at[c])

    for c in range(sem.shape[0]):
        rows = slice(c * part, (c + 1) * part)
        index = 0
        for qf_ref, inner_ref in zip(qf_refs, inner_refs):
            for i in range(qf_ref.shape[0]):
                t, h = index // heads, index % heads
                cols = slice(index * HDIM, (index + 1) * HDIM)
                o = inner_ref[i, rows] + dot(qf_ref[i, rows], buf[t, h, 0:HDIM], ((1,), (0,)))
                o = o * lax.rsqrt(jnp.mean(o * o, axis=1, keepdims=True) + 1e-06) * gain_ref[:, cols]
                if c == 0:
                    fixed = buf[t, h, HDIM:].astype(F32)
                    there = rows_iota((FIX, HDIM)) < CONV - 1
                    o = jnp.concatenate([jnp.where(there, fixed, o[0:FIX]), o[FIX:]], axis=0)
                out_buf[rows, cols] = o.astype(BF16)
                index += 1
        send(c).start()
    for c in range(sem.shape[0]):
        send(c).wait()


def finish(m, prefixes, qfs, inners, gain):
    tokens = qfs[0].shape[1]
    width = gain.shape[1]
    heads = width // GROUP // HDIM
    return pl.pallas_call(
        functools.partial(finish_kernel, len(qfs)),
        in_specs=[SMEM] + [VMEM] * (GROUP + 2 * len(qfs) + 1),
        out_specs=HBM,
        out_shape=jax.ShapeDtypeStruct((tokens, width), BF16),
        scratch_shapes=[
            pltpu.VMEM((GROUP, heads, HDIM + FIX, HDIM), BF16),
            pltpu.VMEM((tokens, width), BF16),
            pltpu.SemaphoreType.DMA((PARTS,)),
        ],
        compiler_params=pltpu.CompilerParams(vmem_limit_bytes=24 << 20),
        name="finish",
    )(m, *prefixes, *qfs, *inners, gain)


def swapped(value, bits):
    count = lax.axis_size("ctx")
    return lax.ppermute(value, "ctx", [(s, s ^ bits) for s in range(count)])


def to_next_group(value):
    count = lax.axis_size("ctx")
    return lax.ppermute(value, "ctx", [(s, s + GROUP) for s in range(count - GROUP)])


def body(queries, key_rows, value_rows, conv_weight, head_gain):
    width = queries.shape[1]
    heads = width // GROUP // HDIM
    groups = lax.axis_size("ctx") // GROUP
    place = lax.axis_index("ctx")
    m = jnp.stack([place % GROUP, place // GROUP]).astype(jnp.int32)
    gain = head_gain.reshape(1, width)
    kf, vf, messages = block_states(m, queries, key_rows, value_rows, conv_weight)
    bounds = [0]
    for piece in PIECES:
        bounds.append(bounds[-1] + piece * (width // HDIM) // 8)
    qfs, inners = [], []

    def beside(piece, arrays):
        first, end = bounds[piece : piece + 2]
        qf, inner = inner_attention(first, end - first, queries, kf, vf, conv_weight)
        arrays, qf, inner = lax.optimization_barrier((arrays, qf, inner))
        qfs.append(qf)
        inners.append(inner)
        return arrays

    packets = [messages[0:heads]]
    packets += [swapped(messages[j * heads : (j + 1) * heads], j) for j in range(1, GROUP)]
    packets = beside(0, packets)
    if groups == 2:
        incoming = swapped(group_total(m, packets, None, conv_weight), GROUP)
    else:
        last = jnp.stack(packets)[m[0] ^ (GROUP - 1)][:, HDIM:]
        tail = to_next_group(last)
        total = group_total(m, packets, tail, conv_weight)[:, 0:HDIM].astype(F32)
        tail = jnp.concatenate([tail[:, 21:24], tail[:, 3:16]], axis=1)
        prefix, passed = jnp.zeros_like(total), total
        for _ in range(groups - 1):
            prefix = to_next_group(passed)
            passed = prefix + total
        incoming = jnp.concatenate([prefix.astype(BF16), tail], axis=1)
    edges = member_edges(m, packets, conv_weight)
    incoming, edges = beside(1, (incoming, edges))
    sends = member_prefixes(m, edges, incoming, conv_weight, gain)
    prefixes = [sends[0]] + [swapped(sends[j], j) for j in range(1, GROUP)]
    prefixes = beside(2, prefixes)
    return finish(m, prefixes, qfs, inners, gain)


def solution(mesh):
    return jax.shard_map(
        body,
        mesh=mesh,
        in_specs=(
            P(("mp", "ctx"), None),
            P(("mp", "ctx"), None),
            P(("mp", "ctx"), None),
            P("mp", None, None),
            P("mp"),
        ),
        out_specs=P(("mp", "ctx"), None),
        check_vma=False,
    )
```

```python
import functools

import jax
import jax.numpy as jnp
from jax import lax
from jax.experimental import pallas as pl
from jax.experimental.pallas import tpu as pltpu
from jax.sharding import PartitionSpec as P

HDIM = 128
CONV = 4
GROUP = 4
ROWS = 256
CHUNK = 256
PARTS = 4
PAIR = 2
AUX = 32
TAIL = 16
FIX = 16
SCALE = HDIM ** (-0.5)
F32, BF16 = jnp.float32, jnp.bfloat16


def rows_iota(shape):
    return lax.broadcasted_iota(jnp.int32, shape, 0)


def dot(a, b, dims):
    return lax.dot_general(a, b, (dims, ((), ())), preferred_element_type=F32)


def conv_rows(x, earlier, taps):
    x = x.astype(F32)
    earlier = jnp.zeros((8, HDIM), F32) if earlier is None else earlier.astype(F32)[8:16]
    x = jnp.concatenate([earlier, x], axis=0)
    x1 = pltpu.roll(x, 1, 0)
    late = taps[3:4] * x + taps[2:3] * x1
    early = taps[1:2] * x + taps[0:1] * x1
    return (late + pltpu.roll(early, 2, 0))[8:]


def silu_of_twice(half):
    return half + half * jnp.tanh(half)


def merged_rows(first16, last16):
    first = first16.astype(F32)[0:8]
    last = last16.astype(F32)[8:16]
    return jnp.where(rows_iota((8, HDIM)) < 4, first, last)


def conv_from(wide, rows, taps):
    at = lambda back: wide[rows.start + 8 - back : rows.stop + 8 - back]
    return (taps[3:4] * at(0) + taps[2:3] * at(1)) + (taps[1:2] * at(2) + taps[0:1] * at(3))


def state_kernel(m_ref, q_hbm, k_hbm, v_hbm, w_hbm, kf_ref, vf_ref, msg_ref, q_ref, w_ref, k_buf, v_buf, wide, k_sem, v_sem, sem):
    heads, tokens = k_buf.shape[0:2]

    def fetch(source, target, semaphore, h):
        cols = pl.ds(pl.multiple_of(h * HDIM, HDIM), HDIM)
        return pltpu.make_async_copy(source.at[:, cols], target.at[h], semaphore.at[h])

    def fetch_pair(first):
        for source, target, semaphore in ((k_hbm, k_buf, k_sem), (v_hbm, v_buf, v_sem)):
            for u in range(PAIR):
                fetch(source, target, semaphore, first + u).start()

    fetch_taps = pltpu.make_async_copy(w_hbm, w_ref, sem.at[0])
    fetch_queries = pltpu.make_async_copy(q_hbm, q_ref, sem.at[1])
    fetch_taps.start()
    fetch_pair(0)
    for u in range(PAIR):
        for a in range(2):
            wide[u, a, 0:8] = jnp.zeros((8, HDIM), F32)
    fetch_taps.wait()

    def some_heads(i, carry):
        first = i * PAIR

        @pl.when(first + PAIR < heads)
        def _():
            fetch_pair(first + PAIR)

        @pl.when(first + 2 * PAIR == heads)
        def _():
            fetch_queries.start()

        for u in range(PAIR):
            fetch(k_hbm, k_buf, k_sem, first + u).wait()
        for u in range(PAIR):
            h = first + u
            wk = w_ref[1, :, pl.ds(pl.multiple_of(h * HDIM, HDIM), HDIM)] * 0.5
            for start in range(0, tokens, ROWS):
                rows = slice(start, start + ROWS)
                wide[u, 0, start + 8 : start + 8 + ROWS] = k_buf[h, rows].astype(F32)
                kf = silu_of_twice(conv_from(wide.at[u, 0], rows, wk))
                if start == 0:
                    kf = jnp.where(rows_iota(kf.shape) < CONV - 1, 0.0, kf)
                kf_ref[h, rows] = kf.astype(BF16)
        for u in range(PAIR):
            fetch(v_hbm, v_buf, v_sem, first + u).wait()
        for u in range(PAIR):
            h = first + u
            cols = pl.ds(pl.multiple_of(h * HDIM, HDIM), HDIM)
            wv = w_ref[2, :, cols]
            local = jnp.zeros((HDIM, HDIM), F32)
            for start in range(0, tokens, ROWS):
                rows = slice(start, start + ROWS)
                wide[u, 1, start + 8 : start + 8 + ROWS] = v_buf[h, rows].astype(F32)
                vf = conv_from(wide.at[u, 1], rows, wv).astype(BF16)
                vf_ref[h, rows] = vf
                local = local + dot(kf_ref[h, rows], vf, ((0,), (0,)))
            per = heads // GROUP
            place = (lax.div(h, per) ^ m_ref[0]) * per + lax.rem(h, per)
            msg_ref[place, 0:HDIM] = local.astype(BF16)
            mk = merged_rows(k_buf[h, 0:16], k_buf[h, tokens - 16 : tokens])
            mv = merged_rows(v_buf[h, 0:16], v_buf[h, tokens - 16 : tokens])
            msg_ref[place, HDIM : HDIM + 16] = jnp.concatenate([mk, mv], axis=0).astype(BF16)
        return carry

    lax.fori_loop(0, heads // PAIR, some_heads, 0)
    fetch_queries.wait()
    for h in range(heads):
        cols = slice(h * HDIM, (h + 1) * HDIM)
        per = heads // GROUP
        place = (h // per ^ m_ref[0]) * per + h % per
        mq = merged_rows(q_ref[0:16, cols], q_ref[tokens - 16 : tokens, cols])
        msg_ref[place, HDIM + 16 : HDIM + 32] = jnp.concatenate([mq, mq], axis=0).astype(BF16)


VMEM = pl.BlockSpec(memory_space=pltpu.VMEM)
SMEM = pl.BlockSpec(memory_space=pltpu.SMEM)
HBM = pl.BlockSpec(memory_space=pltpu.HBM)


def block_states(m, queries, key_rows, value_rows, conv_weight):
    tokens, width = key_rows.shape
    heads = width // HDIM
    features = jax.ShapeDtypeStruct((heads, tokens, HDIM), BF16)
    arrays = [pltpu.with_memory_space_constraint(a, pltpu.HBM) for a in (queries, key_rows, value_rows, conv_weight)]
    return pl.pallas_call(
        state_kernel,
        in_specs=[SMEM, HBM, HBM, HBM, HBM],
        out_specs=[VMEM] * 5,
        out_shape=[
            features,
            features,
            jax.ShapeDtypeStruct((heads, HDIM + AUX, HDIM), BF16),
            jax.ShapeDtypeStruct(queries.shape, BF16),
            jax.ShapeDtypeStruct(conv_weight.shape, F32),
        ],
        scratch_shapes=[
            pltpu.VMEM((heads, tokens, HDIM), BF16),
            pltpu.VMEM((heads, tokens, HDIM), BF16),
            pltpu.VMEM((PAIR, 2, tokens + 8, HDIM), F32),
            pltpu.SemaphoreType.DMA((heads,)),
            pltpu.SemaphoreType.DMA((heads,)),
            pltpu.SemaphoreType.DMA((2,)),
        ],
        compiler_params=pltpu.CompilerParams(vmem_limit_bytes=24 << 20),
        cost_estimate=pl.CostEstimate(flops=2 * tokens * width * HDIM, bytes_accessed=8 * tokens * width, transcendentals=tokens * width),
        name="block_states",
    )(m, *arrays)


def taps_of(w_ref, which, m, h, per):
    return w_ref[which, :, pl.ds(pl.multiple_of((m * per + h) * HDIM, HDIM), HDIM)]


def edge_rows(own, before, taps):
    z = pltpu.roll(jnp.where(rows_iota((8, HDIM)) < 4, own, before), 3, 0)
    y = taps[3:4] * z
    for back in range(1, CONV):
        y = y + taps[3 - back : 4 - back] * pltpu.roll(z, back, 0)
    return y


def edge_only(y):
    rows = rows_iota(y.shape)
    return jnp.where((rows >= 3) & (rows < 6), y, 0.0)


def edge_kv(own, before, wk, wv):
    kf = silu_of_twice(edge_rows(own[0:8], before[0:8], wk * 0.5))
    vf = edge_rows(own[8:16], before[8:16], wv)
    return edge_only(kf), edge_only(vf)


def gather_packets(m_ref, packets, buf):
    for j, packet in enumerate(packets):
        buf[m_ref[0] ^ j] = packet[...]


def gather_edges(m_ref, packets, buf):
    for j, packet in enumerate(packets):
        buf[m_ref[0] ^ j] = packet[:, HDIM:]


def total_kernel(has_tail, m_ref, *refs):
    packets, refs = refs[:GROUP], refs[GROUP:]
    if has_tail:
        tail_ref, refs = refs[0], refs[1:]
    w_ref, out_ref, buf = refs
    gather_edges(m_ref, packets, buf)
    per = out_ref.shape[0]
    for h in range(per):
        wk, wv = (taps_of(w_ref, which, m_ref[0], h, per) for which in (1, 2))
        before = tail_ref[h].astype(F32) if has_tail else jnp.zeros((AUX, HDIM), F32)
        kfs, vfs = [], []
        total = sum(packet[h, 0:HDIM].astype(F32) for packet in packets)
        for t in range(GROUP):
            own = buf[t, h].astype(F32)
            kf, vf = edge_kv(own, before, wk, wv)
            kfs.append(kf)
            vfs.append(vf)
            before = own
        kf = jnp.concatenate(kfs, axis=0).astype(BF16)
        vf = jnp.concatenate(vfs, axis=0).astype(BF16)
        total = total + dot(kf, vf, ((0,), (0,)))
        out_ref[h, 0:HDIM] = total.astype(BF16)
        out_ref[h, HDIM:] = pack_tail(before).astype(BF16)


def pack_tail(raw):
    k = jnp.where(rows_iota((8, HDIM)) < 4, pltpu.roll(raw[16:24], 3, 0), raw[0:8])
    return jnp.concatenate([k, raw[8:16]], axis=0)


def unpack_tail(tail):
    q = pltpu.roll(tail[0:8], 5, 0)
    return jnp.concatenate([tail, q, q], axis=0)


def group_total(m, packets, tail, conv_weight):
    heads = packets[0].shape[0]
    tails = [] if tail is None else [tail]
    return pl.pallas_call(
        functools.partial(total_kernel, tail is not None),
        in_specs=[SMEM] + [VMEM] * (GROUP + len(tails) + 1),
        out_specs=VMEM,
        out_shape=jax.ShapeDtypeStruct((heads, HDIM + TAIL, HDIM), BF16),
        scratch_shapes=[pltpu.VMEM((GROUP, heads, AUX, HDIM), BF16)],
        compiler_params=pltpu.CompilerParams(vmem_limit_bytes=8 << 20),
        name="group_total",
    )(m, *packets, *tails, conv_weight)


def edge_features(own, before, wq, wk, wv):
    kf, vf = edge_kv(own, before, wk, wv)
    qf = silu_of_twice(edge_rows(own[16:24], before[16:24], wq * 0.5)) * SCALE
    blank = jnp.zeros((8, HDIM), F32)
    qf, kf, vf = (jnp.concatenate([a, blank], axis=0).astype(BF16) for a in (edge_only(qf), kf, vf))
    scores = dot(qf, kf, ((1,), (1,)))
    causal = rows_iota(scores.shape) >= lax.broadcasted_iota(jnp.int32, scores.shape, 1)
    scores = jnp.where(causal, scores, 0.0).astype(BF16)
    return qf, dot(scores, vf, ((1,), (0,))), dot(kf, vf, ((0,), (0,)))


def edges_kernel(m_ref, p0, p1, p2, p3, w_ref, qf_ref, inner_ref, before_ref, with_ref, first_ref, buf):
    gather_packets(m_ref, (p0, p1, p2, p3), buf)
    per = p0.shape[0]
    for h in range(per):
        taps = [taps_of(w_ref, which, m_ref[0], h, per) for which in range(3)]
        first_ref[h] = buf[0, h, HDIM:]
        state = buf[0, h, 0:HDIM].astype(F32)
        for t in range(1, GROUP):
            own, before = buf[t, h, HDIM:].astype(F32), buf[t - 1, h, HDIM:].astype(F32)
            qf, inner, first = edge_features(own, before, *taps)
            qf_ref[t - 1, h] = qf
            inner_ref[t - 1, h] = inner
            before_ref[t - 1, h] = state
            state = state + first
            with_ref[t - 1, h] = state
            state = state + buf[t, h, 0:HDIM].astype(F32)


def member_edges(m, packets, conv_weight):
    heads = packets[0].shape[0]
    later = GROUP - 1
    return pl.pallas_call(
        edges_kernel,
        in_specs=[SMEM] + [VMEM] * (GROUP + 1),
        out_specs=[VMEM] * 5,
        out_shape=[
            jax.ShapeDtypeStruct((later, heads, 16, HDIM), BF16),
            jax.ShapeDtypeStruct((later, heads, 16, HDIM), F32),
            jax.ShapeDtypeStruct((later, heads, HDIM, HDIM), F32),
            jax.ShapeDtypeStruct((later, heads, HDIM, HDIM), F32),
            jax.ShapeDtypeStruct((heads, AUX, HDIM), BF16),
        ],
        scratch_shapes=[pltpu.VMEM((GROUP, heads, HDIM + AUX, HDIM), BF16)],
        compiler_params=pltpu.CompilerParams(vmem_limit_bytes=8 << 20),
        name="member_edges",
    )(m, *packets, conv_weight)


def prefix_kernel(m_ref, qf_ref, inner_ref, before_ref, with_ref, first_ref, x_ref, w_ref, gain_ref, o0, o1, o2, o3, out):
    later = (m_ref[1] > 0).astype(F32)
    blank = jnp.zeros((8, HDIM), F32)
    per = x_ref.shape[0]
    for h in range(per):
        taps = [taps_of(w_ref, which, m_ref[0], h, per) for which in range(3)]
        gain = gain_ref[:, pl.ds(pl.multiple_of((m_ref[0] * per + h) * HDIM, HDIM), HDIM)]
        base = x_ref[h, 0:HDIM].astype(F32) * later
        tail = unpack_tail(x_ref[h, HDIM:].astype(F32) * later)
        qf, inner, first = edge_features(first_ref[h].astype(F32), tail, *taps)
        prefix = base
        base = base + first
        shifted = base
        for t in range(GROUP):
            if t:
                qf, inner = qf_ref[t - 1, h], inner_ref[t - 1, h]
                prefix = base + before_ref[t - 1, h]
                shifted = base + with_ref[t - 1, h]
            o = inner + dot(qf, prefix.astype(BF16), ((1,), (0,)))
            o = o * lax.rsqrt(jnp.mean(o * o, axis=1, keepdims=True) + 1e-06) * gain
            out[t, h, 0:HDIM] = shifted.astype(BF16)
            out[t, h, HDIM:] = jnp.concatenate([pltpu.roll(o[0:8], 5, 0), blank], axis=0).astype(BF16)
    for j, o_ref in enumerate((o0, o1, o2, o3)):
        o_ref[...] = out[m_ref[0] ^ j]


def member_prefixes(m, edges, incoming, conv_weight, gain):
    heads = incoming.shape[0]
    out = jax.ShapeDtypeStruct((heads, HDIM + FIX, HDIM), BF16)
    return pl.pallas_call(
        prefix_kernel,
        in_specs=[SMEM] + [VMEM] * (len(edges) + 3),
        out_specs=[VMEM] * GROUP,
        out_shape=[out] * GROUP,
        scratch_shapes=[pltpu.VMEM((GROUP, heads, HDIM + FIX, HDIM), BF16)],
        compiler_params=pltpu.CompilerParams(vmem_limit_bytes=8 << 20),
        name="member_prefixes",
    )(m, *edges, incoming, conv_weight, gain)


def inner_kernel(quarters, m_ref, q_ref, kf_ref, vf_ref, w_ref, qf_ref, inner_ref):
    heads, tokens = qf_ref.shape[0:2]
    per = heads // len(quarters)
    shape = (CHUNK, CHUNK)
    causal = rows_iota(shape) >= lax.broadcasted_iota(jnp.int32, shape, 1)
    for place in range(heads):
        h = (m_ref[0] ^ quarters[place // per]) * per + place % per
        cols = pl.ds(pl.multiple_of(h * HDIM, HDIM), HDIM)
        wq = w_ref[0, :, cols] * 0.5
        state = None
        for start in range(0, tokens, CHUNK):
            rows = slice(start, start + CHUNK)
            above = q_ref[start - 16 : start, cols] if start else None
            qf = (silu_of_twice(conv_rows(q_ref[rows, cols], above, wq)) * SCALE).astype(BF16)
            qf_ref[place, rows] = qf
            kf, vf = kf_ref[h, rows], vf_ref[h, rows]
            scores = jnp.where(causal, dot(qf, kf, ((1,), (1,))), 0.0).astype(BF16)
            inner = dot(scores, vf, ((1,), (0,)))
            if state is not None:
                inner = inner + dot(qf, state.astype(BF16), ((1,), (0,)))
            inner_ref[place, rows] = inner
            if start + CHUNK < tokens:
                new = dot(kf, vf, ((0,), (0,)))
                state = new if state is None else state + new


def inner_attention(quarters, m, queries, kf, vf, conv_weight):
    heads, tokens = kf.shape[0:2]
    count = heads // GROUP * len(quarters)
    return pl.pallas_call(
        functools.partial(inner_kernel, quarters),
        in_specs=[SMEM] + [VMEM] * 4,
        out_specs=[VMEM] * 2,
        out_shape=[
            jax.ShapeDtypeStruct((count, tokens, HDIM), BF16),
            jax.ShapeDtypeStruct((count, tokens, HDIM), F32),
        ],
        compiler_params=pltpu.CompilerParams(vmem_limit_bytes=24 << 20),
        cost_estimate=pl.CostEstimate(
            flops=8 * count * tokens * HDIM * HDIM,
            bytes_accessed=12 * tokens * count * HDIM,
            transcendentals=tokens * count * HDIM,
        ),
        name="inner_attention",
    )(m, queries, kf, vf, conv_weight)


def finish_kernel(quarters, places, aliased, m_ref, gain_ref, *refs):
    n = len(quarters)
    packets, qf_refs, inner_refs, refs = refs[0:n], refs[n : 2 * n], refs[2 * n : 3 * n], refs[3 * n + aliased :]
    out_hbm, out_buf, sem = refs
    per = packets[0].shape[0]
    tokens = out_buf.shape[1]
    part = tokens // PARTS
    there = rows_iota((FIX, HDIM)) < CONV - 1
    copies = []
    for i in range(n):
        quarter = m_ref[0] ^ quarters[i]
        for c in range(PARTS):
            rows = slice(c * part, (c + 1) * part)
            for h in range(per):
                place = places[i] * per + h
                gain = gain_ref[:, pl.ds(pl.multiple_of((quarter * per + h) * HDIM, HDIM), HDIM)]
                o = inner_refs[i][place, rows] + dot(qf_refs[i][place, rows], packets[i][h, 0:HDIM], ((1,), (0,)))
                o = o * lax.rsqrt(jnp.mean(o * o, axis=1, keepdims=True) + 1e-06) * gain
                if c == 0:
                    fixed = packets[i][h, HDIM:].astype(F32)
                    o = jnp.concatenate([jnp.where(there, fixed, o[0:FIX]), o[FIX:]], axis=0)
                out_buf[i, rows, h * HDIM : (h + 1) * HDIM] = o.astype(BF16)
            cols = pl.ds(pl.multiple_of(quarter * per * HDIM, per * HDIM), per * HDIM)
            copies.append(pltpu.make_async_copy(out_buf.at[i, rows], out_hbm.at[rows, cols], sem.at[i, c]))
            copies[-1].start()
    for copy in copies:
        copy.wait()


def finish(quarters, m, prefixes, pieces, places, gain, begun=None):
    tokens = pieces[0][0].shape[1]
    width = gain.shape[1]
    n = len(quarters)
    others = [] if begun is None else [begun]
    return pl.pallas_call(
        functools.partial(finish_kernel, quarters, places, len(others)),
        in_specs=[SMEM] + [VMEM] * (1 + 3 * n) + [HBM] * len(others),
        out_specs=HBM,
        out_shape=jax.ShapeDtypeStruct((tokens, width), BF16),
        input_output_aliases={2 + 3 * n: 0} if others else {},
        scratch_shapes=[
            pltpu.VMEM((n, tokens, width // GROUP), BF16),
            pltpu.SemaphoreType.DMA((n, PARTS)),
        ],
        compiler_params=pltpu.CompilerParams(vmem_limit_bytes=24 << 20),
        cost_estimate=pl.CostEstimate(
            flops=2 * n * tokens * width // GROUP * HDIM,
            bytes_accessed=8 * n * tokens * width // GROUP,
            transcendentals=n * tokens * width // GROUP // HDIM,
        ),
        name="finish",
    )(m, gain, *prefixes, *[p[0] for p in pieces], *[p[1] for p in pieces], *others)


def swapped(value, bits):
    count = lax.axis_size("ctx")
    return lax.ppermute(value, "ctx", [(s, s ^ bits) for s in range(count)])


def to_next_group(value):
    count = lax.axis_size("ctx")
    return lax.ppermute(value, "ctx", [(s, s + GROUP) for s in range(count - GROUP)])


def body(queries, key_rows, value_rows, conv_weight, head_gain):
    width = queries.shape[1]
    heads = width // GROUP // HDIM
    groups = lax.axis_size("ctx") // GROUP
    place = lax.axis_index("ctx")
    m = jnp.stack([place % GROUP, place // GROUP]).astype(jnp.int32)
    gain = head_gain.reshape(1, width)
    kf, vf, messages, queries, conv_weight = block_states(m, queries, key_rows, value_rows, conv_weight)

    def beside(quarters, arrays):
        piece = inner_attention(quarters, m, queries, kf, vf, conv_weight)
        return lax.optimization_barrier((arrays, piece))

    packets = [messages[0:heads]]
    packets += [swapped(messages[j * heads : (j + 1) * heads], j) for j in range(1, GROUP)]
    packets, piece01 = beside((0, 1), packets)
    if groups == 2:
        incoming = swapped(group_total(m, packets, None, conv_weight), GROUP)
    else:
        last = jnp.stack(packets)[m[0] ^ (GROUP - 1)][:, HDIM:]
        tail = to_next_group(last)
        total = group_total(m, packets, tail, conv_weight)[:, 0:HDIM].astype(F32)
        tail = jnp.concatenate([tail[:, 21:24], tail[:, 3:16]], axis=1)
        prefix, passed = jnp.zeros_like(total), total
        for _ in range(groups - 1):
            prefix = to_next_group(passed)
            passed = prefix + total
        incoming = jnp.concatenate([prefix.astype(BF16), tail], axis=1)
    edges = member_edges(m, packets, conv_weight)
    (incoming, edges), piece2 = beside((2,), (incoming, edges))
    sends = member_prefixes(m, edges, incoming, conv_weight, gain)
    near = [swapped(sends[j], j) for j in (1, 2)]
    far = swapped(sends[3], 3)
    near, piece3 = beside((3,), near)
    out = finish((0, 1, 2), m, [sends[0]] + near, [piece01, piece01, piece2], (0, 1, 0), gain)
    return finish((3,), m, [far], [piece3], (0,), gain, out)


def solution(mesh):
    return jax.shard_map(
        body,
        mesh=mesh,
        in_specs=(
            P(("mp", "ctx"), None),
            P(("mp", "ctx"), None),
            P(("mp", "ctx"), None),
            P("mp", None, None),
            P("mp"),
        ),
        out_specs=P(("mp", "ctx"), None),
        check_vma=False,
    )
```

```python
import functools

import jax
import jax.numpy as jnp
from jax import lax
from jax.experimental import pallas as pl
from jax.experimental.pallas import tpu as pltpu
from jax.sharding import PartitionSpec as P

HDIM = 128
CONV = 4
GROUP = 4
ROWS = 256
CHUNK = 256
PARTS = 4
PAIR = 2
AUX = 32
TAIL = 16
FIX = 16
SCALE = HDIM ** (-0.5)
F32, BF16 = jnp.float32, jnp.bfloat16


def member():
    return lax.rem(lax.axis_index("ctx"), GROUP)


def group():
    return lax.div(lax.axis_index("ctx"), GROUP)


def rows_iota(shape):
    return lax.broadcasted_iota(jnp.int32, shape, 0)


def dot(a, b, dims):
    return lax.dot_general(a, b, (dims, ((), ())), preferred_element_type=F32)


def conv_rows(x, earlier, taps):
    x = x.astype(F32)
    earlier = jnp.zeros((8, HDIM), F32) if earlier is None else earlier.astype(F32)[8:16]
    x = jnp.concatenate([earlier, x], axis=0)
    x1 = pltpu.roll(x, 1, 0)
    late = taps[3:4] * x + taps[2:3] * x1
    early = taps[1:2] * x + taps[0:1] * x1
    return (late + pltpu.roll(early, 2, 0))[8:]


def silu_of_twice(half):
    return half + half * jnp.tanh(half)


def merged_rows(first16, last16):
    first = first16.astype(F32)[0:8]
    last = last16.astype(F32)[8:16]
    return jnp.where(rows_iota((8, HDIM)) < 4, first, last)


def conv_from(wide, rows, taps):
    at = lambda back: wide[rows.start + 8 - back : rows.stop + 8 - back]
    return (taps[3:4] * at(0) + taps[2:3] * at(1)) + (taps[1:2] * at(2) + taps[0:1] * at(3))


def state_kernel(q_hbm, k_hbm, v_hbm, w_hbm, kf_ref, vf_ref, msg_ref, q_ref, w_ref, k_buf, v_buf, wide, k_sem, v_sem, sem):
    heads, tokens = k_buf.shape[0:2]

    def fetch(source, target, semaphore, h):
        cols = pl.ds(pl.multiple_of(h * HDIM, HDIM), HDIM)
        return pltpu.make_async_copy(source.at[:, cols], target.at[h], semaphore.at[h])

    def fetch_pair(first):
        for source, target, semaphore in ((k_hbm, k_buf, k_sem), (v_hbm, v_buf, v_sem)):
            for u in range(PAIR):
                fetch(source, target, semaphore, first + u).start()

    fetch_taps = pltpu.make_async_copy(w_hbm, w_ref, sem.at[0])
    fetch_queries = pltpu.make_async_copy(q_hbm, q_ref, sem.at[1])
    fetch_taps.start()
    fetch_pair(0)
    for u in range(PAIR):
        for a in range(2):
            wide[u, a, 0:8] = jnp.zeros((8, HDIM), F32)
    fetch_taps.wait()

    def some_heads(i, carry):
        first = i * PAIR

        @pl.when(first + PAIR < heads)
        def _():
            fetch_pair(first + PAIR)

        @pl.when(first + 2 * PAIR == heads)
        def _():
            fetch_queries.start()

        for u in range(PAIR):
            fetch(k_hbm, k_buf, k_sem, first + u).wait()
        for u in range(PAIR):
            h = first + u
            wk = w_ref[1, :, pl.ds(pl.multiple_of(h * HDIM, HDIM), HDIM)] * 0.5
            for start in range(0, tokens, ROWS):
                rows = slice(start, start + ROWS)
                wide[u, 0, start + 8 : start + 8 + ROWS] = k_buf[h, rows].astype(F32)
                kf = silu_of_twice(conv_from(wide.at[u, 0], rows, wk))
                if start == 0:
                    kf = jnp.where(rows_iota(kf.shape) < CONV - 1, 0.0, kf)
                kf_ref[h, rows] = kf.astype(BF16)
        for u in range(PAIR):
            fetch(v_hbm, v_buf, v_sem, first + u).wait()
        for u in range(PAIR):
            h = first + u
            cols = pl.ds(pl.multiple_of(h * HDIM, HDIM), HDIM)
            wv = w_ref[2, :, cols]
            local = jnp.zeros((HDIM, HDIM), F32)
            for start in range(0, tokens, ROWS):
                rows = slice(start, start + ROWS)
                wide[u, 1, start + 8 : start + 8 + ROWS] = v_buf[h, rows].astype(F32)
                vf = conv_from(wide.at[u, 1], rows, wv).astype(BF16)
                vf_ref[h, rows] = vf
                local = local + dot(kf_ref[h, rows], vf, ((0,), (0,)))
            per = heads // GROUP
            place = (lax.div(h, per) ^ member()) * per + lax.rem(h, per)
            msg_ref[place, 0:HDIM] = local.astype(BF16)
            mk = merged_rows(k_buf[h, 0:16], k_buf[h, tokens - 16 : tokens])
            mv = merged_rows(v_buf[h, 0:16], v_buf[h, tokens - 16 : tokens])
            msg_ref[place, HDIM : HDIM + 16] = jnp.concatenate([mk, mv], axis=0).astype(BF16)
        return carry

    lax.fori_loop(0, heads // PAIR, some_heads, 0)
    fetch_queries.wait()
    for h in range(heads):
        cols = slice(h * HDIM, (h + 1) * HDIM)
        per = heads // GROUP
        place = (h // per ^ member()) * per + h % per
        mq = merged_rows(q_ref[0:16, cols], q_ref[tokens - 16 : tokens, cols])
        msg_ref[place, HDIM + 16 : HDIM + 32] = jnp.concatenate([mq, mq], axis=0).astype(BF16)


VMEM = pl.BlockSpec(memory_space=pltpu.VMEM)
HBM = pl.BlockSpec(memory_space=pltpu.HBM)


def block_states(queries, key_rows, value_rows, conv_weight):
    tokens, width = key_rows.shape
    heads = width // HDIM
    features = jax.ShapeDtypeStruct((heads, tokens, HDIM), BF16)
    arrays = [pltpu.with_memory_space_constraint(a, pltpu.HBM) for a in (queries, key_rows, value_rows, conv_weight)]
    return pl.pallas_call(
        state_kernel,
        in_specs=[HBM, HBM, HBM, HBM],
        out_specs=[VMEM] * 5,
        out_shape=[
            features,
            features,
            jax.ShapeDtypeStruct((heads, HDIM + AUX, HDIM), BF16),
            jax.ShapeDtypeStruct(queries.shape, BF16),
            jax.ShapeDtypeStruct(conv_weight.shape, F32),
        ],
        scratch_shapes=[
            pltpu.VMEM((heads, tokens, HDIM), BF16),
            pltpu.VMEM((heads, tokens, HDIM), BF16),
            pltpu.VMEM((PAIR, 2, tokens + 8, HDIM), F32),
            pltpu.SemaphoreType.DMA((heads,)),
            pltpu.SemaphoreType.DMA((heads,)),
            pltpu.SemaphoreType.DMA((2,)),
        ],
        compiler_params=pltpu.CompilerParams(vmem_limit_bytes=24 << 20),
        cost_estimate=pl.CostEstimate(flops=2 * tokens * width * HDIM, bytes_accessed=8 * tokens * width, transcendentals=tokens * width),
        name="block_states",
    )(*arrays)


def taps_of(w_ref, which, m, h, per):
    return w_ref[which, :, pl.ds(pl.multiple_of((m * per + h) * HDIM, HDIM), HDIM)]


def edge_rows(own, before, taps):
    z = pltpu.roll(jnp.where(rows_iota((8, HDIM)) < 4, own, before), 3, 0)
    y = taps[3:4] * z
    for back in range(1, CONV):
        y = y + taps[3 - back : 4 - back] * pltpu.roll(z, back, 0)
    return y


def edge_only(y):
    rows = rows_iota(y.shape)
    return jnp.where((rows >= 3) & (rows < 6), y, 0.0)


def edge_kv(own, before, wk, wv):
    kf = silu_of_twice(edge_rows(own[0:8], before[0:8], wk * 0.5))
    vf = edge_rows(own[8:16], before[8:16], wv)
    return edge_only(kf), edge_only(vf)


def gather_packets(packets, buf):
    for j, packet in enumerate(packets):
        buf[member() ^ j] = packet[...]


def gather_edges(packets, buf):
    for j, packet in enumerate(packets):
        buf[member() ^ j] = packet[:, HDIM:]


def total_kernel(has_tail, *refs):
    packets, refs = refs[:GROUP], refs[GROUP:]
    if has_tail:
        tail_ref, refs = refs[0], refs[1:]
    w_ref, out_ref, buf = refs
    gather_edges(packets, buf)
    per = out_ref.shape[0]
    for h in range(per):
        wk, wv = (taps_of(w_ref, which, member(), h, per) for which in (1, 2))
        before = tail_ref[h].astype(F32) if has_tail else jnp.zeros((AUX, HDIM), F32)
        kfs, vfs = [], []
        total = sum(packet[h, 0:HDIM].astype(F32) for packet in packets)
        for t in range(GROUP):
            own = buf[t, h].astype(F32)
            kf, vf = edge_kv(own, before, wk, wv)
            kfs.append(kf)
            vfs.append(vf)
            before = own
        kf = jnp.concatenate(kfs, axis=0).astype(BF16)
        vf = jnp.concatenate(vfs, axis=0).astype(BF16)
        total = total + dot(kf, vf, ((0,), (0,)))
        out_ref[h, 0:HDIM] = total.astype(BF16)
        out_ref[h, HDIM:] = pack_tail(before).astype(BF16)


def pack_tail(raw):
    k = jnp.where(rows_iota((8, HDIM)) < 4, pltpu.roll(raw[16:24], 3, 0), raw[0:8])
    return jnp.concatenate([k, raw[8:16]], axis=0)


def unpack_tail(tail):
    q = pltpu.roll(tail[0:8], 5, 0)
    return jnp.concatenate([tail, q, q], axis=0)


def group_total(packets, tail, conv_weight):
    heads = packets[0].shape[0]
    tails = [] if tail is None else [tail]
    return pl.pallas_call(
        functools.partial(total_kernel, tail is not None),
        in_specs=[VMEM] * (GROUP + len(tails) + 1),
        out_specs=VMEM,
        out_shape=jax.ShapeDtypeStruct((heads, HDIM + TAIL, HDIM), BF16),
        scratch_shapes=[pltpu.VMEM((GROUP, heads, AUX, HDIM), BF16)],
        compiler_params=pltpu.CompilerParams(vmem_limit_bytes=8 << 20),
        name="group_total",
    )(*packets, *tails, conv_weight)


def edge_features(own, before, wq, wk, wv):
    kf, vf = edge_kv(own, before, wk, wv)
    qf = silu_of_twice(edge_rows(own[16:24], before[16:24], wq * 0.5)) * SCALE
    blank = jnp.zeros((8, HDIM), F32)
    qf, kf, vf = (jnp.concatenate([a, blank], axis=0).astype(BF16) for a in (edge_only(qf), kf, vf))
    scores = dot(qf, kf, ((1,), (1,)))
    causal = rows_iota(scores.shape) >= lax.broadcasted_iota(jnp.int32, scores.shape, 1)
    scores = jnp.where(causal, scores, 0.0).astype(BF16)
    return qf, dot(scores, vf, ((1,), (0,))), dot(kf, vf, ((0,), (0,)))


def edges_kernel(p0, p1, p2, p3, w_ref, qf_ref, inner_ref, before_ref, with_ref, first_ref, buf):
    gather_packets((p0, p1, p2, p3), buf)
    per = p0.shape[0]
    for h in range(per):
        taps = [taps_of(w_ref, which, member(), h, per) for which in range(3)]
        first_ref[h] = buf[0, h, HDIM:]
        state = buf[0, h, 0:HDIM].astype(F32)
        for t in range(1, GROUP):
            own, before = buf[t, h, HDIM:].astype(F32), buf[t - 1, h, HDIM:].astype(F32)
            qf, inner, first = edge_features(own, before, *taps)
            qf_ref[t - 1, h] = qf
            inner_ref[t - 1, h] = inner
            before_ref[t - 1, h] = state
            state = state + first
            with_ref[t - 1, h] = state
            state = state + buf[t, h, 0:HDIM].astype(F32)


def member_edges(packets, conv_weight):
    heads = packets[0].shape[0]
    later = GROUP - 1
    return pl.pallas_call(
        edges_kernel,
        in_specs=[VMEM] * (GROUP + 1),
        out_specs=[VMEM] * 5,
        out_shape=[
            jax.ShapeDtypeStruct((later, heads, 16, HDIM), BF16),
            jax.ShapeDtypeStruct((later, heads, 16, HDIM), F32),
            jax.ShapeDtypeStruct((later, heads, HDIM, HDIM), F32),
            jax.ShapeDtypeStruct((later, heads, HDIM, HDIM), F32),
            jax.ShapeDtypeStruct((heads, AUX, HDIM), BF16),
        ],
        scratch_shapes=[pltpu.VMEM((GROUP, heads, HDIM + AUX, HDIM), BF16)],
        compiler_params=pltpu.CompilerParams(vmem_limit_bytes=8 << 20),
        name="member_edges",
    )(*packets, conv_weight)


def prefix_kernel(qf_ref, inner_ref, before_ref, with_ref, first_ref, x_ref, w_ref, gain_ref, o0, o1, o2, o3, out):
    later = (group() > 0).astype(F32)
    blank = jnp.zeros((8, HDIM), F32)
    per = x_ref.shape[0]
    for h in range(per):
        taps = [taps_of(w_ref, which, member(), h, per) for which in range(3)]
        gain = gain_ref[:, pl.ds(pl.multiple_of((member() * per + h) * HDIM, HDIM), HDIM)]
        base = x_ref[h, 0:HDIM].astype(F32) * later
        tail = unpack_tail(x_ref[h, HDIM:].astype(F32) * later)
        qf, inner, first = edge_features(first_ref[h].astype(F32), tail, *taps)
        prefix = base
        base = base + first
        shifted = base
        for t in range(GROUP):
            if t:
                qf, inner = qf_ref[t - 1, h], inner_ref[t - 1, h]
                prefix = base + before_ref[t - 1, h]
                shifted = base + with_ref[t - 1, h]
            o = inner + dot(qf, prefix.astype(BF16), ((1,), (0,)))
            o = o * lax.rsqrt(jnp.mean(o * o, axis=1, keepdims=True) + 1e-06) * gain
            out[t, h, 0:HDIM] = shifted.astype(BF16)
            out[t, h, HDIM:] = jnp.concatenate([pltpu.roll(o[0:8], 5, 0), blank], axis=0).astype(BF16)
    for j, o_ref in enumerate((o0, o1, o2, o3)):
        o_ref[...] = out[member() ^ j]


def member_prefixes(edges, incoming, conv_weight, gain):
    heads = incoming.shape[0]
    out = jax.ShapeDtypeStruct((heads, HDIM + FIX, HDIM), BF16)
    return pl.pallas_call(
        prefix_kernel,
        in_specs=[VMEM] * (len(edges) + 3),
        out_specs=[VMEM] * GROUP,
        out_shape=[out] * GROUP,
        scratch_shapes=[pltpu.VMEM((GROUP, heads, HDIM + FIX, HDIM), BF16)],
        compiler_params=pltpu.CompilerParams(vmem_limit_bytes=8 << 20),
        name="member_prefixes",
    )(*edges, incoming, conv_weight, gain)


def inner_kernel(quarters, q_ref, kf_ref, vf_ref, w_ref, qf_ref, inner_ref):
    heads, tokens = qf_ref.shape[0:2]
    per = heads // len(quarters)
    shape = (CHUNK, CHUNK)
    causal = rows_iota(shape) >= lax.broadcasted_iota(jnp.int32, shape, 1)
    for place in range(heads):
        h = (member() ^ quarters[place // per]) * per + place % per
        cols = pl.ds(pl.multiple_of(h * HDIM, HDIM), HDIM)
        wq = w_ref[0, :, cols] * 0.5
        state = None
        for start in range(0, tokens, CHUNK):
            rows = slice(start, start + CHUNK)
            above = q_ref[start - 16 : start, cols] if start else None
            qf = (silu_of_twice(conv_rows(q_ref[rows, cols], above, wq)) * SCALE).astype(BF16)
            qf_ref[place, rows] = qf
            kf, vf = kf_ref[h, rows], vf_ref[h, rows]
            scores = jnp.where(causal, dot(qf, kf, ((1,), (1,))), 0.0).astype(BF16)
            inner = dot(scores, vf, ((1,), (0,)))
            if state is not None:
                inner = inner + dot(qf, state.astype(BF16), ((1,), (0,)))
            inner_ref[place, rows] = inner
            if start + CHUNK < tokens:
                new = dot(kf, vf, ((0,), (0,)))
                state = new if state is None else state + new


def inner_attention(quarters, queries, kf, vf, conv_weight):
    heads, tokens = kf.shape[0:2]
    count = heads // GROUP * len(quarters)
    return pl.pallas_call(
        functools.partial(inner_kernel, quarters),
        in_specs=[VMEM] * 4,
        out_specs=[VMEM] * 2,
        out_shape=[
            jax.ShapeDtypeStruct((count, tokens, HDIM), BF16),
            jax.ShapeDtypeStruct((count, tokens, HDIM), F32),
        ],
        compiler_params=pltpu.CompilerParams(vmem_limit_bytes=24 << 20),
        cost_estimate=pl.CostEstimate(
            flops=8 * count * tokens * HDIM * HDIM,
            bytes_accessed=12 * tokens * count * HDIM,
            transcendentals=tokens * count * HDIM,
        ),
        name="inner_attention",
    )(queries, kf, vf, conv_weight)


def finish_kernel(quarters, places, aliased, gain_ref, *refs):
    n = len(quarters)
    packets, qf_refs, inner_refs, refs = refs[0:n], refs[n : 2 * n], refs[2 * n : 3 * n], refs[3 * n + aliased :]
    out_hbm, out_buf, sem = refs
    per = packets[0].shape[0]
    tokens = out_buf.shape[1]
    part = tokens // PARTS
    there = rows_iota((FIX, HDIM)) < CONV - 1
    copies = []
    for i in range(n):
        quarter = member() ^ quarters[i]
        for c in range(PARTS):
            rows = slice(c * part, (c + 1) * part)
            for h in range(per):
                place = places[i] * per + h
                gain = gain_ref[:, pl.ds(pl.multiple_of((quarter * per + h) * HDIM, HDIM), HDIM)]
                o = inner_refs[i][place, rows] + dot(qf_refs[i][place, rows], packets[i][h, 0:HDIM], ((1,), (0,)))
                o = o * lax.rsqrt(jnp.mean(o * o, axis=1, keepdims=True) + 1e-06) * gain
                if c == 0:
                    fixed = packets[i][h, HDIM:].astype(F32)
                    o = jnp.concatenate([jnp.where(there, fixed, o[0:FIX]), o[FIX:]], axis=0)
                out_buf[i, rows, h * HDIM : (h + 1) * HDIM] = o.astype(BF16)
            cols = pl.ds(pl.multiple_of(quarter * per * HDIM, per * HDIM), per * HDIM)
            copies.append(pltpu.make_async_copy(out_buf.at[i, rows], out_hbm.at[rows, cols], sem.at[i, c]))
            copies[-1].start()
    for copy in copies:
        copy.wait()


def finish(quarters, prefixes, pieces, places, gain, begun=None):
    tokens = pieces[0][0].shape[1]
    width = gain.shape[1]
    n = len(quarters)
    others = [] if begun is None else [begun]
    return pl.pallas_call(
        functools.partial(finish_kernel, quarters, places, len(others)),
        in_specs=[VMEM] * (1 + 3 * n) + [HBM] * len(others),
        out_specs=HBM,
        out_shape=jax.ShapeDtypeStruct((tokens, width), BF16),
        input_output_aliases={1 + 3 * n: 0} if others else {},
        scratch_shapes=[
            pltpu.VMEM((n, tokens, width // GROUP), BF16),
            pltpu.SemaphoreType.DMA((n, PARTS)),
        ],
        compiler_params=pltpu.CompilerParams(vmem_limit_bytes=24 << 20),
        cost_estimate=pl.CostEstimate(
            flops=2 * n * tokens * width // GROUP * HDIM,
            bytes_accessed=8 * n * tokens * width // GROUP,
            transcendentals=n * tokens * width // GROUP // HDIM,
        ),
        name="finish",
    )(gain, *prefixes, *[p[0] for p in pieces], *[p[1] for p in pieces], *others)


def swapped(value, bits):
    count = lax.axis_size("ctx")
    return lax.ppermute(value, "ctx", [(s, s ^ bits) for s in range(count)])


def to_next_group(value):
    count = lax.axis_size("ctx")
    return lax.ppermute(value, "ctx", [(s, s + GROUP) for s in range(count - GROUP)])


def body(queries, key_rows, value_rows, conv_weight, head_gain):
    width = queries.shape[1]
    heads = width // GROUP // HDIM
    groups = lax.axis_size("ctx") // GROUP
    gain = head_gain.reshape(1, width)
    kf, vf, messages, queries, conv_weight = block_states(queries, key_rows, value_rows, conv_weight)

    def beside(quarters, arrays):
        piece = inner_attention(quarters, queries, kf, vf, conv_weight)
        return lax.optimization_barrier((arrays, piece))

    packets = [messages[0:heads]]
    packets += [swapped(messages[j * heads : (j + 1) * heads], j) for j in range(1, GROUP)]
    packets, piece01 = beside((0, 1), packets)
    if groups == 2:
        incoming = swapped(group_total(packets, None, conv_weight), GROUP)
    else:
        last = jnp.stack(packets)[member() ^ (GROUP - 1)][:, HDIM:]
        tail = to_next_group(last)
        total = group_total(packets, tail, conv_weight)[:, 0:HDIM].astype(F32)
        tail = jnp.concatenate([tail[:, 21:24], tail[:, 3:16]], axis=1)
        prefix, passed = jnp.zeros_like(total), total
        for _ in range(groups - 1):
            prefix = to_next_group(passed)
            passed = prefix + total
        incoming = jnp.concatenate([prefix.astype(BF16), tail], axis=1)
    edges = member_edges(packets, conv_weight)
    (incoming, edges), piece2 = beside((2,), (incoming, edges))
    sends = member_prefixes(edges, incoming, conv_weight, gain)
    near = [swapped(sends[j], j) for j in (1, 2)]
    far = swapped(sends[3], 3)
    near, piece3 = beside((3,), near)
    out = finish((0, 1, 2), [sends[0]] + near, [piece01, piece01, piece2], (0, 1, 0), gain)
    return finish((3,), [far], [piece3], (0,), gain, out)


def solution(mesh):
    return jax.shard_map(
        body,
        mesh=mesh,
        in_specs=(
            P(("mp", "ctx"), None),
            P(("mp", "ctx"), None),
            P(("mp", "ctx"), None),
            P("mp", None, None),
            P("mp"),
        ),
        out_specs=P(("mp", "ctx"), None),
        check_vma=False,
    )
```

```python
import functools

import jax
import jax.numpy as jnp
from jax import lax
from jax.experimental import pallas as pl
from jax.experimental.pallas import tpu as pltpu
from jax.sharding import PartitionSpec as P

HDIM = 128
CONV = 4
GROUP = 4
ROWS = 64
CHUNK = 256
PARTS = 4
AHEAD = 2
PAIR = 2
AUX = 32
TAIL = 16
FIX = 16
SCALE = HDIM ** (-0.5)
F32, BF16 = jnp.float32, jnp.bfloat16


def member():
    return lax.rem(lax.axis_index("ctx"), GROUP)


def group():
    return lax.div(lax.axis_index("ctx"), GROUP)


def rows_iota(shape):
    return lax.broadcasted_iota(jnp.int32, shape, 0)


def dot(a, b, dims):
    return lax.dot_general(a, b, (dims, ((), ())), preferred_element_type=F32)


def conv_rows(x, earlier, taps):
    x = x.astype(F32)
    earlier = jnp.zeros((8, HDIM), F32) if earlier is None else earlier.astype(F32)[8:16]
    x = jnp.concatenate([earlier, x], axis=0)
    x1 = pltpu.roll(x, 1, 0)
    late = taps[3:4] * x + taps[2:3] * x1
    early = taps[1:2] * x + taps[0:1] * x1
    return (late + pltpu.roll(early, 2, 0))[8:]


def silu_of_twice(half):
    return half + half * jnp.tanh(half)


def merged_rows(first16, last16):
    first = first16.astype(F32)[0:8]
    last = last16.astype(F32)[8:16]
    return jnp.where(rows_iota((8, HDIM)) < 4, first, last)


def conv_from(wide, rows, taps):
    at = lambda back: wide[rows.start + 8 - back : rows.stop + 8 - back]
    return (taps[3:4] * at(0) + taps[2:3] * at(1)) + (taps[1:2] * at(2) + taps[0:1] * at(3))


def state_kernel(q_hbm, k_hbm, v_hbm, w_hbm, kf_ref, vf_ref, msg_ref, q_ref, w_ref, k_buf, v_buf, wide, k_sem, v_sem, sem):
    pairs, tokens = k_buf.shape[0:2]
    heads = pairs * PAIR

    def fetch(source, target, semaphore, i):
        cols = pl.ds(pl.multiple_of(i * PAIR * HDIM, PAIR * HDIM), PAIR * HDIM)
        return pltpu.make_async_copy(source.at[:, cols], target.at[i], semaphore.at[i])

    def fetch_pair(i):
        fetch(k_hbm, k_buf, k_sem, i).start()
        fetch(v_hbm, v_buf, v_sem, i).start()

    fetch_taps = pltpu.make_async_copy(w_hbm, w_ref, sem.at[0])
    fetch_queries = pltpu.make_async_copy(q_hbm, q_ref, sem.at[1])
    fetch_taps.start()
    for i in range(AHEAD):
        fetch_pair(i)
    for u in range(PAIR):
        for a in range(2):
            wide[u, a, 0:8] = jnp.zeros((8, HDIM), F32)
    fetch_taps.wait()

    def some_heads(i, carry):
        first = i * PAIR

        @pl.when(i + AHEAD < pairs)
        def _():
            fetch_pair(i + AHEAD)

        @pl.when(i + 2 == pairs)
        def _():
            fetch_queries.start()

        fetch(k_hbm, k_buf, k_sem, i).wait()
        for u in range(PAIR):
            h = first + u
            wk = w_ref[1, :, pl.ds(pl.multiple_of(h * HDIM, HDIM), HDIM)] * 0.5
            for start in range(0, tokens, ROWS):
                rows = slice(start, start + ROWS)
                wide[u, 0, start + 8 : start + 8 + ROWS] = k_buf[i, rows, u * HDIM : (u + 1) * HDIM].astype(F32)
                kf = silu_of_twice(conv_from(wide.at[u, 0], rows, wk))
                if start == 0:
                    kf = jnp.where(rows_iota(kf.shape) < CONV - 1, 0.0, kf)
                kf_ref[h, rows] = kf.astype(BF16)
        fetch(v_hbm, v_buf, v_sem, i).wait()
        for u in range(PAIR):
            h = first + u
            cols = pl.ds(pl.multiple_of(h * HDIM, HDIM), HDIM)
            wv = w_ref[2, :, cols]
            local = jnp.zeros((HDIM, HDIM), F32)
            for start in range(0, tokens, ROWS):
                rows = slice(start, start + ROWS)
                wide[u, 1, start + 8 : start + 8 + ROWS] = v_buf[i, rows, u * HDIM : (u + 1) * HDIM].astype(F32)
                vf = conv_from(wide.at[u, 1], rows, wv).astype(BF16)
                vf_ref[h, rows] = vf
                local = local + dot(kf_ref[h, rows], vf, ((0,), (0,)))
            per = heads // GROUP
            place = (lax.div(h, per) ^ member()) * per + lax.rem(h, per)
            msg_ref[place, 0:HDIM] = local.astype(BF16)
            own = slice(u * HDIM, (u + 1) * HDIM)
            mk = merged_rows(k_buf[i, 0:16, own], k_buf[i, tokens - 16 : tokens, own])
            mv = merged_rows(v_buf[i, 0:16, own], v_buf[i, tokens - 16 : tokens, own])
            msg_ref[place, HDIM : HDIM + 16] = jnp.concatenate([mk, mv], axis=0).astype(BF16)
        return carry

    lax.fori_loop(0, heads // PAIR, some_heads, 0)
    fetch_queries.wait()
    for h in range(heads):
        cols = slice(h * HDIM, (h + 1) * HDIM)
        per = heads // GROUP
        place = (h // per ^ member()) * per + h % per
        mq = merged_rows(q_ref[0:16, cols], q_ref[tokens - 16 : tokens, cols])
        msg_ref[place, HDIM + 16 : HDIM + 32] = jnp.concatenate([mq, mq], axis=0).astype(BF16)


VMEM = pl.BlockSpec(memory_space=pltpu.VMEM)
HBM = pl.BlockSpec(memory_space=pltpu.HBM)


def block_states(queries, key_rows, value_rows, conv_weight):
    tokens, width = key_rows.shape
    heads = width // HDIM
    features = jax.ShapeDtypeStruct((heads, tokens, HDIM), BF16)
    arrays = [pltpu.with_memory_space_constraint(a, pltpu.HBM) for a in (queries, key_rows, value_rows, conv_weight)]
    return pl.pallas_call(
        state_kernel,
        in_specs=[HBM, HBM, HBM, HBM],
        out_specs=[VMEM] * 5,
        out_shape=[
            features,
            features,
            jax.ShapeDtypeStruct((heads, HDIM + AUX, HDIM), BF16),
            jax.ShapeDtypeStruct(queries.shape, BF16),
            jax.ShapeDtypeStruct(conv_weight.shape, F32),
        ],
        scratch_shapes=[
            pltpu.VMEM((heads // PAIR, tokens, PAIR * HDIM), BF16),
            pltpu.VMEM((heads // PAIR, tokens, PAIR * HDIM), BF16),
            pltpu.VMEM((PAIR, 2, tokens + 8, HDIM), F32),
            pltpu.SemaphoreType.DMA((heads // PAIR,)),
            pltpu.SemaphoreType.DMA((heads // PAIR,)),
            pltpu.SemaphoreType.DMA((2,)),
        ],
        compiler_params=pltpu.CompilerParams(vmem_limit_bytes=24 << 20),
        cost_estimate=pl.CostEstimate(flops=2 * tokens * width * HDIM, bytes_accessed=8 * tokens * width, transcendentals=tokens * width),
        name="block_states",
    )(*arrays)


def taps_of(w_ref, which, m, h, per):
    return w_ref[which, :, pl.ds(pl.multiple_of((m * per + h) * HDIM, HDIM), HDIM)]


def edge_rows(own, before, taps):
    z = pltpu.roll(jnp.where(rows_iota((8, HDIM)) < 4, own, before), 3, 0)
    y = taps[3:4] * z
    for back in range(1, CONV):
        y = y + taps[3 - back : 4 - back] * pltpu.roll(z, back, 0)
    return y


def edge_only(y):
    rows = rows_iota(y.shape)
    return jnp.where((rows >= 3) & (rows < 6), y, 0.0)


def edge_kv(own, before, wk, wv):
    kf = silu_of_twice(edge_rows(own[0:8], before[0:8], wk * 0.5))
    vf = edge_rows(own[8:16], before[8:16], wv)
    return edge_only(kf), edge_only(vf)


def gather_packets(packets, buf):
    for j, packet in enumerate(packets):
        buf[member() ^ j] = packet[...]


def gather_edges(packets, buf):
    for j, packet in enumerate(packets):
        buf[member() ^ j] = packet[:, HDIM:]


def total_kernel(has_tail, *refs):
    packets, refs = refs[:GROUP], refs[GROUP:]
    if has_tail:
        tail_ref, refs = refs[0], refs[1:]
    w_ref, out_ref, buf = refs
    gather_edges(packets, buf)
    per = out_ref.shape[0]
    for h in range(per):
        wk, wv = (taps_of(w_ref, which, member(), h, per) for which in (1, 2))
        before = tail_ref[h].astype(F32) if has_tail else jnp.zeros((AUX, HDIM), F32)
        kfs, vfs = [], []
        total = sum(packet[h, 0:HDIM].astype(F32) for packet in packets)
        for t in range(GROUP):
            own = buf[t, h].astype(F32)
            kf, vf = edge_kv(own, before, wk, wv)
            kfs.append(kf)
            vfs.append(vf)
            before = own
        kf = jnp.concatenate(kfs, axis=0).astype(BF16)
        vf = jnp.concatenate(vfs, axis=0).astype(BF16)
        total = total + dot(kf, vf, ((0,), (0,)))
        out_ref[h, 0:HDIM] = total.astype(BF16)
        out_ref[h, HDIM:] = pack_tail(before).astype(BF16)


def pack_tail(raw):
    k = jnp.where(rows_iota((8, HDIM)) < 4, pltpu.roll(raw[16:24], 3, 0), raw[0:8])
    return jnp.concatenate([k, raw[8:16]], axis=0)


def unpack_tail(tail):
    q = pltpu.roll(tail[0:8], 5, 0)
    return jnp.concatenate([tail, q, q], axis=0)


def group_total(packets, tail, conv_weight):
    heads = packets[0].shape[0]
    tails = [] if tail is None else [tail]
    return pl.pallas_call(
        functools.partial(total_kernel, tail is not None),
        in_specs=[VMEM] * (GROUP + len(tails) + 1),
        out_specs=VMEM,
        out_shape=jax.ShapeDtypeStruct((heads, HDIM + TAIL, HDIM), BF16),
        scratch_shapes=[pltpu.VMEM((GROUP, heads, AUX, HDIM), BF16)],
        compiler_params=pltpu.CompilerParams(vmem_limit_bytes=8 << 20),
        name="group_total",
    )(*packets, *tails, conv_weight)


def edge_features(own, before, wq, wk, wv):
    kf, vf = edge_kv(own, before, wk, wv)
    qf = silu_of_twice(edge_rows(own[16:24], before[16:24], wq * 0.5)) * SCALE
    blank = jnp.zeros((8, HDIM), F32)
    qf, kf, vf = (jnp.concatenate([a, blank], axis=0).astype(BF16) for a in (edge_only(qf), kf, vf))
    scores = dot(qf, kf, ((1,), (1,)))
    causal = rows_iota(scores.shape) >= lax.broadcasted_iota(jnp.int32, scores.shape, 1)
    scores = jnp.where(causal, scores, 0.0).astype(BF16)
    return qf, dot(scores, vf, ((1,), (0,))), dot(kf, vf, ((0,), (0,)))


def edges_kernel(p0, p1, p2, p3, w_ref, qf_ref, inner_ref, before_ref, with_ref, first_ref, buf):
    gather_packets((p0, p1, p2, p3), buf)
    per = p0.shape[0]
    for h in range(per):
        taps = [taps_of(w_ref, which, member(), h, per) for which in range(3)]
        first_ref[h] = buf[0, h, HDIM:]
        state = buf[0, h, 0:HDIM].astype(F32)
        for t in range(1, GROUP):
            own, before = buf[t, h, HDIM:].astype(F32), buf[t - 1, h, HDIM:].astype(F32)
            qf, inner, first = edge_features(own, before, *taps)
            qf_ref[t - 1, h] = qf
            inner_ref[t - 1, h] = inner
            before_ref[t - 1, h] = state
            state = state + first
            with_ref[t - 1, h] = state
            state = state + buf[t, h, 0:HDIM].astype(F32)


def member_edges(packets, conv_weight):
    heads = packets[0].shape[0]
    later = GROUP - 1
    return pl.pallas_call(
        edges_kernel,
        in_specs=[VMEM] * (GROUP + 1),
        out_specs=[VMEM] * 5,
        out_shape=[
            jax.ShapeDtypeStruct((later, heads, 16, HDIM), BF16),
            jax.ShapeDtypeStruct((later, heads, 16, HDIM), F32),
            jax.ShapeDtypeStruct((later, heads, HDIM, HDIM), F32),
            jax.ShapeDtypeStruct((later, heads, HDIM, HDIM), F32),
            jax.ShapeDtypeStruct((heads, AUX, HDIM), BF16),
        ],
        scratch_shapes=[pltpu.VMEM((GROUP, heads, HDIM + AUX, HDIM), BF16)],
        compiler_params=pltpu.CompilerParams(vmem_limit_bytes=8 << 20),
        name="member_edges",
    )(*packets, conv_weight)


def prefix_kernel(qf_ref, inner_ref, before_ref, with_ref, first_ref, x_ref, w_ref, gain_ref, o0, o1, o2, o3, out):
    later = (group() > 0).astype(F32)
    blank = jnp.zeros((8, HDIM), F32)
    per = x_ref.shape[0]
    for h in range(per):
        taps = [taps_of(w_ref, which, member(), h, per) for which in range(3)]
        gain = gain_ref[:, pl.ds(pl.multiple_of((member() * per + h) * HDIM, HDIM), HDIM)]
        base = x_ref[h, 0:HDIM].astype(F32) * later
        tail = unpack_tail(x_ref[h, HDIM:].astype(F32) * later)
        qf, inner, first = edge_features(first_ref[h].astype(F32), tail, *taps)
        prefix = base
        base = base + first
        shifted = base
        for t in range(GROUP):
            if t:
                qf, inner = qf_ref[t - 1, h], inner_ref[t - 1, h]
                prefix = base + before_ref[t - 1, h]
                shifted = base + with_ref[t - 1, h]
            o = inner + dot(qf, prefix.astype(BF16), ((1,), (0,)))
            o = o * lax.rsqrt(jnp.mean(o * o, axis=1, keepdims=True) + 1e-06) * gain
            out[t, h, 0:HDIM] = shifted.astype(BF16)
            out[t, h, HDIM:] = jnp.concatenate([pltpu.roll(o[0:8], 5, 0), blank], axis=0).astype(BF16)
    for j, o_ref in enumerate((o0, o1, o2, o3)):
        o_ref[...] = out[member() ^ j]


def member_prefixes(edges, incoming, conv_weight, gain):
    heads = incoming.shape[0]
    out = jax.ShapeDtypeStruct((heads, HDIM + FIX, HDIM), BF16)
    return pl.pallas_call(
        prefix_kernel,
        in_specs=[VMEM] * (len(edges) + 3),
        out_specs=[VMEM] * GROUP,
        out_shape=[out] * GROUP,
        scratch_shapes=[pltpu.VMEM((GROUP, heads, HDIM + FIX, HDIM), BF16)],
        compiler_params=pltpu.CompilerParams(vmem_limit_bytes=8 << 20),
        name="member_prefixes",
    )(*edges, incoming, conv_weight, gain)


def inner_kernel(quarters, q_ref, kf_ref, vf_ref, w_ref, qf_ref, inner_ref):
    heads, tokens = qf_ref.shape[0:2]
    per = heads // len(quarters)
    shape = (CHUNK, CHUNK)
    causal = rows_iota(shape) >= lax.broadcasted_iota(jnp.int32, shape, 1)
    for place in range(heads):
        h = (member() ^ quarters[place // per]) * per + place % per
        cols = pl.ds(pl.multiple_of(h * HDIM, HDIM), HDIM)
        wq = w_ref[0, :, cols] * 0.5
        state = None
        for start in range(0, tokens, CHUNK):
            rows = slice(start, start + CHUNK)
            above = q_ref[start - 16 : start, cols] if start else None
            qf = (silu_of_twice(conv_rows(q_ref[rows, cols], above, wq)) * SCALE).astype(BF16)
            qf_ref[place, rows] = qf
            kf, vf = kf_ref[h, rows], vf_ref[h, rows]
            scores = jnp.where(causal, dot(qf, kf, ((1,), (1,))), 0.0).astype(BF16)
            inner = dot(scores, vf, ((1,), (0,)))
            if state is not None:
                inner = inner + dot(qf, state.astype(BF16), ((1,), (0,)))
            inner_ref[place, rows] = inner
            if start + CHUNK < tokens:
                new = dot(kf, vf, ((0,), (0,)))
                state = new if state is None else state + new


def inner_attention(quarters, queries, kf, vf, conv_weight):
    heads, tokens = kf.shape[0:2]
    count = heads // GROUP * len(quarters)
    return pl.pallas_call(
        functools.partial(inner_kernel, quarters),
        in_specs=[VMEM] * 4,
        out_specs=[VMEM] * 2,
        out_shape=[
            jax.ShapeDtypeStruct((count, tokens, HDIM), BF16),
            jax.ShapeDtypeStruct((count, tokens, HDIM), F32),
        ],
        compiler_params=pltpu.CompilerParams(vmem_limit_bytes=24 << 20),
        cost_estimate=pl.CostEstimate(
            flops=8 * count * tokens * HDIM * HDIM,
            bytes_accessed=12 * tokens * count * HDIM,
            transcendentals=tokens * count * HDIM,
        ),
        name="inner_attention",
    )(queries, kf, vf, conv_weight)


def finish_kernel(quarters, places, aliased, gain_ref, *refs):
    n = len(quarters)
    packets, qf_refs, inner_refs, refs = refs[0:n], refs[n : 2 * n], refs[2 * n : 3 * n], refs[3 * n + aliased :]
    out_hbm, out_buf, sem = refs
    per = packets[0].shape[0]
    tokens = out_buf.shape[1]
    part = tokens // PARTS
    there = rows_iota((FIX, HDIM)) < CONV - 1
    copies = []
    for i in range(n):
        quarter = member() ^ quarters[i]
        for c in range(PARTS):
            rows = slice(c * part, (c + 1) * part)
            for h in range(per):
                place = places[i] * per + h
                gain = gain_ref[:, pl.ds(pl.multiple_of((quarter * per + h) * HDIM, HDIM), HDIM)]
                o = inner_refs[i][place, rows] + dot(qf_refs[i][place, rows], packets[i][h, 0:HDIM], ((1,), (0,)))
                o = o * lax.rsqrt(jnp.mean(o * o, axis=1, keepdims=True) + 1e-06) * gain
                if c == 0:
                    fixed = packets[i][h, HDIM:].astype(F32)
                    o = jnp.concatenate([jnp.where(there, fixed, o[0:FIX]), o[FIX:]], axis=0)
                out_buf[i, rows, h * HDIM : (h + 1) * HDIM] = o.astype(BF16)
            cols = pl.ds(pl.multiple_of(quarter * per * HDIM, per * HDIM), per * HDIM)
            copies.append(pltpu.make_async_copy(out_buf.at[i, rows], out_hbm.at[rows, cols], sem.at[i, c]))
            copies[-1].start()
    for copy in copies:
        copy.wait()


def finish(quarters, prefixes, pieces, places, gain, begun=None):
    tokens = pieces[0][0].shape[1]
    width = gain.shape[1]
    n = len(quarters)
    others = [] if begun is None else [begun]
    return pl.pallas_call(
        functools.partial(finish_kernel, quarters, places, len(others)),
        in_specs=[VMEM] * (1 + 3 * n) + [HBM] * len(others),
        out_specs=HBM,
        out_shape=jax.ShapeDtypeStruct((tokens, width), BF16),
        input_output_aliases={1 + 3 * n: 0} if others else {},
        scratch_shapes=[
            pltpu.VMEM((n, tokens, width // GROUP), BF16),
            pltpu.SemaphoreType.DMA((n, PARTS)),
        ],
        compiler_params=pltpu.CompilerParams(vmem_limit_bytes=24 << 20),
        cost_estimate=pl.CostEstimate(
            flops=2 * n * tokens * width // GROUP * HDIM,
            bytes_accessed=8 * n * tokens * width // GROUP,
            transcendentals=n * tokens * width // GROUP // HDIM,
        ),
        name="finish",
    )(gain, *prefixes, *[p[0] for p in pieces], *[p[1] for p in pieces], *others)


def swapped(value, bits):
    count = lax.axis_size("ctx")
    return lax.ppermute(value, "ctx", [(s, s ^ bits) for s in range(count)])


def to_next_group(value):
    count = lax.axis_size("ctx")
    return lax.ppermute(value, "ctx", [(s, s + GROUP) for s in range(count - GROUP)])


def body(queries, key_rows, value_rows, conv_weight, head_gain):
    width = queries.shape[1]
    heads = width // GROUP // HDIM
    groups = lax.axis_size("ctx") // GROUP
    gain = head_gain.reshape(1, width)
    kf, vf, messages, queries, conv_weight = block_states(queries, key_rows, value_rows, conv_weight)

    def beside(quarters, arrays):
        piece = inner_attention(quarters, queries, kf, vf, conv_weight)
        return lax.optimization_barrier((arrays, piece))

    packets = [swapped(messages[j * heads : (j + 1) * heads], j) for j in (3, 2, 1)]
    packets, piece01 = beside((0, 1), packets)
    packets = [messages[0:heads]] + packets[::-1]
    if groups == 2:
        incoming = swapped(group_total(packets, None, conv_weight), GROUP)
    else:
        last = jnp.stack(packets)[member() ^ (GROUP - 1)][:, HDIM:]
        tail = to_next_group(last)
        total = group_total(packets, tail, conv_weight)[:, 0:HDIM].astype(F32)
        tail = jnp.concatenate([tail[:, 21:24], tail[:, 3:16]], axis=1)
        prefix, passed = jnp.zeros_like(total), total
        for _ in range(groups - 1):
            prefix = to_next_group(passed)
            passed = prefix + total
        incoming = jnp.concatenate([prefix.astype(BF16), tail], axis=1)
    edges = member_edges(packets, conv_weight)
    (incoming, edges), piece2 = beside((2,), (incoming, edges))
    sends = member_prefixes(edges, incoming, conv_weight, gain)
    near = [swapped(sends[j], j) for j in (1, 2)]
    far = swapped(sends[3], 3)
    near, piece3 = beside((3,), near)
    out = finish((0, 1, 2), [sends[0]] + near, [piece01, piece01, piece2], (0, 1, 0), gain)
    return finish((3,), [far], [piece3], (0,), gain, out)


def solution(mesh):
    return jax.shard_map(
        body,
        mesh=mesh,
        in_specs=(
            P(("mp", "ctx"), None),
            P(("mp", "ctx"), None),
            P(("mp", "ctx"), None),
            P("mp", None, None),
            P("mp"),
        ),
        out_specs=P(("mp", "ctx"), None),
        check_vma=False,
    )
```

```python
import functools

import jax
import jax.numpy as jnp
from jax import lax
from jax.experimental import pallas as pl
from jax.experimental.pallas import tpu as pltpu
from jax.sharding import PartitionSpec as P

HDIM = 128
CONV = 4
GROUP = 4
ROWS = 64
CHUNK = 256
PARTS = 4
AHEAD = 1
PAIR = 4
AUX = 32
TAIL = 16
FIX = 16
SCALE = HDIM ** (-0.5)
F32, BF16 = jnp.float32, jnp.bfloat16


def member():
    return lax.rem(lax.axis_index("ctx"), GROUP)


def group():
    return lax.div(lax.axis_index("ctx"), GROUP)


def rows_iota(shape):
    return lax.broadcasted_iota(jnp.int32, shape, 0)


def dot(a, b, dims):
    return lax.dot_general(a, b, (dims, ((), ())), preferred_element_type=F32)


def conv_rows(x, earlier, taps):
    x = x.astype(F32)
    earlier = jnp.zeros((8, HDIM), F32) if earlier is None else earlier.astype(F32)[8:16]
    x = jnp.concatenate([earlier, x], axis=0)
    x1 = pltpu.roll(x, 1, 0)
    late = taps[3:4] * x + taps[2:3] * x1
    early = taps[1:2] * x + taps[0:1] * x1
    return (late + pltpu.roll(early, 2, 0))[8:]


def silu_of_twice(half):
    return half + half * jnp.tanh(half)


def merged_rows(first16, last16):
    first = first16.astype(F32)[0:8]
    last = last16.astype(F32)[8:16]
    return jnp.where(rows_iota((8, HDIM)) < 4, first, last)


def conv_from(wide, rows, taps):
    at = lambda back: wide[rows.start + 8 - back : rows.stop + 8 - back]
    return (taps[3:4] * at(0) + taps[2:3] * at(1)) + (taps[1:2] * at(2) + taps[0:1] * at(3))


def state_kernel(q_hbm, k_hbm, v_hbm, w_hbm, kf_ref, vf_ref, msg_ref, q_ref, w_ref, k_buf, v_buf, wide, k_sem, v_sem, sem):
    pairs, tokens = k_buf.shape[0:2]
    heads = pairs * PAIR

    def fetch(source, target, semaphore, i):
        cols = pl.ds(pl.multiple_of(i * PAIR * HDIM, PAIR * HDIM), PAIR * HDIM)
        return pltpu.make_async_copy(source.at[:, cols], target.at[i], semaphore.at[i])

    def fetch_pair(i):
        fetch(k_hbm, k_buf, k_sem, i).start()
        fetch(v_hbm, v_buf, v_sem, i).start()

    fetch_taps = pltpu.make_async_copy(w_hbm, w_ref, sem.at[0])
    fetch_queries = pltpu.make_async_copy(q_hbm, q_ref, sem.at[1])
    fetch_taps.start()
    for i in range(AHEAD):
        fetch_pair(i)
    for u in range(PAIR):
        for a in range(2):
            wide[u, a, 0:8] = jnp.zeros((8, HDIM), F32)
    fetch_taps.wait()

    def some_heads(i, carry):
        first = i * PAIR

        @pl.when(i + AHEAD < pairs)
        def _():
            fetch_pair(i + AHEAD)

        @pl.when(i + 2 == pairs)
        def _():
            fetch_queries.start()

        fetch(k_hbm, k_buf, k_sem, i).wait()
        for u in range(PAIR):
            h = first + u
            wk = w_ref[1, :, pl.ds(pl.multiple_of(h * HDIM, HDIM), HDIM)] * 0.5
            for start in range(0, tokens, ROWS):
                rows = slice(start, start + ROWS)
                wide[u, 0, start + 8 : start + 8 + ROWS] = k_buf[i, rows, u * HDIM : (u + 1) * HDIM].astype(F32)
                kf = silu_of_twice(conv_from(wide.at[u, 0], rows, wk))
                if start == 0:
                    kf = jnp.where(rows_iota(kf.shape) < CONV - 1, 0.0, kf)
                kf_ref[h, rows] = kf.astype(BF16)
        fetch(v_hbm, v_buf, v_sem, i).wait()
        for u in range(PAIR):
            h = first + u
            cols = pl.ds(pl.multiple_of(h * HDIM, HDIM), HDIM)
            wv = w_ref[2, :, cols]
            local = jnp.zeros((HDIM, HDIM), F32)
            for start in range(0, tokens, ROWS):
                rows = slice(start, start + ROWS)
                wide[u, 1, start + 8 : start + 8 + ROWS] = v_buf[i, rows, u * HDIM : (u + 1) * HDIM].astype(F32)
                vf = conv_from(wide.at[u, 1], rows, wv).astype(BF16)
                vf_ref[h, rows] = vf
                local = local + dot(kf_ref[h, rows], vf, ((0,), (0,)))
            per = heads // GROUP
            place = (lax.div(h, per) ^ member()) * per + lax.rem(h, per)
            msg_ref[place, 0:HDIM] = local.astype(BF16)
            own = slice(u * HDIM, (u + 1) * HDIM)
            mk = merged_rows(k_buf[i, 0:16, own], k_buf[i, tokens - 16 : tokens, own])
            mv = merged_rows(v_buf[i, 0:16, own], v_buf[i, tokens - 16 : tokens, own])
            msg_ref[place, HDIM : HDIM + 16] = jnp.concatenate([mk, mv], axis=0).astype(BF16)
        return carry

    lax.fori_loop(0, heads // PAIR, some_heads, 0)
    fetch_queries.wait()
    for h in range(heads):
        cols = slice(h * HDIM, (h + 1) * HDIM)
        per = heads // GROUP
        place = (h // per ^ member()) * per + h % per
        mq = merged_rows(q_ref[0:16, cols], q_ref[tokens - 16 : tokens, cols])
        msg_ref[place, HDIM + 16 : HDIM + 32] = jnp.concatenate([mq, mq], axis=0).astype(BF16)


VMEM = pl.BlockSpec(memory_space=pltpu.VMEM)
HBM = pl.BlockSpec(memory_space=pltpu.HBM)


def block_states(queries, key_rows, value_rows, conv_weight):
    tokens, width = key_rows.shape
    heads = width // HDIM
    features = jax.ShapeDtypeStruct((heads, tokens, HDIM), BF16)
    arrays = [pltpu.with_memory_space_constraint(a, pltpu.HBM) for a in (queries, key_rows, value_rows, conv_weight)]
    return pl.pallas_call(
        state_kernel,
        in_specs=[HBM, HBM, HBM, HBM],
        out_specs=[VMEM] * 5,
        out_shape=[
            features,
            features,
            jax.ShapeDtypeStruct((heads, HDIM + AUX, HDIM), BF16),
            jax.ShapeDtypeStruct(queries.shape, BF16),
            jax.ShapeDtypeStruct(conv_weight.shape, F32),
        ],
        scratch_shapes=[
            pltpu.VMEM((heads // PAIR, tokens, PAIR * HDIM), BF16),
            pltpu.VMEM((heads // PAIR, tokens, PAIR * HDIM), BF16),
            pltpu.VMEM((PAIR, 2, tokens + 8, HDIM), F32),
            pltpu.SemaphoreType.DMA((heads // PAIR,)),
            pltpu.SemaphoreType.DMA((heads // PAIR,)),
            pltpu.SemaphoreType.DMA((2,)),
        ],
        compiler_params=pltpu.CompilerParams(vmem_limit_bytes=24 << 20),
        cost_estimate=pl.CostEstimate(flops=2 * tokens * width * HDIM, bytes_accessed=8 * tokens * width, transcendentals=tokens * width),
        name="block_states",
    )(*arrays)


def taps_of(w_ref, which, m, h, per):
    return w_ref[which, :, pl.ds(pl.multiple_of((m * per + h) * HDIM, HDIM), HDIM)]


def edge_rows(own, before, taps):
    z = pltpu.roll(jnp.where(rows_iota((8, HDIM)) < 4, own, before), 3, 0)
    y = taps[3:4] * z
    for back in range(1, CONV):
        y = y + taps[3 - back : 4 - back] * pltpu.roll(z, back, 0)
    return y


def edge_only(y):
    rows = rows_iota(y.shape)
    return jnp.where((rows >= 3) & (rows < 6), y, 0.0)


def edge_kv(own, before, wk, wv):
    kf = silu_of_twice(edge_rows(own[0:8], before[0:8], wk * 0.5))
    vf = edge_rows(own[8:16], before[8:16], wv)
    return edge_only(kf), edge_only(vf)


def gather_packets(packets, buf):
    for j, packet in enumerate(packets):
        buf[member() ^ j] = packet[...]


def gather_edges(packets, buf):
    for j, packet in enumerate(packets):
        buf[member() ^ j] = packet[:, HDIM:]


def total_kernel(has_tail, *refs):
    packets, refs = refs[:GROUP], refs[GROUP:]
    if has_tail:
        tail_ref, refs = refs[0], refs[1:]
    w_ref, out_ref, buf = refs
    gather_edges(packets, buf)
    per = out_ref.shape[0]
    for h in range(per):
        wk, wv = (taps_of(w_ref, which, member(), h, per) for which in (1, 2))
        before = tail_ref[h].astype(F32) if has_tail else jnp.zeros((AUX, HDIM), F32)
        kfs, vfs = [], []
        total = sum(packet[h, 0:HDIM].astype(F32) for packet in packets)
        for t in range(GROUP):
            own = buf[t, h].astype(F32)
            kf, vf = edge_kv(own, before, wk, wv)
            kfs.append(kf)
            vfs.append(vf)
            before = own
        kf = jnp.concatenate(kfs, axis=0).astype(BF16)
        vf = jnp.concatenate(vfs, axis=0).astype(BF16)
        total = total + dot(kf, vf, ((0,), (0,)))
        out_ref[h, 0:HDIM] = total.astype(BF16)
        out_ref[h, HDIM:] = pack_tail(before).astype(BF16)


def pack_tail(raw):
    k = jnp.where(rows_iota((8, HDIM)) < 4, pltpu.roll(raw[16:24], 3, 0), raw[0:8])
    return jnp.concatenate([k, raw[8:16]], axis=0)


def unpack_tail(tail):
    q = pltpu.roll(tail[0:8], 5, 0)
    return jnp.concatenate([tail, q, q], axis=0)


def group_total(packets, tail, conv_weight):
    heads = packets[0].shape[0]
    tails = [] if tail is None else [tail]
    return pl.pallas_call(
        functools.partial(total_kernel, tail is not None),
        in_specs=[VMEM] * (GROUP + len(tails) + 1),
        out_specs=VMEM,
        out_shape=jax.ShapeDtypeStruct((heads, HDIM + TAIL, HDIM), BF16),
        scratch_shapes=[pltpu.VMEM((GROUP, heads, AUX, HDIM), BF16)],
        compiler_params=pltpu.CompilerParams(vmem_limit_bytes=8 << 20),
        name="group_total",
    )(*packets, *tails, conv_weight)


def edge_features(own, before, wq, wk, wv):
    kf, vf = edge_kv(own, before, wk, wv)
    qf = silu_of_twice(edge_rows(own[16:24], before[16:24], wq * 0.5)) * SCALE
    blank = jnp.zeros((8, HDIM), F32)
    qf, kf, vf = (jnp.concatenate([a, blank], axis=0).astype(BF16) for a in (edge_only(qf), kf, vf))
    scores = dot(qf, kf, ((1,), (1,)))
    causal = rows_iota(scores.shape) >= lax.broadcasted_iota(jnp.int32, scores.shape, 1)
    scores = jnp.where(causal, scores, 0.0).astype(BF16)
    return qf, dot(scores, vf, ((1,), (0,))), dot(kf, vf, ((0,), (0,)))


def edges_kernel(p0, p1, p2, p3, w_ref, qf_ref, inner_ref, before_ref, with_ref, first_ref, buf):
    gather_packets((p0, p1, p2, p3), buf)
    per = p0.shape[0]
    for h in range(per):
        taps = [taps_of(w_ref, which, member(), h, per) for which in range(3)]
        first_ref[h] = buf[0, h, HDIM:]
        state = buf[0, h, 0:HDIM].astype(F32)
        for t in range(1, GROUP):
            own, before = buf[t, h, HDIM:].astype(F32), buf[t - 1, h, HDIM:].astype(F32)
            qf, inner, first = edge_features(own, before, *taps)
            qf_ref[t - 1, h] = qf
            inner_ref[t - 1, h] = inner
            before_ref[t - 1, h] = state
            state = state + first
            with_ref[t - 1, h] = state
            state = state + buf[t, h, 0:HDIM].astype(F32)


def member_edges(packets, conv_weight):
    heads = packets[0].shape[0]
    later = GROUP - 1
    return pl.pallas_call(
        edges_kernel,
        in_specs=[VMEM] * (GROUP + 1),
        out_specs=[VMEM] * 5,
        out_shape=[
            jax.ShapeDtypeStruct((later, heads, 16, HDIM), BF16),
            jax.ShapeDtypeStruct((later, heads, 16, HDIM), F32),
            jax.ShapeDtypeStruct((later, heads, HDIM, HDIM), F32),
            jax.ShapeDtypeStruct((later, heads, HDIM, HDIM), F32),
            jax.ShapeDtypeStruct((heads, AUX, HDIM), BF16),
        ],
        scratch_shapes=[pltpu.VMEM((GROUP, heads, HDIM + AUX, HDIM), BF16)],
        compiler_params=pltpu.CompilerParams(vmem_limit_bytes=8 << 20),
        name="member_edges",
    )(*packets, conv_weight)


def prefix_kernel(qf_ref, inner_ref, before_ref, with_ref, first_ref, x_ref, w_ref, gain_ref, o0, o1, o2, o3, out):
    later = (group() > 0).astype(F32)
    blank = jnp.zeros((8, HDIM), F32)
    per = x_ref.shape[0]
    for h in range(per):
        taps = [taps_of(w_ref, which, member(), h, per) for which in range(3)]
        gain = gain_ref[:, pl.ds(pl.multiple_of((member() * per + h) * HDIM, HDIM), HDIM)]
        base = x_ref[h, 0:HDIM].astype(F32) * later
        tail = unpack_tail(x_ref[h, HDIM:].astype(F32) * later)
        qf, inner, first = edge_features(first_ref[h].astype(F32), tail, *taps)
        prefix = base
        base = base + first
        shifted = base
        for t in range(GROUP):
            if t:
                qf, inner = qf_ref[t - 1, h], inner_ref[t - 1, h]
                prefix = base + before_ref[t - 1, h]
                shifted = base + with_ref[t - 1, h]
            o = inner + dot(qf, prefix.astype(BF16), ((1,), (0,)))
            o = o * lax.rsqrt(jnp.mean(o * o, axis=1, keepdims=True) + 1e-06) * gain
            out[t, h, 0:HDIM] = shifted.astype(BF16)
            out[t, h, HDIM:] = jnp.concatenate([pltpu.roll(o[0:8], 5, 0), blank], axis=0).astype(BF16)
    for j, o_ref in enumerate((o0, o1, o2, o3)):
        o_ref[...] = out[member() ^ j]


def member_prefixes(edges, incoming, conv_weight, gain):
    heads = incoming.shape[0]
    out = jax.ShapeDtypeStruct((heads, HDIM + FIX, HDIM), BF16)
    return pl.pallas_call(
        prefix_kernel,
        in_specs=[VMEM] * (len(edges) + 3),
        out_specs=[VMEM] * GROUP,
        out_shape=[out] * GROUP,
        scratch_shapes=[pltpu.VMEM((GROUP, heads, HDIM + FIX, HDIM), BF16)],
        compiler_params=pltpu.CompilerParams(vmem_limit_bytes=8 << 20),
        name="member_prefixes",
    )(*edges, incoming, conv_weight, gain)


def inner_kernel(quarters, q_ref, kf_ref, vf_ref, w_ref, qf_ref, inner_ref):
    heads, tokens = qf_ref.shape[0:2]
    per = heads // len(quarters)
    shape = (CHUNK, CHUNK)
    causal = rows_iota(shape) >= lax.broadcasted_iota(jnp.int32, shape, 1)
    for place in range(heads):
        h = (member() ^ quarters[place // per]) * per + place % per
        cols = pl.ds(pl.multiple_of(h * HDIM, HDIM), HDIM)
        wq = w_ref[0, :, cols] * 0.5
        state = None
        for start in range(0, tokens, CHUNK):
            rows = slice(start, start + CHUNK)
            above = q_ref[start - 16 : start, cols] if start else None
            qf = (silu_of_twice(conv_rows(q_ref[rows, cols], above, wq)) * SCALE).astype(BF16)
            qf_ref[place, rows] = qf
            kf, vf = kf_ref[h, rows], vf_ref[h, rows]
            scores = jnp.where(causal, dot(qf, kf, ((1,), (1,))), 0.0).astype(BF16)
            inner = dot(scores, vf, ((1,), (0,)))
            if state is not None:
                inner = inner + dot(qf, state.astype(BF16), ((1,), (0,)))
            inner_ref[place, rows] = inner
            if start + CHUNK < tokens:
                new = dot(kf, vf, ((0,), (0,)))
                state = new if state is None else state + new


def inner_attention(quarters, queries, kf, vf, conv_weight):
    heads, tokens = kf.shape[0:2]
    count = heads // GROUP * len(quarters)
    return pl.pallas_call(
        functools.partial(inner_kernel, quarters),
        in_specs=[VMEM] * 4,
        out_specs=[VMEM] * 2,
        out_shape=[
            jax.ShapeDtypeStruct((count, tokens, HDIM), BF16),
            jax.ShapeDtypeStruct((count, tokens, HDIM), F32),
        ],
        compiler_params=pltpu.CompilerParams(vmem_limit_bytes=24 << 20),
        cost_estimate=pl.CostEstimate(
            flops=8 * count * tokens * HDIM * HDIM,
            bytes_accessed=12 * tokens * count * HDIM,
            transcendentals=tokens * count * HDIM,
        ),
        name="inner_attention",
    )(queries, kf, vf, conv_weight)


def finish_kernel(quarters, places, aliased, gain_ref, *refs):
    n = len(quarters)
    packets, qf_refs, inner_refs, refs = refs[0:n], refs[n : 2 * n], refs[2 * n : 3 * n], refs[3 * n + aliased :]
    out_hbm, out_buf, sem = refs
    per = packets[0].shape[0]
    tokens = out_buf.shape[1]
    part = tokens // PARTS
    there = rows_iota((FIX, HDIM)) < CONV - 1
    copies = []
    for i in range(n):
        quarter = member() ^ quarters[i]
        for c in range(PARTS):
            rows = slice(c * part, (c + 1) * part)
            for h in range(per):
                place = places[i] * per + h
                gain = gain_ref[:, pl.ds(pl.multiple_of((quarter * per + h) * HDIM, HDIM), HDIM)]
                o = inner_refs[i][place, rows] + dot(qf_refs[i][place, rows], packets[i][h, 0:HDIM], ((1,), (0,)))
                o = o * lax.rsqrt(jnp.mean(o * o, axis=1, keepdims=True) + 1e-06) * gain
                if c == 0:
                    fixed = packets[i][h, HDIM:].astype(F32)
                    o = jnp.concatenate([jnp.where(there, fixed, o[0:FIX]), o[FIX:]], axis=0)
                out_buf[i, rows, h * HDIM : (h + 1) * HDIM] = o.astype(BF16)
            cols = pl.ds(pl.multiple_of(quarter * per * HDIM, per * HDIM), per * HDIM)
            copies.append(pltpu.make_async_copy(out_buf.at[i, rows], out_hbm.at[rows, cols], sem.at[i, c]))
            copies[-1].start()
    for copy in copies:
        copy.wait()


def finish(quarters, prefixes, pieces, places, gain, begun=None):
    tokens = pieces[0][0].shape[1]
    width = gain.shape[1]
    n = len(quarters)
    others = [] if begun is None else [begun]
    return pl.pallas_call(
        functools.partial(finish_kernel, quarters, places, len(others)),
        in_specs=[VMEM] * (1 + 3 * n) + [HBM] * len(others),
        out_specs=HBM,
        out_shape=jax.ShapeDtypeStruct((tokens, width), BF16),
        input_output_aliases={1 + 3 * n: 0} if others else {},
        scratch_shapes=[
            pltpu.VMEM((n, tokens, width // GROUP), BF16),
            pltpu.SemaphoreType.DMA((n, PARTS)),
        ],
        compiler_params=pltpu.CompilerParams(vmem_limit_bytes=24 << 20),
        cost_estimate=pl.CostEstimate(
            flops=2 * n * tokens * width // GROUP * HDIM,
            bytes_accessed=8 * n * tokens * width // GROUP,
            transcendentals=n * tokens * width // GROUP // HDIM,
        ),
        name="finish",
    )(gain, *prefixes, *[p[0] for p in pieces], *[p[1] for p in pieces], *others)


def swapped(value, bits):
    count = lax.axis_size("ctx")
    return lax.ppermute(value, "ctx", [(s, s ^ bits) for s in range(count)])


def to_next_group(value):
    count = lax.axis_size("ctx")
    return lax.ppermute(value, "ctx", [(s, s + GROUP) for s in range(count - GROUP)])


def body(queries, key_rows, value_rows, conv_weight, head_gain):
    width = queries.shape[1]
    heads = width // GROUP // HDIM
    groups = lax.axis_size("ctx") // GROUP
    gain = head_gain.reshape(1, width)
    kf, vf, messages, queries, conv_weight = block_states(queries, key_rows, value_rows, conv_weight)

    def beside(quarters, arrays):
        piece = inner_attention(quarters, queries, kf, vf, conv_weight)
        return lax.optimization_barrier((arrays, piece))

    packets = [swapped(messages[j * heads : (j + 1) * heads], j) for j in (3, 2, 1)]
    packets, piece_a = beside((0, 3), packets)
    packets = [messages[0:heads]] + packets[::-1]
    if groups == 2:
        incoming = swapped(group_total(packets, None, conv_weight), GROUP)
    else:
        last = jnp.stack(packets)[member() ^ (GROUP - 1)][:, HDIM:]
        tail = to_next_group(last)
        total = group_total(packets, tail, conv_weight)[:, 0:HDIM].astype(F32)
        tail = jnp.concatenate([tail[:, 21:24], tail[:, 3:16]], axis=1)
        prefix, passed = jnp.zeros_like(total), total
        for _ in range(groups - 1):
            prefix = to_next_group(passed)
            passed = prefix + total
        incoming = jnp.concatenate([prefix.astype(BF16), tail], axis=1)
    edges = member_edges(packets, conv_weight)
    (incoming, edges), piece_b = beside((2,), (incoming, edges))
    sends = member_prefixes(edges, incoming, conv_weight, gain)
    first = [swapped(sends[j], j) for j in (3,)]
    last = [swapped(sends[j], j) for j in (2, 1)]
    first, piece_c = beside((1,), first)
    out = finish((0, 3), [sends[0]] + first, [piece_a, piece_a], (0, 1, ), gain)
    return finish((2, 1), last, [piece_b, piece_c], (0, 0, ), gain, out)


def solution(mesh):
    return jax.shard_map(
        body,
        mesh=mesh,
        in_specs=(
            P(("mp", "ctx"), None),
            P(("mp", "ctx"), None),
            P(("mp", "ctx"), None),
            P("mp", None, None),
            P("mp"),
        ),
        out_specs=P(("mp", "ctx"), None),
        check_vma=False,
    )
```

```python
import functools

import jax
import jax.numpy as jnp
from jax import lax
from jax.experimental import pallas as pl
from jax.experimental.pallas import tpu as pltpu
from jax.sharding import PartitionSpec as P

HDIM = 128
CONV = 4
GROUP = 4
ROWS = 64
CHUNK = 256
PARTS = 4
AUX = 32
TAIL = 16
FIX = 16
SCALE = HDIM ** (-0.5)
F32, BF16 = jnp.float32, jnp.bfloat16


def member():
    return lax.rem(lax.axis_index("ctx"), GROUP)


def group():
    return lax.div(lax.axis_index("ctx"), GROUP)


def rows_iota(shape):
    return lax.broadcasted_iota(jnp.int32, shape, 0)


def dot(a, b, dims):
    return lax.dot_general(a, b, (dims, ((), ())), preferred_element_type=F32)


def conv_rows(x, earlier, taps):
    x = x.astype(F32)
    earlier = jnp.zeros((8, HDIM), F32) if earlier is None else earlier.astype(F32)[8:16]
    x = jnp.concatenate([earlier, x], axis=0)
    x1 = pltpu.roll(x, 1, 0)
    late = taps[3:4] * x + taps[2:3] * x1
    early = taps[1:2] * x + taps[0:1] * x1
    return (late + pltpu.roll(early, 2, 0))[8:]


def silu_of_twice(half):
    return half + half * jnp.tanh(half)


def merged_rows(first16, last16):
    first = first16.astype(F32)[0:8]
    last = last16.astype(F32)[8:16]
    return jnp.where(rows_iota((8, HDIM)) < 4, first, last)


def conv_from(wide, rows, taps):
    at = lambda back: wide[rows.start + 8 - back : rows.stop + 8 - back]
    return (taps[3:4] * at(0) + taps[2:3] * at(1)) + (taps[1:2] * at(2) + taps[0:1] * at(3))


def heads_of(quarter, per):
    return [pl.ds(pl.multiple_of((quarter * per + u) * HDIM, HDIM), HDIM) for u in range(per)]


def key_features(n, quarter, k_ref, w_ref, kf_ref, wide):
    tokens, per = k_ref.shape[1], k_ref.shape[2] // HDIM
    for u, cols in enumerate(heads_of(quarter, per)):
        wk = w_ref[1, :, cols] * 0.5
        for start in range(0, tokens, ROWS):
            rows = slice(start, start + ROWS)
            wide[n, u, 0, start + 8 : start + 8 + ROWS] = k_ref[n, rows, u * HDIM : (u + 1) * HDIM].astype(F32)
            kf = silu_of_twice(conv_from(wide.at[n, u, 0], rows, wk))
            if start == 0:
                kf = jnp.where(rows_iota(kf.shape) < CONV - 1, 0.0, kf)
            kf_ref[n * per + u, rows] = kf.astype(BF16)


def states(n, quarter, k_ref, v_ref, w_ref, kf_ref, vf_ref, msg_ref, wide):
    tokens, per = v_ref.shape[1], v_ref.shape[2] // HDIM
    for u, cols in enumerate(heads_of(quarter, per)):
        own = slice(u * HDIM, (u + 1) * HDIM)
        wv = w_ref[2, :, cols]
        local = jnp.zeros((HDIM, HDIM), F32)
        for start in range(0, tokens, ROWS):
            rows = slice(start, start + ROWS)
            wide[n, u, 1, start + 8 : start + 8 + ROWS] = v_ref[n, rows, own].astype(F32)
            vf = conv_from(wide.at[n, u, 1], rows, wv).astype(BF16)
            vf_ref[n * per + u, rows] = vf
            local = local + dot(kf_ref[n * per + u, rows], vf, ((0,), (0,)))
        msg_ref[n * per + u, 0:HDIM] = local.astype(BF16)
        mk = merged_rows(k_ref[n, 0:16, own], k_ref[n, tokens - 16 : tokens, own])
        mv = merged_rows(v_ref[n, 0:16, own], v_ref[n, tokens - 16 : tokens, own])
        msg_ref[n * per + u, HDIM : HDIM + 16] = jnp.concatenate([mk, mv], axis=0).astype(BF16)


def query_rows(n, quarter, per, q_ref, msg_ref):
    tokens = q_ref.shape[0]
    for u, cols in enumerate(heads_of(quarter, per)):
        mq = merged_rows(q_ref[0:16, cols], q_ref[tokens - 16 : tokens, cols])
        msg_ref[n * per + u, HDIM + 16 : HDIM + 32] = jnp.concatenate([mq, mq], axis=0).astype(BF16)


def clear_above(wide):
    for n in range(wide.shape[0]):
        for u in range(wide.shape[1]):
            for a in range(2):
                wide[n, u, a, 0:8] = jnp.zeros((8, HDIM), F32)


def early_kernel(quarters, q_hbm, k_hbm, v_hbm, w_hbm, kf_ref, vf_ref, msg_ref, k_rest, v_rest, q_ref, w_ref, k_buf, v_buf, wide, k_sem, v_sem, sem):
    count, tokens, part = k_buf.shape
    per = part // HDIM
    mine = [member() ^ j for j in quarters]

    def fetch(source, target, rest, semaphore, n):
        cols = pl.ds(pl.multiple_of(mine[n] * part, part), part)
        place = target.at[n] if n < count else rest.at[0]
        return pltpu.make_async_copy(source.at[:, cols], place, semaphore.at[n])

    fetch_k = [fetch(k_hbm, k_buf, k_rest, k_sem, n) for n in range(GROUP)]
    fetch_v = [fetch(v_hbm, v_buf, v_rest, v_sem, n) for n in range(GROUP)]
    fetch_taps = pltpu.make_async_copy(w_hbm, w_ref, sem.at[0])
    fetch_queries = pltpu.make_async_copy(q_hbm, q_ref, sem.at[1])

    def keys(n):
        key_features(n, mine[n], k_buf, w_ref, kf_ref, wide)

    def values(n):
        states(n, mine[n], k_buf, v_buf, w_ref, kf_ref, vf_ref, msg_ref, wide)

    for copy in (fetch_taps, fetch_k[0], fetch_v[0], fetch_k[1]):
        copy.start()
    clear_above(wide)
    fetch_taps.wait()
    fetch_k[0].wait()
    for copy in (fetch_v[1], fetch_k[2], fetch_v[2]):
        copy.start()
    keys(0)
    fetch_v[0].wait()
    fetch_k[1].wait()
    for copy in (fetch_k[3], fetch_v[3], fetch_queries):
        copy.start()
    values(0)
    keys(1)
    fetch_v[1].wait()
    fetch_k[2].wait()
    values(1)
    keys(2)
    fetch_v[2].wait()
    values(2)
    fetch_queries.wait()
    for n in range(count):
        query_rows(n, mine[n], per, q_ref, msg_ref)
    fetch_k[3].wait()
    fetch_v[3].wait()


def own_kernel(k_ref, v_ref, q_ref, w_ref, kf_ref, vf_ref, msg_ref, wide):
    per = k_ref.shape[2] // HDIM
    clear_above(wide)
    key_features(0, member(), k_ref, w_ref, kf_ref, wide)
    states(0, member(), k_ref, v_ref, w_ref, kf_ref, vf_ref, msg_ref, wide)
    query_rows(0, member(), per, q_ref, msg_ref)


VMEM = pl.BlockSpec(memory_space=pltpu.VMEM)
HBM = pl.BlockSpec(memory_space=pltpu.HBM)


def state_cost(tokens, width):
    return pl.CostEstimate(flops=2 * tokens * width * HDIM, bytes_accessed=8 * tokens * width, transcendentals=tokens * width)


def early_states(quarters, queries, key_rows, value_rows, conv_weight):
    tokens, width = key_rows.shape
    count, part = len(quarters) - 1, width // GROUP
    per = part // HDIM
    features = jax.ShapeDtypeStruct((count * per, tokens, HDIM), BF16)
    rest = jax.ShapeDtypeStruct((1, tokens, part), BF16)
    arrays = [pltpu.with_memory_space_constraint(a, pltpu.HBM) for a in (queries, key_rows, value_rows, conv_weight)]
    return pl.pallas_call(
        functools.partial(early_kernel, quarters),
        in_specs=[HBM] * 4,
        out_specs=[VMEM] * 7,
        out_shape=[
            features,
            features,
            jax.ShapeDtypeStruct((count * per, HDIM + AUX, HDIM), BF16),
            rest,
            rest,
            jax.ShapeDtypeStruct(queries.shape, BF16),
            jax.ShapeDtypeStruct(conv_weight.shape, F32),
        ],
        scratch_shapes=[
            pltpu.VMEM((count, tokens, part), BF16),
            pltpu.VMEM((count, tokens, part), BF16),
            pltpu.VMEM((count, per, 2, tokens + 8, HDIM), F32),
            pltpu.SemaphoreType.DMA((GROUP,)),
            pltpu.SemaphoreType.DMA((GROUP,)),
            pltpu.SemaphoreType.DMA((2,)),
        ],
        compiler_params=pltpu.CompilerParams(vmem_limit_bytes=28 << 20),
        cost_estimate=state_cost(tokens, width),
        name="early_states",
    )(*arrays)


def own_states(k_rest, v_rest, queries, conv_weight):
    tokens, part = k_rest.shape[1:3]
    per = part // HDIM
    features = jax.ShapeDtypeStruct((per, tokens, HDIM), BF16)
    return pl.pallas_call(
        own_kernel,
        in_specs=[VMEM] * 4,
        out_specs=[VMEM] * 3,
        out_shape=[features, features, jax.ShapeDtypeStruct((per, HDIM + AUX, HDIM), BF16)],
        scratch_shapes=[pltpu.VMEM((1, per, 2, tokens + 8, HDIM), F32)],
        compiler_params=pltpu.CompilerParams(vmem_limit_bytes=16 << 20),
        cost_estimate=state_cost(tokens, part),
        name="own_states",
    )(k_rest, v_rest, queries, conv_weight)


def taps_of(w_ref, which, m, h, per):
    return w_ref[which, :, pl.ds(pl.multiple_of((m * per + h) * HDIM, HDIM), HDIM)]


def edge_rows(own, before, taps):
    z = pltpu.roll(jnp.where(rows_iota((8, HDIM)) < 4, own, before), 3, 0)
    y = taps[3:4] * z
    for back in range(1, CONV):
        y = y + taps[3 - back : 4 - back] * pltpu.roll(z, back, 0)
    return y


def edge_only(y):
    rows = rows_iota(y.shape)
    return jnp.where((rows >= 3) & (rows < 6), y, 0.0)


def edge_kv(own, before, wk, wv):
    kf = silu_of_twice(edge_rows(own[0:8], before[0:8], wk * 0.5))
    vf = edge_rows(own[8:16], before[8:16], wv)
    return edge_only(kf), edge_only(vf)


def gather_packets(packets, buf):
    for j, packet in enumerate(packets):
        buf[member() ^ j] = packet[...]


def gather_edges(packets, buf):
    for j, packet in enumerate(packets):
        buf[member() ^ j] = packet[:, HDIM:]


def total_kernel(has_tail, *refs):
    packets, refs = refs[:GROUP], refs[GROUP:]
    if has_tail:
        tail_ref, refs = refs[0], refs[1:]
    w_ref, out_ref, buf = refs
    gather_edges(packets, buf)
    per = out_ref.shape[0]
    for h in range(per):
        wk, wv = (taps_of(w_ref, which, member(), h, per) for which in (1, 2))
        before = tail_ref[h].astype(F32) if has_tail else jnp.zeros((AUX, HDIM), F32)
        kfs, vfs = [], []
        total = sum(packet[h, 0:HDIM].astype(F32) for packet in packets)
        for t in range(GROUP):
            own = buf[t, h].astype(F32)
            kf, vf = edge_kv(own, before, wk, wv)
            kfs.append(kf)
            vfs.append(vf)
            before = own
        kf = jnp.concatenate(kfs, axis=0).astype(BF16)
        vf = jnp.concatenate(vfs, axis=0).astype(BF16)
        total = total + dot(kf, vf, ((0,), (0,)))
        out_ref[h, 0:HDIM] = total.astype(BF16)
        out_ref[h, HDIM:] = pack_tail(before).astype(BF16)


def pack_tail(raw):
    k = jnp.where(rows_iota((8, HDIM)) < 4, pltpu.roll(raw[16:24], 3, 0), raw[0:8])
    return jnp.concatenate([k, raw[8:16]], axis=0)


def unpack_tail(tail):
    q = pltpu.roll(tail[0:8], 5, 0)
    return jnp.concatenate([tail, q, q], axis=0)


def group_total(packets, tail, conv_weight):
    heads = packets[0].shape[0]
    tails = [] if tail is None else [tail]
    return pl.pallas_call(
        functools.partial(total_kernel, tail is not None),
        in_specs=[VMEM] * (GROUP + len(tails) + 1),
        out_specs=VMEM,
        out_shape=jax.ShapeDtypeStruct((heads, HDIM + TAIL, HDIM), BF16),
        scratch_shapes=[pltpu.VMEM((GROUP, heads, AUX, HDIM), BF16)],
        compiler_params=pltpu.CompilerParams(vmem_limit_bytes=8 << 20),
        name="group_total",
    )(*packets, *tails, conv_weight)


def edge_features(own, before, wq, wk, wv):
    kf, vf = edge_kv(own, before, wk, wv)
    qf = silu_of_twice(edge_rows(own[16:24], before[16:24], wq * 0.5)) * SCALE
    blank = jnp.zeros((8, HDIM), F32)
    qf, kf, vf = (jnp.concatenate([a, blank], axis=0).astype(BF16) for a in (edge_only(qf), kf, vf))
    scores = dot(qf, kf, ((1,), (1,)))
    causal = rows_iota(scores.shape) >= lax.broadcasted_iota(jnp.int32, scores.shape, 1)
    scores = jnp.where(causal, scores, 0.0).astype(BF16)
    return qf, dot(scores, vf, ((1,), (0,))), dot(kf, vf, ((0,), (0,)))


def edges_kernel(p0, p1, p2, p3, w_ref, qf_ref, inner_ref, before_ref, with_ref, first_ref, buf):
    gather_packets((p0, p1, p2, p3), buf)
    per = p0.shape[0]
    for h in range(per):
        taps = [taps_of(w_ref, which, member(), h, per) for which in range(3)]
        first_ref[h] = buf[0, h, HDIM:]
        state = buf[0, h, 0:HDIM].astype(F32)
        for t in range(1, GROUP):
            own, before = buf[t, h, HDIM:].astype(F32), buf[t - 1, h, HDIM:].astype(F32)
            qf, inner, first = edge_features(own, before, *taps)
            qf_ref[t - 1, h] = qf
            inner_ref[t - 1, h] = inner
            before_ref[t - 1, h] = state
            state = state + first
            with_ref[t - 1, h] = state
            state = state + buf[t, h, 0:HDIM].astype(F32)


def member_edges(packets, conv_weight):
    heads = packets[0].shape[0]
    later = GROUP - 1
    return pl.pallas_call(
        edges_kernel,
        in_specs=[VMEM] * (GROUP + 1),
        out_specs=[VMEM] * 5,
        out_shape=[
            jax.ShapeDtypeStruct((later, heads, 16, HDIM), BF16),
            jax.ShapeDtypeStruct((later, heads, 16, HDIM), F32),
            jax.ShapeDtypeStruct((later, heads, HDIM, HDIM), F32),
            jax.ShapeDtypeStruct((later, heads, HDIM, HDIM), F32),
            jax.ShapeDtypeStruct((heads, AUX, HDIM), BF16),
        ],
        scratch_shapes=[pltpu.VMEM((GROUP, heads, HDIM + AUX, HDIM), BF16)],
        compiler_params=pltpu.CompilerParams(vmem_limit_bytes=8 << 20),
        name="member_edges",
    )(*packets, conv_weight)


def prefix_kernel(qf_ref, inner_ref, before_ref, with_ref, first_ref, x_ref, w_ref, gain_ref, o0, o1, o2, o3, out):
    later = (group() > 0).astype(F32)
    blank = jnp.zeros((8, HDIM), F32)
    per = x_ref.shape[0]
    for h in range(per):
        taps = [taps_of(w_ref, which, member(), h, per) for which in range(3)]
        gain = gain_ref[:, pl.ds(pl.multiple_of((member() * per + h) * HDIM, HDIM), HDIM)]
        base = x_ref[h, 0:HDIM].astype(F32) * later
        tail = unpack_tail(x_ref[h, HDIM:].astype(F32) * later)
        qf, inner, first = edge_features(first_ref[h].astype(F32), tail, *taps)
        prefix = base
        base = base + first
        shifted = base
        for t in range(GROUP):
            if t:
                qf, inner = qf_ref[t - 1, h], inner_ref[t - 1, h]
                prefix = base + before_ref[t - 1, h]
                shifted = base + with_ref[t - 1, h]
            o = inner + dot(qf, prefix.astype(BF16), ((1,), (0,)))
            o = o * lax.rsqrt(jnp.mean(o * o, axis=1, keepdims=True) + 1e-06) * gain
            out[t, h, 0:HDIM] = shifted.astype(BF16)
            out[t, h, HDIM:] = jnp.concatenate([pltpu.roll(o[0:8], 5, 0), blank], axis=0).astype(BF16)
    for j, o_ref in enumerate((o0, o1, o2, o3)):
        o_ref[...] = out[member() ^ j]


def member_prefixes(edges, incoming, conv_weight, gain):
    heads = incoming.shape[0]
    out = jax.ShapeDtypeStruct((heads, HDIM + FIX, HDIM), BF16)
    return pl.pallas_call(
        prefix_kernel,
        in_specs=[VMEM] * (len(edges) + 3),
        out_specs=[VMEM] * GROUP,
        out_shape=[out] * GROUP,
        scratch_shapes=[pltpu.VMEM((GROUP, heads, HDIM + FIX, HDIM), BF16)],
        compiler_params=pltpu.CompilerParams(vmem_limit_bytes=8 << 20),
        name="member_prefixes",
    )(*edges, incoming, conv_weight, gain)


def inner_kernel(quarters, slots, q_ref, w_ref, *refs):
    n = len(quarters)
    kf_refs, vf_refs, (qf_ref, inner_ref) = refs[0:n], refs[n : 2 * n], refs[2 * n :]
    heads, tokens = qf_ref.shape[0:2]
    per = heads // n
    shape = (CHUNK, CHUNK)
    causal = rows_iota(shape) >= lax.broadcasted_iota(jnp.int32, shape, 1)
    for place in range(heads):
        h = (member() ^ quarters[place // per]) * per + place % per
        cols = pl.ds(pl.multiple_of(h * HDIM, HDIM), HDIM)
        wq = w_ref[0, :, cols] * 0.5
        state = None
        for start in range(0, tokens, CHUNK):
            rows = slice(start, start + CHUNK)
            above = q_ref[start - 16 : start, cols] if start else None
            qf = (silu_of_twice(conv_rows(q_ref[rows, cols], above, wq)) * SCALE).astype(BF16)
            qf_ref[place, rows] = qf
            kept = slots[place // per] * per + place % per
            kf, vf = kf_refs[place // per][kept, rows], vf_refs[place // per][kept, rows]
            scores = jnp.where(causal, dot(qf, kf, ((1,), (1,))), 0.0).astype(BF16)
            inner = dot(scores, vf, ((1,), (0,)))
            if state is not None:
                inner = inner + dot(qf, state.astype(BF16), ((1,), (0,)))
            inner_ref[place, rows] = inner
            if start + CHUNK < tokens:
                new = dot(kf, vf, ((0,), (0,)))
                state = new if state is None else state + new


def inner_attention(quarters, queries, kept, conv_weight):
    tokens, width = queries.shape
    count = width // HDIM // GROUP * len(quarters)
    kfs, vfs, slots = zip(*(kept[j] for j in quarters))
    return pl.pallas_call(
        functools.partial(inner_kernel, quarters, slots),
        in_specs=[VMEM] * (2 + 2 * len(quarters)),
        out_specs=[VMEM] * 2,
        out_shape=[
            jax.ShapeDtypeStruct((count, tokens, HDIM), BF16),
            jax.ShapeDtypeStruct((count, tokens, HDIM), F32),
        ],
        compiler_params=pltpu.CompilerParams(vmem_limit_bytes=24 << 20),
        cost_estimate=pl.CostEstimate(
            flops=8 * count * tokens * HDIM * HDIM,
            bytes_accessed=12 * tokens * count * HDIM,
            transcendentals=tokens * count * HDIM,
        ),
        name="inner_attention",
    )(queries, conv_weight, *kfs, *vfs)


def finish_kernel(quarters, places, aliased, gain_ref, *refs):
    n = len(quarters)
    packets, qf_refs, inner_refs, refs = refs[0:n], refs[n : 2 * n], refs[2 * n : 3 * n], refs[3 * n + aliased :]
    out_hbm, out_buf, sem = refs
    per = packets[0].shape[0]
    tokens = out_buf.shape[1]
    part = tokens // PARTS
    there = rows_iota((FIX, HDIM)) < CONV - 1
    copies = []
    for i in range(n):
        quarter = member() ^ quarters[i]
        for c in range(PARTS):
            rows = slice(c * part, (c + 1) * part)
            for h in range(per):
                place = places[i] * per + h
                gain = gain_ref[:, pl.ds(pl.multiple_of((quarter * per + h) * HDIM, HDIM), HDIM)]
                o = inner_refs[i][place, rows] + dot(qf_refs[i][place, rows], packets[i][h, 0:HDIM], ((1,), (0,)))
                o = o * lax.rsqrt(jnp.mean(o * o, axis=1, keepdims=True) + 1e-06) * gain
                if c == 0:
                    fixed = packets[i][h, HDIM:].astype(F32)
                    o = jnp.concatenate([jnp.where(there, fixed, o[0:FIX]), o[FIX:]], axis=0)
                out_buf[i, rows, h * HDIM : (h + 1) * HDIM] = o.astype(BF16)
            cols = pl.ds(pl.multiple_of(quarter * per * HDIM, per * HDIM), per * HDIM)
            copies.append(pltpu.make_async_copy(out_buf.at[i, rows], out_hbm.at[rows, cols], sem.at[i, c]))
            copies[-1].start()
    for copy in copies:
        copy.wait()


def finish(quarters, prefixes, pieces, places, gain, begun=None):
    tokens = pieces[0][0].shape[1]
    width = gain.shape[1]
    n = len(quarters)
    others = [] if begun is None else [begun]
    return pl.pallas_call(
        functools.partial(finish_kernel, quarters, places, len(others)),
        in_specs=[VMEM] * (1 + 3 * n) + [HBM] * len(others),
        out_specs=HBM,
        out_shape=jax.ShapeDtypeStruct((tokens, width), BF16),
        input_output_aliases={1 + 3 * n: 0} if others else {},
        scratch_shapes=[
            pltpu.VMEM((n, tokens, width // GROUP), BF16),
            pltpu.SemaphoreType.DMA((n, PARTS)),
        ],
        compiler_params=pltpu.CompilerParams(vmem_limit_bytes=24 << 20),
        cost_estimate=pl.CostEstimate(
            flops=2 * n * tokens * width // GROUP * HDIM,
            bytes_accessed=8 * n * tokens * width // GROUP,
            transcendentals=n * tokens * width // GROUP // HDIM,
        ),
        name="finish",
    )(gain, *prefixes, *[p[0] for p in pieces], *[p[1] for p in pieces], *others)


def swapped(value, bits):
    count = lax.axis_size("ctx")
    return lax.ppermute(value, "ctx", [(s, s ^ bits) for s in range(count)])


def to_next_group(value):
    count = lax.axis_size("ctx")
    return lax.ppermute(value, "ctx", [(s, s + GROUP) for s in range(count - GROUP)])


def body(queries, key_rows, value_rows, conv_weight, head_gain):
    width = queries.shape[1]
    heads = width // GROUP // HDIM
    groups = lax.axis_size("ctx") // GROUP
    gain = head_gain.reshape(1, width)
    order = (3, 2, 1)
    kf, vf, early, k_rest, v_rest, queries, conv_weight = early_states(
        order + (0,), queries, key_rows, value_rows, conv_weight
    )
    kept = {j: (kf, vf, n) for n, j in enumerate(order)}
    sent = [swapped(early[n * heads : (n + 1) * heads], j) for n, j in enumerate(order)]
    kf, vf, own = own_states(k_rest, v_rest, queries, conv_weight)
    kept[0] = (kf, vf, 0)

    def beside(quarters, arrays):
        piece = inner_attention(quarters, queries, kept, conv_weight)
        return lax.optimization_barrier((arrays, piece))

    sent, piece_a = beside((0, 3), sent)
    packets = [own] + sent[::-1]
    if groups == 2:
        incoming = swapped(group_total(packets, None, conv_weight), GROUP)
    else:
        last = jnp.stack(packets)[member() ^ (GROUP - 1)][:, HDIM:]
        tail = to_next_group(last)
        total = group_total(packets, tail, conv_weight)[:, 0:HDIM].astype(F32)
        tail = jnp.concatenate([tail[:, 21:24], tail[:, 3:16]], axis=1)
        prefix, passed = jnp.zeros_like(total), total
        for _ in range(groups - 1):
            prefix = to_next_group(passed)
            passed = prefix + total
        incoming = jnp.concatenate([prefix.astype(BF16), tail], axis=1)
    edges = member_edges(packets, conv_weight)
    (incoming, edges), piece_b = beside((2,), (incoming, edges))
    sends = member_prefixes(edges, incoming, conv_weight, gain)
    first = [swapped(sends[j], j) for j in (3,)]
    last = [swapped(sends[j], j) for j in (2, 1)]
    first, piece_c = beside((1,), first)
    out = finish((0, 3), [sends[0]] + first, [piece_a, piece_a], (0, 1, ), gain)
    return finish((2, 1), last, [piece_b, piece_c], (0, 0, ), gain, out)


def solution(mesh):
    return jax.shard_map(
        body,
        mesh=mesh,
        in_specs=(
            P(("mp", "ctx"), None),
            P(("mp", "ctx"), None),
            P(("mp", "ctx"), None),
            P("mp", None, None),
            P("mp"),
        ),
        out_specs=P(("mp", "ctx"), None),
        check_vma=False,
    )
```

```python
import functools

import jax
import jax.numpy as jnp
from jax import lax
from jax.experimental import pallas as pl
from jax.experimental.pallas import tpu as pltpu
from jax.sharding import PartitionSpec as P

HDIM = 128
CONV = 4
GROUP = 4
ROWS = 64
CHUNK = 256
PARTS = 4
AUX = 32
TAIL = 16
FIX = 16
SCALE = HDIM ** (-0.5)
F32, BF16 = jnp.float32, jnp.bfloat16


def member():
    return lax.rem(lax.axis_index("ctx"), GROUP)


def group():
    return lax.div(lax.axis_index("ctx"), GROUP)


def rows_iota(shape):
    return lax.broadcasted_iota(jnp.int32, shape, 0)


def dot(a, b, dims):
    return lax.dot_general(a, b, (dims, ((), ())), preferred_element_type=F32)


def conv_rows(x, earlier, taps):
    x = x.astype(F32)
    earlier = jnp.zeros((8, HDIM), F32) if earlier is None else earlier.astype(F32)[8:16]
    x = jnp.concatenate([earlier, x], axis=0)
    x1 = pltpu.roll(x, 1, 0)
    late = taps[3:4] * x + taps[2:3] * x1
    early = taps[1:2] * x + taps[0:1] * x1
    return (late + pltpu.roll(early, 2, 0))[8:]


def silu_of_twice(half):
    return half + half * jnp.tanh(half)


def merged_rows(first16, last16):
    first = first16.astype(F32)[0:8]
    last = last16.astype(F32)[8:16]
    return jnp.where(rows_iota((8, HDIM)) < 4, first, last)


def conv_from(wide, rows, taps):
    at = lambda back: wide[rows.start + 8 - back : rows.stop + 8 - back]
    return (taps[3:4] * at(0) + taps[2:3] * at(1)) + (taps[1:2] * at(2) + taps[0:1] * at(3))


def heads_of(quarter, per):
    return [pl.ds(pl.multiple_of((quarter * per + u) * HDIM, HDIM), HDIM) for u in range(per)]


def key_features(n, quarter, k_ref, w_ref, kf_ref, wide):
    tokens, per = k_ref.shape[1], k_ref.shape[2] // HDIM
    for u, cols in enumerate(heads_of(quarter, per)):
        wk = w_ref[1, :, cols] * 0.5
        for start in range(0, tokens, ROWS):
            rows = slice(start, start + ROWS)
            wide[n, u, 0, start + 8 : start + 8 + ROWS] = k_ref[n, rows, u * HDIM : (u + 1) * HDIM].astype(F32)
            kf = silu_of_twice(conv_from(wide.at[n, u, 0], rows, wk))
            if start == 0:
                kf = jnp.where(rows_iota(kf.shape) < CONV - 1, 0.0, kf)
            kf_ref[n * per + u, rows] = kf.astype(BF16)


def states(n, quarter, k_ref, v_ref, w_ref, kf_ref, vf_ref, msg_ref, wide):
    tokens, per = v_ref.shape[1], v_ref.shape[2] // HDIM
    for u, cols in enumerate(heads_of(quarter, per)):
        own = slice(u * HDIM, (u + 1) * HDIM)
        wv = w_ref[2, :, cols]
        local = jnp.zeros((HDIM, HDIM), F32)
        for start in range(0, tokens, ROWS):
            rows = slice(start, start + ROWS)
            wide[n, u, 1, start + 8 : start + 8 + ROWS] = v_ref[n, rows, own].astype(F32)
            vf = conv_from(wide.at[n, u, 1], rows, wv).astype(BF16)
            vf_ref[n * per + u, rows] = vf
            local = local + dot(kf_ref[n * per + u, rows], vf, ((0,), (0,)))
        msg_ref[n * per + u, 0:HDIM] = local.astype(BF16)
        mk = merged_rows(k_ref[n, 0:16, own], k_ref[n, tokens - 16 : tokens, own])
        mv = merged_rows(v_ref[n, 0:16, own], v_ref[n, tokens - 16 : tokens, own])
        msg_ref[n * per + u, HDIM : HDIM + 16] = jnp.concatenate([mk, mv], axis=0).astype(BF16)


def query_rows(n, quarter, per, q_ref, msg_ref):
    tokens = q_ref.shape[0]
    for u, cols in enumerate(heads_of(quarter, per)):
        mq = merged_rows(q_ref[0:16, cols], q_ref[tokens - 16 : tokens, cols])
        msg_ref[n * per + u, HDIM + 16 : HDIM + 32] = jnp.concatenate([mq, mq], axis=0).astype(BF16)


def clear_above(wide):
    for n in range(wide.shape[0]):
        for u in range(wide.shape[1]):
            for a in range(2):
                wide[n, u, a, 0:8] = jnp.zeros((8, HDIM), F32)


def early_kernel(quarters, q_hbm, k_hbm, v_hbm, w_hbm, kf_ref, vf_ref, msg_ref, k_rest, v_rest, q_ref, w_ref, k_buf, v_buf, wide, k_sem, v_sem, sem):
    count, tokens, part = k_buf.shape
    per = part // HDIM
    mine = [member() ^ j for j in quarters]

    def fetch(source, target, rest, semaphore, n):
        cols = pl.ds(pl.multiple_of(mine[n] * part, part), part)
        place = target.at[n] if n < count else rest.at[0]
        return pltpu.make_async_copy(source.at[:, cols], place, semaphore.at[n])

    fetch_k = [fetch(k_hbm, k_buf, k_rest, k_sem, n) for n in range(GROUP)]
    fetch_v = [fetch(v_hbm, v_buf, v_rest, v_sem, n) for n in range(GROUP)]
    fetch_taps = pltpu.make_async_copy(w_hbm, w_ref, sem.at[0])
    fetch_queries = pltpu.make_async_copy(q_hbm, q_ref, sem.at[1])

    def keys(n):
        key_features(n, mine[n], k_buf, w_ref, kf_ref, wide)

    def values(n):
        states(n, mine[n], k_buf, v_buf, w_ref, kf_ref, vf_ref, msg_ref, wide)

    for copy in (fetch_taps, fetch_k[0], fetch_v[0], fetch_k[1]):
        copy.start()
    clear_above(wide)
    fetch_taps.wait()
    fetch_k[0].wait()
    for copy in (fetch_v[1], fetch_k[2], fetch_v[2]):
        copy.start()
    keys(0)
    fetch_v[0].wait()
    fetch_k[1].wait()
    for copy in (fetch_k[3], fetch_v[3], fetch_queries):
        copy.start()
    values(0)
    keys(1)
    fetch_v[1].wait()
    fetch_k[2].wait()
    values(1)
    keys(2)
    fetch_v[2].wait()
    values(2)
    fetch_queries.wait()
    for n in range(count):
        query_rows(n, mine[n], per, q_ref, msg_ref)
    fetch_k[3].wait()
    fetch_v[3].wait()


def own_kernel(k_ref, v_ref, q_ref, w_ref, kf_ref, vf_ref, msg_ref, wide):
    per = k_ref.shape[2] // HDIM
    clear_above(wide)
    key_features(0, member(), k_ref, w_ref, kf_ref, wide)
    states(0, member(), k_ref, v_ref, w_ref, kf_ref, vf_ref, msg_ref, wide)
    query_rows(0, member(), per, q_ref, msg_ref)


VMEM = pl.BlockSpec(memory_space=pltpu.VMEM)
HBM = pl.BlockSpec(memory_space=pltpu.HBM)


def state_cost(tokens, width):
    return pl.CostEstimate(flops=2 * tokens * width * HDIM, bytes_accessed=8 * tokens * width, transcendentals=tokens * width)


def early_states(quarters, queries, key_rows, value_rows, conv_weight):
    tokens, width = key_rows.shape
    count, part = len(quarters) - 1, width // GROUP
    per = part // HDIM
    features = jax.ShapeDtypeStruct((count * per, tokens, HDIM), BF16)
    rest = jax.ShapeDtypeStruct((1, tokens, part), BF16)
    arrays = [pltpu.with_memory_space_constraint(a, pltpu.HBM) for a in (queries, key_rows, value_rows, conv_weight)]
    return pl.pallas_call(
        functools.partial(early_kernel, quarters),
        in_specs=[HBM] * 4,
        out_specs=[VMEM] * 7,
        out_shape=[
            features,
            features,
            jax.ShapeDtypeStruct((count * per, HDIM + AUX, HDIM), BF16),
            rest,
            rest,
            jax.ShapeDtypeStruct(queries.shape, BF16),
            jax.ShapeDtypeStruct(conv_weight.shape, F32),
        ],
        scratch_shapes=[
            pltpu.VMEM((count, tokens, part), BF16),
            pltpu.VMEM((count, tokens, part), BF16),
            pltpu.VMEM((count, per, 2, tokens + 8, HDIM), F32),
            pltpu.SemaphoreType.DMA((GROUP,)),
            pltpu.SemaphoreType.DMA((GROUP,)),
            pltpu.SemaphoreType.DMA((2,)),
        ],
        compiler_params=pltpu.CompilerParams(vmem_limit_bytes=28 << 20),
        cost_estimate=state_cost(tokens, width),
        name="early_states",
    )(*arrays)


def own_states(k_rest, v_rest, queries, conv_weight):
    tokens, part = k_rest.shape[1:3]
    per = part // HDIM
    features = jax.ShapeDtypeStruct((per, tokens, HDIM), BF16)
    return pl.pallas_call(
        own_kernel,
        in_specs=[VMEM] * 4,
        out_specs=[VMEM] * 3,
        out_shape=[features, features, jax.ShapeDtypeStruct((per, HDIM + AUX, HDIM), BF16)],
        scratch_shapes=[pltpu.VMEM((1, per, 2, tokens + 8, HDIM), F32)],
        compiler_params=pltpu.CompilerParams(vmem_limit_bytes=16 << 20),
        cost_estimate=state_cost(tokens, part),
        name="own_states",
    )(k_rest, v_rest, queries, conv_weight)


def taps_of(w_ref, which, m, h, per):
    return w_ref[which, :, pl.ds(pl.multiple_of((m * per + h) * HDIM, HDIM), HDIM)]


def edge_rows(own, before, taps):
    z = pltpu.roll(jnp.where(rows_iota((8, HDIM)) < 4, own, before), 3, 0)
    y = taps[3:4] * z
    for back in range(1, CONV):
        y = y + taps[3 - back : 4 - back] * pltpu.roll(z, back, 0)
    return y


def edge_only(y):
    rows = rows_iota(y.shape)
    return jnp.where((rows >= 3) & (rows < 6), y, 0.0)


def edge_kv(own, before, wk, wv):
    kf = silu_of_twice(edge_rows(own[0:8], before[0:8], wk * 0.5))
    vf = edge_rows(own[8:16], before[8:16], wv)
    return edge_only(kf), edge_only(vf)


def gather_packets(packets, buf):
    for j, packet in enumerate(packets):
        buf[member() ^ j] = packet[...]


def gather_edges(packets, buf):
    for j, packet in enumerate(packets):
        buf[member() ^ j] = packet[:, HDIM:]


def total_kernel(has_tail, *refs):
    packets, refs = refs[:GROUP], refs[GROUP:]
    if has_tail:
        tail_ref, refs = refs[0], refs[1:]
    w_ref, out_ref, buf = refs
    gather_edges(packets, buf)
    per = out_ref.shape[0]
    for h in range(per):
        wk, wv = (taps_of(w_ref, which, member(), h, per) for which in (1, 2))
        before = tail_ref[h].astype(F32) if has_tail else jnp.zeros((AUX, HDIM), F32)
        kfs, vfs = [], []
        total = sum(packet[h, 0:HDIM].astype(F32) for packet in packets)
        for t in range(GROUP):
            own = buf[t, h].astype(F32)
            kf, vf = edge_kv(own, before, wk, wv)
            kfs.append(kf)
            vfs.append(vf)
            before = own
        kf = jnp.concatenate(kfs, axis=0).astype(BF16)
        vf = jnp.concatenate(vfs, axis=0).astype(BF16)
        total = total + dot(kf, vf, ((0,), (0,)))
        out_ref[h, 0:HDIM] = total.astype(BF16)
        out_ref[h, HDIM:] = pack_tail(before).astype(BF16)


def pack_tail(raw):
    k = jnp.where(rows_iota((8, HDIM)) < 4, pltpu.roll(raw[16:24], 3, 0), raw[0:8])
    return jnp.concatenate([k, raw[8:16]], axis=0)


def unpack_tail(tail):
    q = pltpu.roll(tail[0:8], 5, 0)
    return jnp.concatenate([tail, q, q], axis=0)


def group_total(packets, tail, conv_weight):
    heads = packets[0].shape[0]
    tails = [] if tail is None else [tail]
    return pl.pallas_call(
        functools.partial(total_kernel, tail is not None),
        in_specs=[VMEM] * (GROUP + len(tails) + 1),
        out_specs=VMEM,
        out_shape=jax.ShapeDtypeStruct((heads, HDIM + TAIL, HDIM), BF16),
        scratch_shapes=[pltpu.VMEM((GROUP, heads, AUX, HDIM), BF16)],
        compiler_params=pltpu.CompilerParams(vmem_limit_bytes=8 << 20),
        name="group_total",
    )(*packets, *tails, conv_weight)


def edge_features(own, before, wq, wk, wv):
    kf, vf = edge_kv(own, before, wk, wv)
    qf = silu_of_twice(edge_rows(own[16:24], before[16:24], wq * 0.5)) * SCALE
    blank = jnp.zeros((8, HDIM), F32)
    qf, kf, vf = (jnp.concatenate([a, blank], axis=0).astype(BF16) for a in (edge_only(qf), kf, vf))
    scores = dot(qf, kf, ((1,), (1,)))
    causal = rows_iota(scores.shape) >= lax.broadcasted_iota(jnp.int32, scores.shape, 1)
    scores = jnp.where(causal, scores, 0.0).astype(BF16)
    return qf, dot(scores, vf, ((1,), (0,))), dot(kf, vf, ((0,), (0,)))


def edges_kernel(p0, p1, p2, p3, w_ref, qf_ref, inner_ref, before_ref, with_ref, first_ref, buf):
    gather_packets((p0, p1, p2, p3), buf)
    per = p0.shape[0]
    for h in range(per):
        taps = [taps_of(w_ref, which, member(), h, per) for which in range(3)]
        first_ref[h] = buf[0, h, HDIM:]
        state = buf[0, h, 0:HDIM].astype(F32)
        for t in range(1, GROUP):
            own, before = buf[t, h, HDIM:].astype(F32), buf[t - 1, h, HDIM:].astype(F32)
            qf, inner, first = edge_features(own, before, *taps)
            qf_ref[t - 1, h] = qf
            inner_ref[t - 1, h] = inner
            before_ref[t - 1, h] = state
            state = state + first
            with_ref[t - 1, h] = state
            state = state + buf[t, h, 0:HDIM].astype(F32)


def member_edges(packets, conv_weight):
    heads = packets[0].shape[0]
    later = GROUP - 1
    return pl.pallas_call(
        edges_kernel,
        in_specs=[VMEM] * (GROUP + 1),
        out_specs=[VMEM] * 5,
        out_shape=[
            jax.ShapeDtypeStruct((later, heads, 16, HDIM), BF16),
            jax.ShapeDtypeStruct((later, heads, 16, HDIM), F32),
            jax.ShapeDtypeStruct((later, heads, HDIM, HDIM), F32),
            jax.ShapeDtypeStruct((later, heads, HDIM, HDIM), F32),
            jax.ShapeDtypeStruct((heads, AUX, HDIM), BF16),
        ],
        scratch_shapes=[pltpu.VMEM((GROUP, heads, HDIM + AUX, HDIM), BF16)],
        compiler_params=pltpu.CompilerParams(vmem_limit_bytes=8 << 20),
        name="member_edges",
    )(*packets, conv_weight)


def prefix_kernel(qf_ref, inner_ref, before_ref, with_ref, first_ref, x_ref, w_ref, gain_ref, o0, o1, o2, o3, out):
    later = (group() > 0).astype(F32)
    blank = jnp.zeros((8, HDIM), F32)
    per = x_ref.shape[0]
    for h in range(per):
        taps = [taps_of(w_ref, which, member(), h, per) for which in range(3)]
        gain = gain_ref[:, pl.ds(pl.multiple_of((member() * per + h) * HDIM, HDIM), HDIM)]
        base = x_ref[h, 0:HDIM].astype(F32) * later
        tail = unpack_tail(x_ref[h, HDIM:].astype(F32) * later)
        qf, inner, first = edge_features(first_ref[h].astype(F32), tail, *taps)
        prefix = base
        base = base + first
        shifted = base
        for t in range(GROUP):
            if t:
                qf, inner = qf_ref[t - 1, h], inner_ref[t - 1, h]
                prefix = base + before_ref[t - 1, h]
                shifted = base + with_ref[t - 1, h]
            o = inner + dot(qf, prefix.astype(BF16), ((1,), (0,)))
            o = o * lax.rsqrt(jnp.mean(o * o, axis=1, keepdims=True) + 1e-06) * gain
            out[t, h, 0:HDIM] = shifted.astype(BF16)
            out[t, h, HDIM:] = jnp.concatenate([pltpu.roll(o[0:8], 5, 0), blank], axis=0).astype(BF16)
    for j, o_ref in enumerate((o0, o1, o2, o3)):
        o_ref[...] = out[member() ^ j]


def member_prefixes(edges, incoming, conv_weight, gain):
    heads = incoming.shape[0]
    out = jax.ShapeDtypeStruct((heads, HDIM + FIX, HDIM), BF16)
    return pl.pallas_call(
        prefix_kernel,
        in_specs=[VMEM] * (len(edges) + 3),
        out_specs=[VMEM] * GROUP,
        out_shape=[out] * GROUP,
        scratch_shapes=[pltpu.VMEM((GROUP, heads, HDIM + FIX, HDIM), BF16)],
        compiler_params=pltpu.CompilerParams(vmem_limit_bytes=8 << 20),
        name="member_prefixes",
    )(*edges, incoming, conv_weight, gain)


def inner_kernel(quarters, slots, q_ref, w_ref, *refs):
    n = len(quarters)
    kf_refs, vf_refs, (qf_ref, inner_ref) = refs[0:n], refs[n : 2 * n], refs[2 * n :]
    heads, tokens = qf_ref.shape[0:2]
    per = heads // n
    shape = (CHUNK, CHUNK)
    causal = rows_iota(shape) >= lax.broadcasted_iota(jnp.int32, shape, 1)
    for place in range(heads):
        h = (member() ^ quarters[place // per]) * per + place % per
        cols = pl.ds(pl.multiple_of(h * HDIM, HDIM), HDIM)
        wq = w_ref[0, :, cols] * 0.5
        state = None
        for start in range(0, tokens, CHUNK):
            rows = slice(start, start + CHUNK)
            above = q_ref[start - 16 : start, cols] if start else None
            qf = (silu_of_twice(conv_rows(q_ref[rows, cols], above, wq)) * SCALE).astype(BF16)
            qf_ref[place, rows] = qf
            kept = slots[place // per] * per + place % per
            kf, vf = kf_refs[place // per][kept, rows], vf_refs[place // per][kept, rows]
            scores = jnp.where(causal, dot(qf, kf, ((1,), (1,))), 0.0).astype(BF16)
            inner = dot(scores, vf, ((1,), (0,)))
            if state is not None:
                inner = inner + dot(qf, state.astype(BF16), ((1,), (0,)))
            inner_ref[place, rows] = inner
            if start + CHUNK < tokens:
                new = dot(kf, vf, ((0,), (0,)))
                state = new if state is None else state + new


def inner_attention(quarters, queries, kept, conv_weight):
    tokens, width = queries.shape
    count = width // HDIM // GROUP * len(quarters)
    kfs, vfs, slots = zip(*(kept[j] for j in quarters))
    return pl.pallas_call(
        functools.partial(inner_kernel, quarters, slots),
        in_specs=[VMEM] * (2 + 2 * len(quarters)),
        out_specs=[VMEM] * 2,
        out_shape=[
            jax.ShapeDtypeStruct((count, tokens, HDIM), BF16),
            jax.ShapeDtypeStruct((count, tokens, HDIM), F32),
        ],
        compiler_params=pltpu.CompilerParams(vmem_limit_bytes=24 << 20),
        cost_estimate=pl.CostEstimate(
            flops=8 * count * tokens * HDIM * HDIM,
            bytes_accessed=12 * tokens * count * HDIM,
            transcendentals=tokens * count * HDIM,
        ),
        name="inner_attention",
    )(queries, conv_weight, *kfs, *vfs)


def finish_kernel(quarters, places, aliased, gain_ref, *refs):
    n = len(quarters)
    packets, qf_refs, inner_refs, refs = refs[0:n], refs[n : 2 * n], refs[2 * n : 3 * n], refs[3 * n + aliased :]
    out_hbm, out_buf, sem = refs
    per = packets[0].shape[0]
    tokens = out_buf.shape[1]
    part = tokens // PARTS
    there = rows_iota((FIX, HDIM)) < CONV - 1
    copies = []
    for i in range(n):
        quarter = member() ^ quarters[i]
        for c in range(PARTS):
            rows = slice(c * part, (c + 1) * part)
            for h in range(per):
                place = places[i] * per + h
                gain = gain_ref[:, pl.ds(pl.multiple_of((quarter * per + h) * HDIM, HDIM), HDIM)]
                o = inner_refs[i][place, rows] + dot(qf_refs[i][place, rows], packets[i][h, 0:HDIM], ((1,), (0,)))
                o = o * lax.rsqrt(jnp.mean(o * o, axis=1, keepdims=True) + 1e-06) * gain
                if c == 0:
                    fixed = packets[i][h, HDIM:].astype(F32)
                    o = jnp.concatenate([jnp.where(there, fixed, o[0:FIX]), o[FIX:]], axis=0)
                out_buf[i, rows, h * HDIM : (h + 1) * HDIM] = o.astype(BF16)
            cols = pl.ds(pl.multiple_of(quarter * per * HDIM, per * HDIM), per * HDIM)
            copies.append(pltpu.make_async_copy(out_buf.at[i, rows], out_hbm.at[rows, cols], sem.at[i, c]))
            copies[-1].start()
    for copy in copies:
        copy.wait()


def finish(quarters, prefixes, pieces, places, gain, begun=None):
    tokens = pieces[0][0].shape[1]
    width = gain.shape[1]
    n = len(quarters)
    others = [] if begun is None else [begun]
    return pl.pallas_call(
        functools.partial(finish_kernel, quarters, places, len(others)),
        in_specs=[VMEM] * (1 + 3 * n) + [HBM] * len(others),
        out_specs=HBM,
        out_shape=jax.ShapeDtypeStruct((tokens, width), BF16),
        input_output_aliases={1 + 3 * n: 0} if others else {},
        scratch_shapes=[
            pltpu.VMEM((n, tokens, width // GROUP), BF16),
            pltpu.SemaphoreType.DMA((n, PARTS)),
        ],
        compiler_params=pltpu.CompilerParams(vmem_limit_bytes=24 << 20),
        cost_estimate=pl.CostEstimate(
            flops=2 * n * tokens * width // GROUP * HDIM,
            bytes_accessed=8 * n * tokens * width // GROUP,
            transcendentals=n * tokens * width // GROUP // HDIM,
        ),
        name="finish",
    )(gain, *prefixes, *[p[0] for p in pieces], *[p[1] for p in pieces], *others)


def swapped(value, bits):
    count = lax.axis_size("ctx")
    return lax.ppermute(value, "ctx", [(s, s ^ bits) for s in range(count)])


def to_next_group(value):
    count = lax.axis_size("ctx")
    return lax.ppermute(value, "ctx", [(s, s + GROUP) for s in range(count - GROUP)])


def body(queries, key_rows, value_rows, conv_weight, head_gain):
    width = queries.shape[1]
    heads = width // GROUP // HDIM
    groups = lax.axis_size("ctx") // GROUP
    gain = head_gain.reshape(1, width)
    order = (3, 2, 1)
    kf, vf, early, k_rest, v_rest, queries, conv_weight = early_states(
        order + (0,), queries, key_rows, value_rows, conv_weight
    )
    kept = {j: (kf, vf, n) for n, j in enumerate(order)}
    sent = [swapped(early[n * heads : (n + 1) * heads], j) for n, j in enumerate(order)]
    kf, vf, own = own_states(k_rest, v_rest, queries, conv_weight)
    kept[0] = (kf, vf, 0)

    def beside(quarters, arrays):
        piece = inner_attention(quarters, queries, kept, conv_weight)
        return lax.optimization_barrier((arrays, piece))

    sent, piece_a = beside((0, 3), sent[::-1])
    packets = [own] + sent
    if groups == 2:
        incoming = swapped(group_total(packets, None, conv_weight), GROUP)
    else:
        last = jnp.stack(packets)[member() ^ (GROUP - 1)][:, HDIM:]
        tail = to_next_group(last)
        total = group_total(packets, tail, conv_weight)[:, 0:HDIM].astype(F32)
        tail = jnp.concatenate([tail[:, 21:24], tail[:, 3:16]], axis=1)
        prefix, passed = jnp.zeros_like(total), total
        for _ in range(groups - 1):
            prefix = to_next_group(passed)
            passed = prefix + total
        incoming = jnp.concatenate([prefix.astype(BF16), tail], axis=1)
    edges = member_edges(packets, conv_weight)
    (incoming, edges), piece_b = beside((2, 1), (incoming, edges))
    sends = member_prefixes(edges, incoming, conv_weight, gain)
    out = finish((0,), [sends[0]], [piece_a], (0,), gain)
    far, near = swapped(sends[3], 3), [swapped(sends[j], j) for j in (2, 1)]
    far, out = lax.optimization_barrier((far, out))
    out = finish((3,), [far], [piece_a], (1,), gain, out)
    return finish((2, 1), near, [piece_b, piece_b], (0, 1), gain, out)


def solution(mesh):
    return jax.shard_map(
        body,
        mesh=mesh,
        in_specs=(
            P(("mp", "ctx"), None),
            P(("mp", "ctx"), None),
            P(("mp", "ctx"), None),
            P("mp", None, None),
            P("mp"),
        ),
        out_specs=P(("mp", "ctx"), None),
        check_vma=False,
    )
```

```python
import functools

import jax
import jax.numpy as jnp
from jax import lax
from jax.experimental import pallas as pl
from jax.experimental.pallas import tpu as pltpu
from jax.sharding import PartitionSpec as P

HDIM = 128
CONV = 4
GROUP = 4
ROWS = 64
CHUNK = 256
PARTS = 4
AUX = 32
TAIL = 16
FIX = 16
SCALE = HDIM ** (-0.5)
F32, BF16 = jnp.float32, jnp.bfloat16


def member():
    return lax.rem(lax.axis_index("ctx"), GROUP)


def group():
    return lax.div(lax.axis_index("ctx"), GROUP)


def rows_iota(shape):
    return lax.broadcasted_iota(jnp.int32, shape, 0)


def dot(a, b, dims):
    return lax.dot_general(a, b, (dims, ((), ())), preferred_element_type=F32)


def conv_rows(x, earlier, taps):
    x = x.astype(F32)
    earlier = jnp.zeros((8, HDIM), F32) if earlier is None else earlier.astype(F32)[8:16]
    x = jnp.concatenate([earlier, x], axis=0)
    x1 = pltpu.roll(x, 1, 0)
    late = taps[3:4] * x + taps[2:3] * x1
    early = taps[1:2] * x + taps[0:1] * x1
    return (late + pltpu.roll(early, 2, 0))[8:]


def silu_of_twice(half):
    return half + half * jnp.tanh(half)


def merged_rows(first16, last16):
    first = first16.astype(F32)[0:8]
    last = last16.astype(F32)[8:16]
    return jnp.where(rows_iota((8, HDIM)) < 4, first, last)


def conv_from(wide, rows, taps):
    at = lambda back: wide[rows.start + 8 - back : rows.stop + 8 - back]
    return (taps[3:4] * at(0) + taps[2:3] * at(1)) + (taps[1:2] * at(2) + taps[0:1] * at(3))


def heads_of(quarter, per):
    return [pl.ds(pl.multiple_of((quarter * per + u) * HDIM, HDIM), HDIM) for u in range(per)]


def key_features(n, quarter, k_ref, w_ref, kf_ref, wide):
    tokens, per = k_ref.shape[1], k_ref.shape[2] // HDIM
    for u, cols in enumerate(heads_of(quarter, per)):
        wk = w_ref[1, :, cols] * 0.5
        for start in range(0, tokens, ROWS):
            rows = slice(start, start + ROWS)
            wide[n, u, 0, start + 8 : start + 8 + ROWS] = k_ref[n, rows, u * HDIM : (u + 1) * HDIM].astype(F32)
            kf = silu_of_twice(conv_from(wide.at[n, u, 0], rows, wk))
            if start == 0:
                kf = jnp.where(rows_iota(kf.shape) < CONV - 1, 0.0, kf)
            kf_ref[n * per + u, rows] = kf.astype(BF16)


def states(n, quarter, k_ref, v_ref, w_ref, kf_ref, vf_ref, msg_ref, wide):
    tokens, per = v_ref.shape[1], v_ref.shape[2] // HDIM
    for u, cols in enumerate(heads_of(quarter, per)):
        own = slice(u * HDIM, (u + 1) * HDIM)
        wv = w_ref[2, :, cols]
        local = jnp.zeros((HDIM, HDIM), F32)
        for start in range(0, tokens, ROWS):
            rows = slice(start, start + ROWS)
            wide[n, u, 1, start + 8 : start + 8 + ROWS] = v_ref[n, rows, own].astype(F32)
            vf = conv_from(wide.at[n, u, 1], rows, wv).astype(BF16)
            vf_ref[n * per + u, rows] = vf
            local = local + dot(kf_ref[n * per + u, rows], vf, ((0,), (0,)))
        msg_ref[n * per + u, 0:HDIM] = local.astype(BF16)
        mk = merged_rows(k_ref[n, 0:16, own], k_ref[n, tokens - 16 : tokens, own])
        mv = merged_rows(v_ref[n, 0:16, own], v_ref[n, tokens - 16 : tokens, own])
        msg_ref[n * per + u, HDIM : HDIM + 16] = jnp.concatenate([mk, mv], axis=0).astype(BF16)


def query_rows(n, quarter, per, q_ref, msg_ref):
    tokens = q_ref.shape[0]
    for u, cols in enumerate(heads_of(quarter, per)):
        mq = merged_rows(q_ref[0:16, cols], q_ref[tokens - 16 : tokens, cols])
        msg_ref[n * per + u, HDIM + 16 : HDIM + 32] = jnp.concatenate([mq, mq], axis=0).astype(BF16)


def clear_above(wide):
    for n in range(wide.shape[0]):
        for u in range(wide.shape[1]):
            for a in range(2):
                wide[n, u, a, 0:8] = jnp.zeros((8, HDIM), F32)


def early_kernel(quarters, q_hbm, k_hbm, v_hbm, w_hbm, kf_ref, vf_ref, msg_ref, k_rest, v_rest, q_ref, w_ref, k_buf, v_buf, wide, k_sem, v_sem, sem):
    count, tokens, part = k_buf.shape
    per = part // HDIM
    mine = [member() ^ j for j in quarters]

    def fetch(source, target, rest, semaphore, n):
        cols = pl.ds(pl.multiple_of(mine[n] * part, part), part)
        place = target.at[n] if n < count else rest.at[0]
        return pltpu.make_async_copy(source.at[:, cols], place, semaphore.at[n])

    fetch_k = [fetch(k_hbm, k_buf, k_rest, k_sem, n) for n in range(GROUP)]
    fetch_v = [fetch(v_hbm, v_buf, v_rest, v_sem, n) for n in range(GROUP)]
    fetch_taps = pltpu.make_async_copy(w_hbm, w_ref, sem.at[0])
    fetch_queries = pltpu.make_async_copy(q_hbm, q_ref, sem.at[1])

    def keys(n):
        key_features(n, mine[n], k_buf, w_ref, kf_ref, wide)

    def values(n):
        states(n, mine[n], k_buf, v_buf, w_ref, kf_ref, vf_ref, msg_ref, wide)

    for copy in (fetch_taps, fetch_k[0], fetch_v[0], fetch_k[1]):
        copy.start()
    clear_above(wide)
    fetch_taps.wait()
    fetch_k[0].wait()
    for copy in (fetch_v[1], fetch_k[2], fetch_v[2]):
        copy.start()
    keys(0)
    fetch_v[0].wait()
    fetch_k[1].wait()
    for copy in (fetch_k[3], fetch_v[3], fetch_queries):
        copy.start()
    values(0)
    keys(1)
    fetch_v[1].wait()
    fetch_k[2].wait()
    values(1)
    keys(2)
    fetch_v[2].wait()
    values(2)
    fetch_queries.wait()
    for n in range(count):
        query_rows(n, mine[n], per, q_ref, msg_ref)
    fetch_k[3].wait()
    fetch_v[3].wait()


def own_kernel(k_ref, v_ref, q_ref, w_ref, kf_ref, vf_ref, msg_ref, wide):
    per = k_ref.shape[2] // HDIM
    clear_above(wide)
    key_features(0, member(), k_ref, w_ref, kf_ref, wide)
    states(0, member(), k_ref, v_ref, w_ref, kf_ref, vf_ref, msg_ref, wide)
    query_rows(0, member(), per, q_ref, msg_ref)


VMEM = pl.BlockSpec(memory_space=pltpu.VMEM)
HBM = pl.BlockSpec(memory_space=pltpu.HBM)


def state_cost(tokens, width):
    return pl.CostEstimate(flops=2 * tokens * width * HDIM, bytes_accessed=8 * tokens * width, transcendentals=tokens * width)


def early_states(quarters, queries, key_rows, value_rows, conv_weight):
    tokens, width = key_rows.shape
    count, part = len(quarters) - 1, width // GROUP
    per = part // HDIM
    features = jax.ShapeDtypeStruct((count * per, tokens, HDIM), BF16)
    rest = jax.ShapeDtypeStruct((1, tokens, part), BF16)
    arrays = [pltpu.with_memory_space_constraint(a, pltpu.HBM) for a in (queries, key_rows, value_rows, conv_weight)]
    return pl.pallas_call(
        functools.partial(early_kernel, quarters),
        in_specs=[HBM] * 4,
        out_specs=[VMEM] * 7,
        out_shape=[
            features,
            features,
            jax.ShapeDtypeStruct((count * per, HDIM + AUX, HDIM), BF16),
            rest,
            rest,
            jax.ShapeDtypeStruct(queries.shape, BF16),
            jax.ShapeDtypeStruct(conv_weight.shape, F32),
        ],
        scratch_shapes=[
            pltpu.VMEM((count, tokens, part), BF16),
            pltpu.VMEM((count, tokens, part), BF16),
            pltpu.VMEM((count, per, 2, tokens + 8, HDIM), F32),
            pltpu.SemaphoreType.DMA((GROUP,)),
            pltpu.SemaphoreType.DMA((GROUP,)),
            pltpu.SemaphoreType.DMA((2,)),
        ],
        compiler_params=pltpu.CompilerParams(vmem_limit_bytes=28 << 20),
        cost_estimate=state_cost(tokens, width),
        name="early_states",
    )(*arrays)


def own_states(k_rest, v_rest, queries, conv_weight):
    tokens, part = k_rest.shape[1:3]
    per = part // HDIM
    features = jax.ShapeDtypeStruct((per, tokens, HDIM), BF16)
    return pl.pallas_call(
        own_kernel,
        in_specs=[VMEM] * 4,
        out_specs=[VMEM] * 3,
        out_shape=[features, features, jax.ShapeDtypeStruct((per, HDIM + AUX, HDIM), BF16)],
        scratch_shapes=[pltpu.VMEM((1, per, 2, tokens + 8, HDIM), F32)],
        compiler_params=pltpu.CompilerParams(vmem_limit_bytes=16 << 20),
        cost_estimate=state_cost(tokens, part),
        name="own_states",
    )(k_rest, v_rest, queries, conv_weight)


def taps_of(w_ref, which, m, h, per):
    return w_ref[which, :, pl.ds(pl.multiple_of((m * per + h) * HDIM, HDIM), HDIM)]


def edge_rows(own, before, taps):
    z = pltpu.roll(jnp.where(rows_iota((8, HDIM)) < 4, own, before), 3, 0)
    y = taps[3:4] * z
    for back in range(1, CONV):
        y = y + taps[3 - back : 4 - back] * pltpu.roll(z, back, 0)
    return y


def edge_only(y):
    rows = rows_iota(y.shape)
    return jnp.where((rows >= 3) & (rows < 6), y, 0.0)


def edge_kv(own, before, wk, wv):
    kf = silu_of_twice(edge_rows(own[0:8], before[0:8], wk * 0.5))
    vf = edge_rows(own[8:16], before[8:16], wv)
    return edge_only(kf), edge_only(vf)


def gather_packets(packets, buf):
    for j, packet in enumerate(packets):
        buf[member() ^ j] = packet[...]


def gather_edges(packets, buf):
    for j, packet in enumerate(packets):
        buf[member() ^ j] = packet[:, HDIM:]


def total_kernel(has_tail, *refs):
    packets, refs = refs[:GROUP], refs[GROUP:]
    if has_tail:
        tail_ref, refs = refs[0], refs[1:]
    w_ref, out_ref, buf = refs
    gather_edges(packets, buf)
    per = out_ref.shape[0]
    for h in range(per):
        wk, wv = (taps_of(w_ref, which, member(), h, per) for which in (1, 2))
        before = tail_ref[h].astype(F32) if has_tail else jnp.zeros((AUX, HDIM), F32)
        kfs, vfs = [], []
        total = sum(packet[h, 0:HDIM].astype(F32) for packet in packets)
        for t in range(GROUP):
            own = buf[t, h].astype(F32)
            kf, vf = edge_kv(own, before, wk, wv)
            kfs.append(kf)
            vfs.append(vf)
            before = own
        kf = jnp.concatenate(kfs, axis=0).astype(BF16)
        vf = jnp.concatenate(vfs, axis=0).astype(BF16)
        total = total + dot(kf, vf, ((0,), (0,)))
        out_ref[h, 0:HDIM] = total.astype(BF16)
        out_ref[h, HDIM:] = pack_tail(before).astype(BF16)


def pack_tail(raw):
    k = jnp.where(rows_iota((8, HDIM)) < 4, pltpu.roll(raw[16:24], 3, 0), raw[0:8])
    return jnp.concatenate([k, raw[8:16]], axis=0)


def unpack_tail(tail):
    q = pltpu.roll(tail[0:8], 5, 0)
    return jnp.concatenate([tail, q, q], axis=0)


def group_total(packets, tail, conv_weight):
    heads = packets[0].shape[0]
    tails = [] if tail is None else [tail]
    return pl.pallas_call(
        functools.partial(total_kernel, tail is not None),
        in_specs=[VMEM] * (GROUP + len(tails) + 1),
        out_specs=VMEM,
        out_shape=jax.ShapeDtypeStruct((heads, HDIM + TAIL, HDIM), BF16),
        scratch_shapes=[pltpu.VMEM((GROUP, heads, AUX, HDIM), BF16)],
        compiler_params=pltpu.CompilerParams(vmem_limit_bytes=8 << 20),
        name="group_total",
    )(*packets, *tails, conv_weight)


def edge_features(own, before, wq, wk, wv):
    kf, vf = edge_kv(own, before, wk, wv)
    qf = silu_of_twice(edge_rows(own[16:24], before[16:24], wq * 0.5)) * SCALE
    blank = jnp.zeros((8, HDIM), F32)
    qf, kf, vf = (a.astype(BF16).astype(F32) for a in (edge_only(qf), kf, vf))
    inner = blank
    for back in range(CONV - 1):
        scores = jnp.sum(qf * pltpu.roll(kf, back, 0), axis=1, keepdims=True)
        inner = inner + scores.astype(BF16).astype(F32) * pltpu.roll(vf, back, 0)
    qf, kf, vf = (jnp.concatenate([a, blank], axis=0).astype(BF16) for a in (qf, kf, vf))
    return qf, jnp.concatenate([inner, blank], axis=0), dot(kf, vf, ((0,), (0,)))


def edges_kernel(p0, p1, p2, p3, w_ref, qf_ref, inner_ref, before_ref, with_ref, first_ref, buf):
    gather_packets((p0, p1, p2, p3), buf)
    per = p0.shape[0]
    for h in range(per):
        taps = [taps_of(w_ref, which, member(), h, per) for which in range(3)]
        first_ref[h] = buf[0, h, HDIM:]
        state = buf[0, h, 0:HDIM].astype(F32)
        for t in range(1, GROUP):
            own, before = buf[t, h, HDIM:].astype(F32), buf[t - 1, h, HDIM:].astype(F32)
            qf, inner, first = edge_features(own, before, *taps)
            qf_ref[t - 1, h] = qf
            inner_ref[t - 1, h] = inner
            before_ref[t - 1, h] = state
            state = state + first
            with_ref[t - 1, h] = state
            state = state + buf[t, h, 0:HDIM].astype(F32)


def member_edges(packets, conv_weight):
    heads = packets[0].shape[0]
    later = GROUP - 1
    return pl.pallas_call(
        edges_kernel,
        in_specs=[VMEM] * (GROUP + 1),
        out_specs=[VMEM] * 5,
        out_shape=[
            jax.ShapeDtypeStruct((later, heads, 16, HDIM), BF16),
            jax.ShapeDtypeStruct((later, heads, 16, HDIM), F32),
            jax.ShapeDtypeStruct((later, heads, HDIM, HDIM), F32),
            jax.ShapeDtypeStruct((later, heads, HDIM, HDIM), F32),
            jax.ShapeDtypeStruct((heads, AUX, HDIM), BF16),
        ],
        scratch_shapes=[pltpu.VMEM((GROUP, heads, HDIM + AUX, HDIM), BF16)],
        compiler_params=pltpu.CompilerParams(vmem_limit_bytes=8 << 20),
        name="member_edges",
    )(*packets, conv_weight)


def prefix_kernel(qf_ref, inner_ref, before_ref, with_ref, first_ref, x_ref, w_ref, o0, o1, o2, o3, out):
    later = (group() > 0).astype(F32)
    blank = jnp.zeros((8, HDIM), F32)
    per = x_ref.shape[0]
    for h in range(per):
        taps = [taps_of(w_ref, which, member(), h, per) for which in range(3)]
        base = x_ref[h, 0:HDIM].astype(F32) * later
        tail = unpack_tail(x_ref[h, HDIM:].astype(F32) * later)
        qf, inner, first = edge_features(first_ref[h].astype(F32), tail, *taps)
        prefix = base
        base = base + first
        shifted = base
        for t in range(GROUP):
            if t:
                qf, inner = qf_ref[t - 1, h], inner_ref[t - 1, h]
                prefix = base + before_ref[t - 1, h]
                shifted = base + with_ref[t - 1, h]
            o = inner + dot(qf, prefix.astype(BF16), ((1,), (0,)))
            out[t, h, 0:HDIM] = shifted.astype(BF16)
            out[t, h, HDIM:] = jnp.concatenate([pltpu.roll(o[0:8], 5, 0), blank], axis=0).astype(BF16)
    for j, o_ref in enumerate((o0, o1, o2, o3)):
        o_ref[...] = out[member() ^ j]


def member_prefixes(edges, incoming, conv_weight):
    heads = incoming.shape[0]
    out = jax.ShapeDtypeStruct((heads, HDIM + FIX, HDIM), BF16)
    return pl.pallas_call(
        prefix_kernel,
        in_specs=[VMEM] * (len(edges) + 2),
        out_specs=[VMEM] * GROUP,
        out_shape=[out] * GROUP,
        scratch_shapes=[pltpu.VMEM((GROUP, heads, HDIM + FIX, HDIM), BF16)],
        compiler_params=pltpu.CompilerParams(vmem_limit_bytes=8 << 20),
        name="member_prefixes",
    )(*edges, incoming, conv_weight)


def inner_kernel(quarters, slots, q_ref, w_ref, *refs):
    n = len(quarters)
    kf_refs, vf_refs, (qf_ref, inner_ref) = refs[0:n], refs[n : 2 * n], refs[2 * n :]
    heads, tokens = qf_ref.shape[0:2]
    per = heads // n
    shape = (CHUNK, CHUNK)
    causal = rows_iota(shape) >= lax.broadcasted_iota(jnp.int32, shape, 1)
    for place in range(heads):
        h = (member() ^ quarters[place // per]) * per + place % per
        cols = pl.ds(pl.multiple_of(h * HDIM, HDIM), HDIM)
        wq = w_ref[0, :, cols] * 0.5
        state = None
        for start in range(0, tokens, CHUNK):
            rows = slice(start, start + CHUNK)
            above = q_ref[start - 16 : start, cols] if start else None
            qf = (silu_of_twice(conv_rows(q_ref[rows, cols], above, wq)) * SCALE).astype(BF16)
            qf_ref[place, rows] = qf
            kept = slots[place // per] * per + place % per
            kf, vf = kf_refs[place // per][kept, rows], vf_refs[place // per][kept, rows]
            scores = jnp.where(causal, dot(qf, kf, ((1,), (1,))), 0.0).astype(BF16)
            inner = dot(scores, vf, ((1,), (0,)))
            if state is not None:
                inner = inner + dot(qf, state.astype(BF16), ((1,), (0,)))
            inner_ref[place, rows] = inner
            if start + CHUNK < tokens:
                new = dot(kf, vf, ((0,), (0,)))
                state = new if state is None else state + new


def inner_attention(quarters, queries, kept, conv_weight):
    tokens, width = queries.shape
    count = width // HDIM // GROUP * len(quarters)
    kfs, vfs, slots = zip(*(kept[j] for j in quarters))
    return pl.pallas_call(
        functools.partial(inner_kernel, quarters, slots),
        in_specs=[VMEM] * (2 + 2 * len(quarters)),
        out_specs=[VMEM] * 2,
        out_shape=[
            jax.ShapeDtypeStruct((count, tokens, HDIM), BF16),
            jax.ShapeDtypeStruct((count, tokens, HDIM), F32),
        ],
        compiler_params=pltpu.CompilerParams(vmem_limit_bytes=24 << 20),
        cost_estimate=pl.CostEstimate(
            flops=8 * count * tokens * HDIM * HDIM,
            bytes_accessed=12 * tokens * count * HDIM,
            transcendentals=tokens * count * HDIM,
        ),
        name="inner_attention",
    )(queries, conv_weight, *kfs, *vfs)


def finish_kernel(quarters, places, aliased, gain_ref, *refs):
    n = len(quarters)
    packets, qf_refs, inner_refs, refs = refs[0:n], refs[n : 2 * n], refs[2 * n : 3 * n], refs[3 * n + aliased :]
    out_hbm, out_buf, sem = refs
    per = packets[0].shape[0]
    tokens = out_buf.shape[1]
    part = tokens // PARTS
    there = rows_iota((FIX, HDIM)) < CONV - 1
    copies = []
    for i in range(n):
        quarter = member() ^ quarters[i]
        for c in range(PARTS):
            rows = slice(c * part, (c + 1) * part)
            for h in range(per):
                place = places[i] * per + h
                gain = gain_ref[:, pl.ds(pl.multiple_of((quarter * per + h) * HDIM, HDIM), HDIM)]
                o = inner_refs[i][place, rows] + dot(qf_refs[i][place, rows], packets[i][h, 0:HDIM], ((1,), (0,)))
                if c == 0:
                    fixed = packets[i][h, HDIM:].astype(F32)
                    o = jnp.concatenate([jnp.where(there, fixed, o[0:FIX]), o[FIX:]], axis=0)
                o = o * lax.rsqrt(jnp.mean(o * o, axis=1, keepdims=True) + 1e-06) * gain
                out_buf[i, rows, h * HDIM : (h + 1) * HDIM] = o.astype(BF16)
            cols = pl.ds(pl.multiple_of(quarter * per * HDIM, per * HDIM), per * HDIM)
            copies.append(pltpu.make_async_copy(out_buf.at[i, rows], out_hbm.at[rows, cols], sem.at[i, c]))
            copies[-1].start()
    for copy in copies:
        copy.wait()


def finish(quarters, prefixes, pieces, places, gain, begun=None):
    tokens = pieces[0][0].shape[1]
    width = gain.shape[1]
    n = len(quarters)
    others = [] if begun is None else [begun]
    return pl.pallas_call(
        functools.partial(finish_kernel, quarters, places, len(others)),
        in_specs=[VMEM] * (1 + 3 * n) + [HBM] * len(others),
        out_specs=HBM,
        out_shape=jax.ShapeDtypeStruct((tokens, width), BF16),
        input_output_aliases={1 + 3 * n: 0} if others else {},
        scratch_shapes=[
            pltpu.VMEM((n, tokens, width // GROUP), BF16),
            pltpu.SemaphoreType.DMA((n, PARTS)),
        ],
        compiler_params=pltpu.CompilerParams(vmem_limit_bytes=24 << 20),
        cost_estimate=pl.CostEstimate(
            flops=2 * n * tokens * width // GROUP * HDIM,
            bytes_accessed=8 * n * tokens * width // GROUP,
            transcendentals=n * tokens * width // GROUP // HDIM,
        ),
        name="finish",
    )(gain, *prefixes, *[p[0] for p in pieces], *[p[1] for p in pieces], *others)


def swapped(value, bits):
    count = lax.axis_size("ctx")
    return lax.ppermute(value, "ctx", [(s, s ^ bits) for s in range(count)])


def to_next_group(value):
    count = lax.axis_size("ctx")
    return lax.ppermute(value, "ctx", [(s, s + GROUP) for s in range(count - GROUP)])


def body(queries, key_rows, value_rows, conv_weight, head_gain):
    width = queries.shape[1]
    heads = width // GROUP // HDIM
    groups = lax.axis_size("ctx") // GROUP
    gain = head_gain.reshape(1, width)
    order = (3, 2, 1)
    kf, vf, early, k_rest, v_rest, queries, conv_weight = early_states(
        order + (0,), queries, key_rows, value_rows, conv_weight
    )
    kept = {j: (kf, vf, n) for n, j in enumerate(order)}
    sent = [swapped(early[n * heads : (n + 1) * heads], j) for n, j in enumerate(order)]
    kf, vf, own = own_states(k_rest, v_rest, queries, conv_weight)
    kept[0] = (kf, vf, 0)

    def beside(quarters, arrays):
        piece = inner_attention(quarters, queries, kept, conv_weight)
        return lax.optimization_barrier((arrays, piece))

    sent, piece_a = beside((0, 3), sent[::-1])
    packets = [own] + sent
    if groups == 2:
        incoming = swapped(group_total(packets, None, conv_weight), GROUP)
    else:
        last = jnp.stack(packets)[member() ^ (GROUP - 1)][:, HDIM:]
        tail = to_next_group(last)
        total = group_total(packets, tail, conv_weight)[:, 0:HDIM].astype(F32)
        tail = jnp.concatenate([tail[:, 21:24], tail[:, 3:16]], axis=1)
        prefix, passed = jnp.zeros_like(total), total
        for _ in range(groups - 1):
            prefix = to_next_group(passed)
            passed = prefix + total
        incoming = jnp.concatenate([prefix.astype(BF16), tail], axis=1)
    edges = member_edges(packets, conv_weight)
    (incoming, edges), piece_b = beside((2, 1), (incoming, edges))
    sends = member_prefixes(edges, incoming, conv_weight)
    out = finish((0,), [sends[0]], [piece_a], (0,), gain)
    far, near = swapped(sends[3], 3), [swapped(sends[j], j) for j in (2, 1)]
    far, out = lax.optimization_barrier((far, out))
    out = finish((3,), [far], [piece_a], (1,), gain, out)
    return finish((2, 1), near, [piece_b, piece_b], (0, 1), gain, out)


def solution(mesh):
    return jax.shard_map(
        body,
        mesh=mesh,
        in_specs=(
            P(("mp", "ctx"), None),
            P(("mp", "ctx"), None),
            P(("mp", "ctx"), None),
            P("mp", None, None),
            P("mp"),
        ),
        out_specs=P(("mp", "ctx"), None),
        check_vma=False,
    )
```

```python
import functools

import jax
import jax.numpy as jnp
from jax import lax
from jax.experimental import pallas as pl
from jax.experimental.pallas import tpu as pltpu
from jax.sharding import PartitionSpec as P

HDIM = 128
CONV = 4
GROUP = 4
ROWS = 64
CHUNK = 256
PARTS = 2
AUX = 32
TAIL = 16
FIX = 16
SCALE = HDIM ** (-0.5)
F32, BF16 = jnp.float32, jnp.bfloat16


def member():
    return lax.rem(lax.axis_index("ctx"), GROUP)


def group():
    return lax.div(lax.axis_index("ctx"), GROUP)


def rows_iota(shape):
    return lax.broadcasted_iota(jnp.int32, shape, 0)


def dot(a, b, dims):
    return lax.dot_general(a, b, (dims, ((), ())), preferred_element_type=F32)


def conv_rows(x, earlier, taps):
    x = x.astype(F32)
    earlier = jnp.zeros((8, HDIM), F32) if earlier is None else earlier.astype(F32)[8:16]
    x = jnp.concatenate([earlier, x], axis=0)
    x1 = pltpu.roll(x, 1, 0)
    late = taps[3:4] * x + taps[2:3] * x1
    early = taps[1:2] * x + taps[0:1] * x1
    return (late + pltpu.roll(early, 2, 0))[8:]


def silu_of_twice(half):
    return half + half * jnp.tanh(half)


def merged_rows(first16, last16):
    first = first16.astype(F32)[0:8]
    last = last16.astype(F32)[8:16]
    return jnp.where(rows_iota((8, HDIM)) < 4, first, last)


def conv_from(wide, rows, taps):
    at = lambda back: wide[rows.start + 8 - back : rows.stop + 8 - back]
    return (taps[3:4] * at(0) + taps[2:3] * at(1)) + (taps[1:2] * at(2) + taps[0:1] * at(3))


def heads_of(quarter, per):
    return [pl.ds(pl.multiple_of((quarter * per + u) * HDIM, HDIM), HDIM) for u in range(per)]


def key_features(n, quarter, k_ref, w_ref, kf_ref, wide):
    tokens, per = k_ref.shape[1], k_ref.shape[2] // HDIM
    for u, cols in enumerate(heads_of(quarter, per)):
        wk = w_ref[1, :, cols] * 0.5
        for start in range(0, tokens, ROWS):
            rows = slice(start, start + ROWS)
            wide[n, u, 0, start + 8 : start + 8 + ROWS] = k_ref[n, rows, u * HDIM : (u + 1) * HDIM].astype(F32)
            kf = silu_of_twice(conv_from(wide.at[n, u, 0], rows, wk))
            if start == 0:
                kf = jnp.where(rows_iota(kf.shape) < CONV - 1, 0.0, kf)
            kf_ref[n * per + u, rows] = kf.astype(BF16)


def states(n, quarter, k_ref, v_ref, w_ref, kf_ref, vf_ref, msg_ref, wide):
    tokens, per = v_ref.shape[1], v_ref.shape[2] // HDIM
    for u, cols in enumerate(heads_of(quarter, per)):
        own = slice(u * HDIM, (u + 1) * HDIM)
        wv = w_ref[2, :, cols]
        local = jnp.zeros((HDIM, HDIM), F32)
        for start in range(0, tokens, ROWS):
            rows = slice(start, start + ROWS)
            wide[n, u, 1, start + 8 : start + 8 + ROWS] = v_ref[n, rows, own].astype(F32)
            vf = conv_from(wide.at[n, u, 1], rows, wv).astype(BF16)
            vf_ref[n * per + u, rows] = vf
            local = local + dot(kf_ref[n * per + u, rows], vf, ((0,), (0,)))
        msg_ref[n * per + u, 0:HDIM] = local.astype(BF16)
        mk = merged_rows(k_ref[n, 0:16, own], k_ref[n, tokens - 16 : tokens, own])
        mv = merged_rows(v_ref[n, 0:16, own], v_ref[n, tokens - 16 : tokens, own])
        msg_ref[n * per + u, HDIM : HDIM + 16] = jnp.concatenate([mk, mv], axis=0).astype(BF16)


def query_rows(n, quarter, per, q_ref, msg_ref):
    tokens = q_ref.shape[0]
    for u, cols in enumerate(heads_of(quarter, per)):
        mq = merged_rows(q_ref[0:16, cols], q_ref[tokens - 16 : tokens, cols])
        msg_ref[n * per + u, HDIM + 16 : HDIM + 32] = jnp.concatenate([mq, mq], axis=0).astype(BF16)


def clear_above(wide):
    for n in range(wide.shape[0]):
        for u in range(wide.shape[1]):
            for a in range(2):
                wide[n, u, a, 0:8] = jnp.zeros((8, HDIM), F32)


def early_kernel(quarters, q_hbm, k_hbm, v_hbm, w_hbm, kf_ref, vf_ref, msg_ref, k_rest, v_rest, q_ref, w_ref, k_buf, v_buf, wide, k_sem, v_sem, sem):
    count, tokens, part = k_buf.shape
    per = part // HDIM
    mine = [member() ^ j for j in quarters]

    def fetch(source, target, rest, semaphore, n):
        cols = pl.ds(pl.multiple_of(mine[n] * part, part), part)
        place = target.at[n] if n < count else rest.at[0]
        return pltpu.make_async_copy(source.at[:, cols], place, semaphore.at[n])

    fetch_k = [fetch(k_hbm, k_buf, k_rest, k_sem, n) for n in range(GROUP)]
    fetch_v = [fetch(v_hbm, v_buf, v_rest, v_sem, n) for n in range(GROUP)]
    fetch_taps = pltpu.make_async_copy(w_hbm, w_ref, sem.at[0])
    fetch_queries = pltpu.make_async_copy(q_hbm, q_ref, sem.at[1])

    def keys(n):
        key_features(n, mine[n], k_buf, w_ref, kf_ref, wide)

    def values(n):
        states(n, mine[n], k_buf, v_buf, w_ref, kf_ref, vf_ref, msg_ref, wide)

    for copy in (fetch_taps, fetch_k[0], fetch_v[0], fetch_k[1]):
        copy.start()
    clear_above(wide)
    fetch_taps.wait()
    fetch_k[0].wait()
    for copy in (fetch_v[1], fetch_k[2], fetch_v[2]):
        copy.start()
    keys(0)
    fetch_v[0].wait()
    fetch_k[1].wait()
    for copy in (fetch_k[3], fetch_v[3], fetch_queries):
        copy.start()
    values(0)
    keys(1)
    fetch_v[1].wait()
    fetch_k[2].wait()
    values(1)
    keys(2)
    fetch_v[2].wait()
    values(2)
    fetch_queries.wait()
    for n in range(count):
        query_rows(n, mine[n], per, q_ref, msg_ref)
    fetch_k[3].wait()
    fetch_v[3].wait()


def own_kernel(k_ref, v_ref, q_ref, w_ref, kf_ref, vf_ref, msg_ref, wide):
    per = k_ref.shape[2] // HDIM
    clear_above(wide)
    key_features(0, member(), k_ref, w_ref, kf_ref, wide)
    states(0, member(), k_ref, v_ref, w_ref, kf_ref, vf_ref, msg_ref, wide)
    query_rows(0, member(), per, q_ref, msg_ref)


VMEM = pl.BlockSpec(memory_space=pltpu.VMEM)
HBM = pl.BlockSpec(memory_space=pltpu.HBM)


def state_cost(tokens, width):
    return pl.CostEstimate(flops=2 * tokens * width * HDIM, bytes_accessed=8 * tokens * width, transcendentals=tokens * width)


def early_states(quarters, queries, key_rows, value_rows, conv_weight):
    tokens, width = key_rows.shape
    count, part = len(quarters) - 1, width // GROUP
    per = part // HDIM
    features = jax.ShapeDtypeStruct((count * per, tokens, HDIM), BF16)
    rest = jax.ShapeDtypeStruct((1, tokens, part), BF16)
    arrays = [pltpu.with_memory_space_constraint(a, pltpu.HBM) for a in (queries, key_rows, value_rows, conv_weight)]
    return pl.pallas_call(
        functools.partial(early_kernel, quarters),
        in_specs=[HBM] * 4,
        out_specs=[VMEM] * 7,
        out_shape=[
            features,
            features,
            jax.ShapeDtypeStruct((count * per, HDIM + AUX, HDIM), BF16),
            rest,
            rest,
            jax.ShapeDtypeStruct(queries.shape, BF16),
            jax.ShapeDtypeStruct(conv_weight.shape, F32),
        ],
        scratch_shapes=[
            pltpu.VMEM((count, tokens, part), BF16),
            pltpu.VMEM((count, tokens, part), BF16),
            pltpu.VMEM((count, per, 2, tokens + 8, HDIM), F32),
            pltpu.SemaphoreType.DMA((GROUP,)),
            pltpu.SemaphoreType.DMA((GROUP,)),
            pltpu.SemaphoreType.DMA((2,)),
        ],
        compiler_params=pltpu.CompilerParams(vmem_limit_bytes=28 << 20),
        cost_estimate=state_cost(tokens, width),
        name="early_states",
    )(*arrays)


def own_states(k_rest, v_rest, queries, conv_weight):
    tokens, part = k_rest.shape[1:3]
    per = part // HDIM
    features = jax.ShapeDtypeStruct((per, tokens, HDIM), BF16)
    return pl.pallas_call(
        own_kernel,
        in_specs=[VMEM] * 4,
        out_specs=[VMEM] * 3,
        out_shape=[features, features, jax.ShapeDtypeStruct((per, HDIM + AUX, HDIM), BF16)],
        scratch_shapes=[pltpu.VMEM((1, per, 2, tokens + 8, HDIM), F32)],
        compiler_params=pltpu.CompilerParams(vmem_limit_bytes=16 << 20),
        cost_estimate=state_cost(tokens, part),
        name="own_states",
    )(k_rest, v_rest, queries, conv_weight)


def taps_of(w_ref, which, m, h, per):
    return w_ref[which, :, pl.ds(pl.multiple_of((m * per + h) * HDIM, HDIM), HDIM)]


def edge_rows(own, before, taps):
    z = pltpu.roll(jnp.where(rows_iota((8, HDIM)) < 4, own, before), 3, 0)
    y = taps[3:4] * z
    for back in range(1, CONV):
        y = y + taps[3 - back : 4 - back] * pltpu.roll(z, back, 0)
    return y


def edge_only(y):
    rows = rows_iota(y.shape)
    return jnp.where((rows >= 3) & (rows < 6), y, 0.0)


def edge_kv(own, before, wk, wv):
    kf = silu_of_twice(edge_rows(own[0:8], before[0:8], wk * 0.5))
    vf = edge_rows(own[8:16], before[8:16], wv)
    return edge_only(kf), edge_only(vf)


def gather_packets(packets, buf):
    for j, packet in enumerate(packets):
        buf[member() ^ j] = packet[...]


def gather_edges(packets, buf):
    for j, packet in enumerate(packets):
        buf[member() ^ j] = packet[:, HDIM:]


def total_kernel(has_tail, *refs):
    packets, refs = refs[:GROUP], refs[GROUP:]
    if has_tail:
        tail_ref, refs = refs[0], refs[1:]
    w_ref, out_ref, buf = refs
    gather_edges(packets, buf)
    per = out_ref.shape[0]
    for h in range(per):
        wk, wv = (taps_of(w_ref, which, member(), h, per) for which in (1, 2))
        before = tail_ref[h].astype(F32) if has_tail else jnp.zeros((AUX, HDIM), F32)
        kfs, vfs = [], []
        total = sum(packet[h, 0:HDIM].astype(F32) for packet in packets)
        for t in range(GROUP):
            own = buf[t, h].astype(F32)
            kf, vf = edge_kv(own, before, wk, wv)
            kfs.append(kf)
            vfs.append(vf)
            before = own
        kf = jnp.concatenate(kfs, axis=0).astype(BF16)
        vf = jnp.concatenate(vfs, axis=0).astype(BF16)
        total = total + dot(kf, vf, ((0,), (0,)))
        out_ref[h, 0:HDIM] = total.astype(BF16)
        out_ref[h, HDIM:] = pack_tail(before).astype(BF16)


def pack_tail(raw):
    k = jnp.where(rows_iota((8, HDIM)) < 4, pltpu.roll(raw[16:24], 3, 0), raw[0:8])
    return jnp.concatenate([k, raw[8:16]], axis=0)


def unpack_tail(tail):
    q = pltpu.roll(tail[0:8], 5, 0)
    return jnp.concatenate([tail, q, q], axis=0)


def group_total(packets, tail, conv_weight):
    heads = packets[0].shape[0]
    tails = [] if tail is None else [tail]
    return pl.pallas_call(
        functools.partial(total_kernel, tail is not None),
        in_specs=[VMEM] * (GROUP + len(tails) + 1),
        out_specs=VMEM,
        out_shape=jax.ShapeDtypeStruct((heads, HDIM + TAIL, HDIM), BF16),
        scratch_shapes=[pltpu.VMEM((GROUP, heads, AUX, HDIM), BF16)],
        compiler_params=pltpu.CompilerParams(vmem_limit_bytes=8 << 20),
        name="group_total",
    )(*packets, *tails, conv_weight)


def edge_features(own, before, wq, wk, wv):
    kf, vf = edge_kv(own, before, wk, wv)
    qf = silu_of_twice(edge_rows(own[16:24], before[16:24], wq * 0.5)) * SCALE
    blank = jnp.zeros((8, HDIM), F32)
    qf, kf, vf = (a.astype(BF16).astype(F32) for a in (edge_only(qf), kf, vf))
    inner = blank
    for back in range(CONV - 1):
        scores = jnp.sum(qf * pltpu.roll(kf, back, 0), axis=1, keepdims=True)
        inner = inner + scores.astype(BF16).astype(F32) * pltpu.roll(vf, back, 0)
    qf, kf, vf = (jnp.concatenate([a, blank], axis=0).astype(BF16) for a in (qf, kf, vf))
    return qf, jnp.concatenate([inner, blank], axis=0), dot(kf, vf, ((0,), (0,)))


def edges_kernel(p0, p1, p2, p3, w_ref, qf_ref, inner_ref, before_ref, with_ref, first_ref, buf):
    gather_packets((p0, p1, p2, p3), buf)
    per = p0.shape[0]
    for h in range(per):
        taps = [taps_of(w_ref, which, member(), h, per) for which in range(3)]
        first_ref[h] = buf[0, h, HDIM:]
        state = buf[0, h, 0:HDIM].astype(F32)
        for t in range(1, GROUP):
            own, before = buf[t, h, HDIM:].astype(F32), buf[t - 1, h, HDIM:].astype(F32)
            qf, inner, first = edge_features(own, before, *taps)
            qf_ref[t - 1, h] = qf
            inner_ref[t - 1, h] = inner
            before_ref[t - 1, h] = state
            state = state + first
            with_ref[t - 1, h] = state
            state = state + buf[t, h, 0:HDIM].astype(F32)


def member_edges(packets, conv_weight):
    heads = packets[0].shape[0]
    later = GROUP - 1
    return pl.pallas_call(
        edges_kernel,
        in_specs=[VMEM] * (GROUP + 1),
        out_specs=[VMEM] * 5,
        out_shape=[
            jax.ShapeDtypeStruct((later, heads, 16, HDIM), BF16),
            jax.ShapeDtypeStruct((later, heads, 16, HDIM), F32),
            jax.ShapeDtypeStruct((later, heads, HDIM, HDIM), F32),
            jax.ShapeDtypeStruct((later, heads, HDIM, HDIM), F32),
            jax.ShapeDtypeStruct((heads, AUX, HDIM), BF16),
        ],
        scratch_shapes=[pltpu.VMEM((GROUP, heads, HDIM + AUX, HDIM), BF16)],
        compiler_params=pltpu.CompilerParams(vmem_limit_bytes=8 << 20),
        name="member_edges",
    )(*packets, conv_weight)


def prefix_kernel(qf_ref, inner_ref, before_ref, with_ref, first_ref, x_ref, w_ref, o0, o1, o2, o3, out):
    later = (group() > 0).astype(F32)
    blank = jnp.zeros((8, HDIM), F32)
    per = x_ref.shape[0]
    for h in range(per):
        taps = [taps_of(w_ref, which, member(), h, per) for which in range(3)]
        base = x_ref[h, 0:HDIM].astype(F32) * later
        tail = unpack_tail(x_ref[h, HDIM:].astype(F32) * later)
        qf, inner, first = edge_features(first_ref[h].astype(F32), tail, *taps)
        prefix = base
        base = base + first
        shifted = base
        for t in range(GROUP):
            if t:
                qf, inner = qf_ref[t - 1, h], inner_ref[t - 1, h]
                prefix = base + before_ref[t - 1, h]
                shifted = base + with_ref[t - 1, h]
            o = inner + dot(qf, prefix.astype(BF16), ((1,), (0,)))
            out[t, h, 0:HDIM] = shifted.astype(BF16)
            out[t, h, HDIM:] = jnp.concatenate([pltpu.roll(o[0:8], 5, 0), blank], axis=0).astype(BF16)
    for j, o_ref in enumerate((o0, o1, o2, o3)):
        o_ref[...] = out[member() ^ j]


def member_prefixes(edges, incoming, conv_weight):
    heads = incoming.shape[0]
    out = jax.ShapeDtypeStruct((heads, HDIM + FIX, HDIM), BF16)
    return pl.pallas_call(
        prefix_kernel,
        in_specs=[VMEM] * (len(edges) + 2),
        out_specs=[VMEM] * GROUP,
        out_shape=[out] * GROUP,
        scratch_shapes=[pltpu.VMEM((GROUP, heads, HDIM + FIX, HDIM), BF16)],
        compiler_params=pltpu.CompilerParams(vmem_limit_bytes=8 << 20),
        name="member_prefixes",
    )(*edges, incoming, conv_weight)


def inner_kernel(quarters, slots, q_ref, w_ref, *refs):
    n = len(quarters)
    kf_refs, vf_refs, (qf_ref, inner_ref) = refs[0:n], refs[n : 2 * n], refs[2 * n :]
    heads, tokens = qf_ref.shape[0:2]
    per = heads // n
    shape = (CHUNK, CHUNK)
    causal = rows_iota(shape) >= lax.broadcasted_iota(jnp.int32, shape, 1)
    for place in range(heads):
        h = (member() ^ quarters[place // per]) * per + place % per
        cols = pl.ds(pl.multiple_of(h * HDIM, HDIM), HDIM)
        wq = w_ref[0, :, cols] * 0.5
        state = None
        for start in range(0, tokens, CHUNK):
            rows = slice(start, start + CHUNK)
            above = q_ref[start - 16 : start, cols] if start else None
            qf = (silu_of_twice(conv_rows(q_ref[rows, cols], above, wq)) * SCALE).astype(BF16)
            qf_ref[place, rows] = qf
            kept = slots[place // per] * per + place % per
            kf, vf = kf_refs[place // per][kept, rows], vf_refs[place // per][kept, rows]
            scores = jnp.where(causal, dot(qf, kf, ((1,), (1,))), 0.0).astype(BF16)
            inner = dot(scores, vf, ((1,), (0,)))
            if state is not None:
                inner = inner + dot(qf, state.astype(BF16), ((1,), (0,)))
            inner_ref[place, rows] = inner
            if start + CHUNK < tokens:
                new = dot(kf, vf, ((0,), (0,)))
                state = new if state is None else state + new


def inner_attention(quarters, queries, kept, conv_weight):
    tokens, width = queries.shape
    count = width // HDIM // GROUP * len(quarters)
    kfs, vfs, slots = zip(*(kept[j] for j in quarters))
    return pl.pallas_call(
        functools.partial(inner_kernel, quarters, slots),
        in_specs=[VMEM] * (2 + 2 * len(quarters)),
        out_specs=[VMEM] * 2,
        out_shape=[
            jax.ShapeDtypeStruct((count, tokens, HDIM), BF16),
            jax.ShapeDtypeStruct((count, tokens, HDIM), F32),
        ],
        compiler_params=pltpu.CompilerParams(vmem_limit_bytes=24 << 20),
        cost_estimate=pl.CostEstimate(
            flops=8 * count * tokens * HDIM * HDIM,
            bytes_accessed=12 * tokens * count * HDIM,
            transcendentals=tokens * count * HDIM,
        ),
        name="inner_attention",
    )(queries, conv_weight, *kfs, *vfs)


def finish_kernel(quarters, places, aliased, gain_ref, *refs):
    n = len(quarters)
    packets, qf_refs, inner_refs, refs = refs[0:n], refs[n : 2 * n], refs[2 * n : 3 * n], refs[3 * n + aliased :]
    out_hbm, out_buf, sem = refs
    per = packets[0].shape[0]
    tokens = out_buf.shape[1]
    part = tokens // PARTS
    there = rows_iota((FIX, HDIM)) < CONV - 1
    copies = []
    for i in range(n):
        quarter = member() ^ quarters[i]
        for c in range(PARTS):
            rows = slice(c * part, (c + 1) * part)
            for h in range(per):
                place = places[i] * per + h
                gain = gain_ref[:, pl.ds(pl.multiple_of((quarter * per + h) * HDIM, HDIM), HDIM)]
                o = inner_refs[i][place, rows] + dot(qf_refs[i][place, rows], packets[i][h, 0:HDIM], ((1,), (0,)))
                if c == 0:
                    fixed = packets[i][h, HDIM:].astype(F32)
                    o = jnp.concatenate([jnp.where(there, fixed, o[0:FIX]), o[FIX:]], axis=0)
                o = o * lax.rsqrt(jnp.mean(o * o, axis=1, keepdims=True) + 1e-06) * gain
                out_buf[i, rows, h * HDIM : (h + 1) * HDIM] = o.astype(BF16)
            cols = pl.ds(pl.multiple_of(quarter * per * HDIM, per * HDIM), per * HDIM)
            copies.append(pltpu.make_async_copy(out_buf.at[i, rows], out_hbm.at[rows, cols], sem.at[i, c]))
            copies[-1].start()
    for copy in copies:
        copy.wait()


def finish(quarters, prefixes, pieces, places, gain, begun=None):
    tokens = pieces[0][0].shape[1]
    width = gain.shape[1]
    n = len(quarters)
    others = [] if begun is None else [begun]
    return pl.pallas_call(
        functools.partial(finish_kernel, quarters, places, len(others)),
        in_specs=[VMEM] * (1 + 3 * n) + [HBM] * len(others),
        out_specs=HBM,
        out_shape=jax.ShapeDtypeStruct((tokens, width), BF16),
        input_output_aliases={1 + 3 * n: 0} if others else {},
        scratch_shapes=[
            pltpu.VMEM((n, tokens, width // GROUP), BF16),
            pltpu.SemaphoreType.DMA((n, PARTS)),
        ],
        compiler_params=pltpu.CompilerParams(vmem_limit_bytes=24 << 20),
        cost_estimate=pl.CostEstimate(
            flops=2 * n * tokens * width // GROUP * HDIM,
            bytes_accessed=8 * n * tokens * width // GROUP,
            transcendentals=n * tokens * width // GROUP // HDIM,
        ),
        name="finish",
    )(gain, *prefixes, *[p[0] for p in pieces], *[p[1] for p in pieces], *others)


def swapped(value, bits):
    count = lax.axis_size("ctx")
    return lax.ppermute(value, "ctx", [(s, s ^ bits) for s in range(count)])


def to_next_group(value):
    count = lax.axis_size("ctx")
    return lax.ppermute(value, "ctx", [(s, s + GROUP) for s in range(count - GROUP)])


def body(queries, key_rows, value_rows, conv_weight, head_gain):
    width = queries.shape[1]
    heads = width // GROUP // HDIM
    groups = lax.axis_size("ctx") // GROUP
    gain = head_gain.reshape(1, width)
    order = (3, 2, 1)
    kf, vf, early, k_rest, v_rest, queries, conv_weight = early_states(
        order + (0,), queries, key_rows, value_rows, conv_weight
    )
    kept = {j: (kf, vf, n) for n, j in enumerate(order)}
    sent = [swapped(early[n * heads : (n + 1) * heads], j) for n, j in enumerate(order)]
    kf, vf, own = own_states(k_rest, v_rest, queries, conv_weight)
    kept[0] = (kf, vf, 0)

    def beside(quarters, arrays):
        piece = inner_attention(quarters, queries, kept, conv_weight)
        return lax.optimization_barrier((arrays, piece))

    sent, piece_a = beside((0, 3), sent[::-1])
    packets = [own] + sent
    if groups == 2:
        incoming = swapped(group_total(packets, None, conv_weight), GROUP)
    else:
        last = jnp.stack(packets)[member() ^ (GROUP - 1)][:, HDIM:]
        tail = to_next_group(last)
        total = group_total(packets, tail, conv_weight)[:, 0:HDIM].astype(F32)
        tail = jnp.concatenate([tail[:, 21:24], tail[:, 3:16]], axis=1)
        prefix, passed = jnp.zeros_like(total), total
        for _ in range(groups - 1):
            prefix = to_next_group(passed)
            passed = prefix + total
        incoming = jnp.concatenate([prefix.astype(BF16), tail], axis=1)
    edges = member_edges(packets, conv_weight)
    (incoming, edges), piece_b = beside((2, 1), (incoming, edges))
    sends = member_prefixes(edges, incoming, conv_weight)
    out = finish((0,), [sends[0]], [piece_a], (0,), gain)
    far, near = swapped(sends[3], 3), [swapped(sends[j], j) for j in (2, 1)]
    far, out = lax.optimization_barrier((far, out))
    out = finish((3,), [far], [piece_a], (1,), gain, out)
    return finish((2, 1), near, [piece_b, piece_b], (0, 1), gain, out)


def solution(mesh):
    return jax.shard_map(
        body,
        mesh=mesh,
        in_specs=(
            P(("mp", "ctx"), None),
            P(("mp", "ctx"), None),
            P(("mp", "ctx"), None),
            P("mp", None, None),
            P("mp"),
        ),
        out_specs=P(("mp", "ctx"), None),
        check_vma=False,
    )
```

```python
import functools

import jax
import jax.numpy as jnp
from jax import lax
from jax.experimental import pallas as pl
from jax.experimental.pallas import tpu as pltpu
from jax.sharding import PartitionSpec as P

HDIM = 128
CONV = 4
GROUP = 4
ROWS = 64
CHUNK = 256
PARTS = 4
AUX = 32
TAIL = 16
FIX = 16
SCALE = HDIM ** (-0.5)
F32, BF16 = jnp.float32, jnp.bfloat16


def member():
    return lax.rem(lax.axis_index("ctx"), GROUP)


def group():
    return lax.div(lax.axis_index("ctx"), GROUP)


def rows_iota(shape):
    return lax.broadcasted_iota(jnp.int32, shape, 0)


def dot(a, b, dims):
    return lax.dot_general(a, b, (dims, ((), ())), preferred_element_type=F32)


def conv_rows(x, earlier, taps):
    x = x.astype(F32)
    earlier = jnp.zeros((8, HDIM), F32) if earlier is None else earlier.astype(F32)[8:16]
    x = jnp.concatenate([earlier, x], axis=0)
    x1 = pltpu.roll(x, 1, 0)
    late = taps[3:4] * x + taps[2:3] * x1
    early = taps[1:2] * x + taps[0:1] * x1
    return (late + pltpu.roll(early, 2, 0))[8:]


def silu_of_twice(half):
    return half + half * jnp.tanh(half)


def merged_rows(first16, last16):
    first = first16.astype(F32)[0:8]
    last = last16.astype(F32)[8:16]
    return jnp.where(rows_iota((8, HDIM)) < 4, first, last)


def conv_from(wide, rows, taps):
    at = lambda back: wide[rows.start + 8 - back : rows.stop + 8 - back]
    return (taps[3:4] * at(0) + taps[2:3] * at(1)) + (taps[1:2] * at(2) + taps[0:1] * at(3))


def heads_of(quarter, per):
    return [pl.ds(pl.multiple_of((quarter * per + u) * HDIM, HDIM), HDIM) for u in range(per)]


def key_features(n, quarter, k_ref, w_ref, kf_ref, wide):
    tokens, per = k_ref.shape[1], k_ref.shape[2] // HDIM
    for u, cols in enumerate(heads_of(quarter, per)):
        wk = w_ref[1, :, cols] * 0.5
        for start in range(0, tokens, ROWS):
            rows = slice(start, start + ROWS)
            wide[n, u, 0, start + 8 : start + 8 + ROWS] = k_ref[n, rows, u * HDIM : (u + 1) * HDIM].astype(F32)
            kf = silu_of_twice(conv_from(wide.at[n, u, 0], rows, wk))
            if start == 0:
                kf = jnp.where(rows_iota(kf.shape) < CONV - 1, 0.0, kf)
            kf_ref[n * per + u, rows] = kf.astype(BF16)


def states(n, quarter, k_ref, v_ref, w_ref, kf_ref, vf_ref, msg_ref, wide):
    tokens, per = v_ref.shape[1], v_ref.shape[2] // HDIM
    for u, cols in enumerate(heads_of(quarter, per)):
        own = slice(u * HDIM, (u + 1) * HDIM)
        wv = w_ref[2, :, cols]
        local = jnp.zeros((HDIM, HDIM), F32)
        for start in range(0, tokens, ROWS):
            rows = slice(start, start + ROWS)
            wide[n, u, 1, start + 8 : start + 8 + ROWS] = v_ref[n, rows, own].astype(F32)
            vf = conv_from(wide.at[n, u, 1], rows, wv).astype(BF16)
            vf_ref[n * per + u, rows] = vf
            local = local + dot(kf_ref[n * per + u, rows], vf, ((0,), (0,)))
        msg_ref[n * per + u, 0:HDIM] = local.astype(BF16)
        mk = merged_rows(k_ref[n, 0:16, own], k_ref[n, tokens - 16 : tokens, own])
        mv = merged_rows(v_ref[n, 0:16, own], v_ref[n, tokens - 16 : tokens, own])
        msg_ref[n * per + u, HDIM : HDIM + 16] = jnp.concatenate([mk, mv], axis=0).astype(BF16)


def query_rows(n, quarter, per, q_ref, msg_ref):
    tokens = q_ref.shape[0]
    for u, cols in enumerate(heads_of(quarter, per)):
        mq = merged_rows(q_ref[0:16, cols], q_ref[tokens - 16 : tokens, cols])
        msg_ref[n * per + u, HDIM + 16 : HDIM + 32] = jnp.concatenate([mq, mq], axis=0).astype(BF16)


def clear_above(wide):
    for n in range(wide.shape[0]):
        for u in range(wide.shape[1]):
            for a in range(2):
                wide[n, u, a, 0:8] = jnp.zeros((8, HDIM), F32)


def early_kernel(quarters, q_hbm, k_hbm, v_hbm, w_hbm, kf_ref, vf_ref, msg_ref, k_rest, v_rest, q_ref, w_ref, k_buf, v_buf, wide, k_sem, v_sem, sem):
    count, tokens, part = k_buf.shape
    per = part // HDIM
    mine = [member() ^ j for j in quarters]

    def fetch(source, target, rest, semaphore, n):
        cols = pl.ds(pl.multiple_of(mine[n] * part, part), part)
        place = target.at[n] if n < count else rest.at[0]
        return pltpu.make_async_copy(source.at[:, cols], place, semaphore.at[n])

    fetch_k = [fetch(k_hbm, k_buf, k_rest, k_sem, n) for n in range(GROUP)]
    fetch_v = [fetch(v_hbm, v_buf, v_rest, v_sem, n) for n in range(GROUP)]
    fetch_taps = pltpu.make_async_copy(w_hbm, w_ref, sem.at[0])
    fetch_queries = pltpu.make_async_copy(q_hbm, q_ref, sem.at[1])

    def keys(n):
        key_features(n, mine[n], k_buf, w_ref, kf_ref, wide)

    def values(n):
        states(n, mine[n], k_buf, v_buf, w_ref, kf_ref, vf_ref, msg_ref, wide)

    for copy in (fetch_taps, fetch_k[0], fetch_v[0], fetch_k[1]):
        copy.start()
    clear_above(wide)
    fetch_taps.wait()
    fetch_k[0].wait()
    for copy in (fetch_v[1], fetch_k[2], fetch_v[2]):
        copy.start()
    keys(0)
    fetch_v[0].wait()
    fetch_k[1].wait()
    for copy in (fetch_k[3], fetch_v[3], fetch_queries):
        copy.start()
    values(0)
    keys(1)
    fetch_v[1].wait()
    fetch_k[2].wait()
    values(1)
    keys(2)
    fetch_v[2].wait()
    values(2)
    fetch_queries.wait()
    for n in range(count):
        query_rows(n, mine[n], per, q_ref, msg_ref)
    fetch_k[3].wait()
    fetch_v[3].wait()


def own_kernel(k_ref, v_ref, q_ref, w_ref, kf_ref, vf_ref, msg_ref, wide):
    per = k_ref.shape[2] // HDIM
    clear_above(wide)
    key_features(0, member(), k_ref, w_ref, kf_ref, wide)
    states(0, member(), k_ref, v_ref, w_ref, kf_ref, vf_ref, msg_ref, wide)
    query_rows(0, member(), per, q_ref, msg_ref)


VMEM = pl.BlockSpec(memory_space=pltpu.VMEM)
HBM = pl.BlockSpec(memory_space=pltpu.HBM)


def state_cost(tokens, width):
    return pl.CostEstimate(flops=2 * tokens * width * HDIM, bytes_accessed=8 * tokens * width, transcendentals=tokens * width)


def early_states(quarters, queries, key_rows, value_rows, conv_weight):
    tokens, width = key_rows.shape
    count, part = len(quarters) - 1, width // GROUP
    per = part // HDIM
    features = jax.ShapeDtypeStruct((count * per, tokens, HDIM), BF16)
    rest = jax.ShapeDtypeStruct((1, tokens, part), BF16)
    arrays = [pltpu.with_memory_space_constraint(a, pltpu.HBM) for a in (queries, key_rows, value_rows, conv_weight)]
    return pl.pallas_call(
        functools.partial(early_kernel, quarters),
        in_specs=[HBM] * 4,
        out_specs=[VMEM] * 7,
        out_shape=[
            features,
            features,
            jax.ShapeDtypeStruct((count * per, HDIM + AUX, HDIM), BF16),
            rest,
            rest,
            jax.ShapeDtypeStruct(queries.shape, BF16),
            jax.ShapeDtypeStruct(conv_weight.shape, F32),
        ],
        scratch_shapes=[
            pltpu.VMEM((count, tokens, part), BF16),
            pltpu.VMEM((count, tokens, part), BF16),
            pltpu.VMEM((count, per, 2, tokens + 8, HDIM), F32),
            pltpu.SemaphoreType.DMA((GROUP,)),
            pltpu.SemaphoreType.DMA((GROUP,)),
            pltpu.SemaphoreType.DMA((2,)),
        ],
        compiler_params=pltpu.CompilerParams(vmem_limit_bytes=28 << 20),
        cost_estimate=state_cost(tokens, width),
        name="early_states",
    )(*arrays)


def own_states(k_rest, v_rest, queries, conv_weight):
    tokens, part = k_rest.shape[1:3]
    per = part // HDIM
    features = jax.ShapeDtypeStruct((per, tokens, HDIM), BF16)
    return pl.pallas_call(
        own_kernel,
        in_specs=[VMEM] * 4,
        out_specs=[VMEM] * 3,
        out_shape=[features, features, jax.ShapeDtypeStruct((per, HDIM + AUX, HDIM), BF16)],
        scratch_shapes=[pltpu.VMEM((1, per, 2, tokens + 8, HDIM), F32)],
        compiler_params=pltpu.CompilerParams(vmem_limit_bytes=16 << 20),
        cost_estimate=state_cost(tokens, part),
        name="own_states",
    )(k_rest, v_rest, queries, conv_weight)


def taps_of(w_ref, which, m, h, per):
    return w_ref[which, :, pl.ds(pl.multiple_of((m * per + h) * HDIM, HDIM), HDIM)]


def edge_rows(own, before, taps):
    z = pltpu.roll(jnp.where(rows_iota((8, HDIM)) < 4, own, before), 3, 0)
    y = taps[3:4] * z
    for back in range(1, CONV):
        y = y + taps[3 - back : 4 - back] * pltpu.roll(z, back, 0)
    return y


def edge_only(y):
    rows = rows_iota(y.shape)
    return jnp.where((rows >= 3) & (rows < 6), y, 0.0)


def edge_kv(own, before, wk, wv):
    kf = silu_of_twice(edge_rows(own[0:8], before[0:8], wk * 0.5))
    vf = edge_rows(own[8:16], before[8:16], wv)
    return edge_only(kf), edge_only(vf)


def gather_packets(packets, buf):
    for j, packet in enumerate(packets):
        buf[member() ^ j] = packet[...]


def gather_edges(packets, buf):
    for j, packet in enumerate(packets):
        buf[member() ^ j] = packet[:, HDIM:]


def total_kernel(has_tail, *refs):
    packets, refs = refs[:GROUP], refs[GROUP:]
    if has_tail:
        tail_ref, refs = refs[0], refs[1:]
    w_ref, out_ref, buf = refs
    gather_edges(packets, buf)
    per = out_ref.shape[0]
    for h in range(per):
        wk, wv = (taps_of(w_ref, which, member(), h, per) for which in (1, 2))
        before = tail_ref[h].astype(F32) if has_tail else jnp.zeros((AUX, HDIM), F32)
        kfs, vfs = [], []
        total = sum(packet[h, 0:HDIM].astype(F32) for packet in packets)
        for t in range(GROUP):
            own = buf[t, h].astype(F32)
            kf, vf = edge_kv(own, before, wk, wv)
            kfs.append(kf)
            vfs.append(vf)
            before = own
        kf = jnp.concatenate(kfs, axis=0).astype(BF16)
        vf = jnp.concatenate(vfs, axis=0).astype(BF16)
        total = total + dot(kf, vf, ((0,), (0,)))
        out_ref[h, 0:HDIM] = total.astype(BF16)
        out_ref[h, HDIM:] = pack_tail(before).astype(BF16)


def pack_tail(raw):
    k = jnp.where(rows_iota((8, HDIM)) < 4, pltpu.roll(raw[16:24], 3, 0), raw[0:8])
    return jnp.concatenate([k, raw[8:16]], axis=0)


def unpack_tail(tail):
    q = pltpu.roll(tail[0:8], 5, 0)
    return jnp.concatenate([tail, q, q], axis=0)


def group_total(packets, tail, conv_weight):
    heads = packets[0].shape[0]
    tails = [] if tail is None else [tail]
    return pl.pallas_call(
        functools.partial(total_kernel, tail is not None),
        in_specs=[VMEM] * (GROUP + len(tails) + 1),
        out_specs=VMEM,
        out_shape=jax.ShapeDtypeStruct((heads, HDIM + TAIL, HDIM), BF16),
        scratch_shapes=[pltpu.VMEM((GROUP, heads, AUX, HDIM), BF16)],
        compiler_params=pltpu.CompilerParams(vmem_limit_bytes=8 << 20),
        name="group_total",
    )(*packets, *tails, conv_weight)


def edge_features(own, before, wq, wk, wv):
    kf, vf = edge_kv(own, before, wk, wv)
    qf = silu_of_twice(edge_rows(own[16:24], before[16:24], wq * 0.5)) * SCALE
    blank = jnp.zeros((8, HDIM), F32)
    qf, kf, vf = (a.astype(BF16).astype(F32) for a in (edge_only(qf), kf, vf))
    inner = blank
    for back in range(CONV - 1):
        scores = jnp.sum(qf * pltpu.roll(kf, back, 0), axis=1, keepdims=True)
        inner = inner + scores.astype(BF16).astype(F32) * pltpu.roll(vf, back, 0)
    qf, kf, vf = (jnp.concatenate([a, blank], axis=0).astype(BF16) for a in (qf, kf, vf))
    return qf, jnp.concatenate([inner, blank], axis=0), dot(kf, vf, ((0,), (0,)))


def edges_kernel(p0, p1, p2, p3, w_ref, qf_ref, inner_ref, before_ref, with_ref, first_ref, buf):
    gather_packets((p0, p1, p2, p3), buf)
    per = p0.shape[0]
    for h in range(per):
        taps = [taps_of(w_ref, which, member(), h, per) for which in range(3)]
        first_ref[h] = buf[0, h, HDIM:]
        state = buf[0, h, 0:HDIM].astype(F32)
        for t in range(1, GROUP):
            own, before = buf[t, h, HDIM:].astype(F32), buf[t - 1, h, HDIM:].astype(F32)
            qf, inner, first = edge_features(own, before, *taps)
            qf_ref[t - 1, h] = qf
            inner_ref[t - 1, h] = inner
            before_ref[t - 1, h] = state
            state = state + first
            with_ref[t - 1, h] = state
            state = state + buf[t, h, 0:HDIM].astype(F32)


def member_edges(packets, conv_weight):
    heads = packets[0].shape[0]
    later = GROUP - 1
    return pl.pallas_call(
        edges_kernel,
        in_specs=[VMEM] * (GROUP + 1),
        out_specs=[VMEM] * 5,
        out_shape=[
            jax.ShapeDtypeStruct((later, heads, 16, HDIM), BF16),
            jax.ShapeDtypeStruct((later, heads, 16, HDIM), F32),
            jax.ShapeDtypeStruct((later, heads, HDIM, HDIM), F32),
            jax.ShapeDtypeStruct((later, heads, HDIM, HDIM), F32),
            jax.ShapeDtypeStruct((heads, AUX, HDIM), BF16),
        ],
        scratch_shapes=[pltpu.VMEM((GROUP, heads, HDIM + AUX, HDIM), BF16)],
        compiler_params=pltpu.CompilerParams(vmem_limit_bytes=8 << 20),
        name="member_edges",
    )(*packets, conv_weight)


def prefix_kernel(qf_ref, inner_ref, before_ref, with_ref, first_ref, x_ref, w_ref, o0, o1, o2, o3, out):
    later = (group() > 0).astype(F32)
    blank = jnp.zeros((8, HDIM), F32)
    per = x_ref.shape[0]
    for h in range(per):
        taps = [taps_of(w_ref, which, member(), h, per) for which in range(3)]
        base = x_ref[h, 0:HDIM].astype(F32) * later
        tail = unpack_tail(x_ref[h, HDIM:].astype(F32) * later)
        qf, inner, first = edge_features(first_ref[h].astype(F32), tail, *taps)
        prefix = base
        base = base + first
        shifted = base
        for t in range(GROUP):
            if t:
                qf, inner = qf_ref[t - 1, h], inner_ref[t - 1, h]
                prefix = base + before_ref[t - 1, h]
                shifted = base + with_ref[t - 1, h]
            o = inner + dot(qf, prefix.astype(BF16), ((1,), (0,)))
            out[t, h, 0:HDIM] = shifted.astype(BF16)
            out[t, h, HDIM:] = jnp.concatenate([pltpu.roll(o[0:8], 5, 0), blank], axis=0).astype(BF16)
    for j, o_ref in enumerate((o0, o1, o2, o3)):
        o_ref[...] = out[member() ^ j]


def member_prefixes(edges, incoming, conv_weight):
    heads = incoming.shape[0]
    out = jax.ShapeDtypeStruct((heads, HDIM + FIX, HDIM), BF16)
    return pl.pallas_call(
        prefix_kernel,
        in_specs=[VMEM] * (len(edges) + 2),
        out_specs=[VMEM] * GROUP,
        out_shape=[out] * GROUP,
        scratch_shapes=[pltpu.VMEM((GROUP, heads, HDIM + FIX, HDIM), BF16)],
        compiler_params=pltpu.CompilerParams(vmem_limit_bytes=8 << 20),
        name="member_prefixes",
    )(*edges, incoming, conv_weight)


def inner_kernel(quarters, slots, q_ref, w_ref, *refs):
    n = len(quarters)
    kf_refs, vf_refs, (qf_ref, inner_ref) = refs[0:n], refs[n : 2 * n], refs[2 * n :]
    heads, tokens = qf_ref.shape[0:2]
    per = heads // n
    shape = (CHUNK, CHUNK)
    causal = rows_iota(shape) >= lax.broadcasted_iota(jnp.int32, shape, 1)
    for place in range(heads):
        h = (member() ^ quarters[place // per]) * per + place % per
        cols = pl.ds(pl.multiple_of(h * HDIM, HDIM), HDIM)
        wq = w_ref[0, :, cols] * 0.5
        state = None
        for start in range(0, tokens, CHUNK):
            rows = slice(start, start + CHUNK)
            above = q_ref[start - 16 : start, cols] if start else None
            qf = (silu_of_twice(conv_rows(q_ref[rows, cols], above, wq)) * SCALE).astype(BF16)
            qf_ref[place, rows] = qf
            kept = slots[place // per] * per + place % per
            kf, vf = kf_refs[place // per][kept, rows], vf_refs[place // per][kept, rows]
            scores = jnp.where(causal, dot(qf, kf, ((1,), (1,))), 0.0).astype(BF16)
            inner = dot(scores, vf, ((1,), (0,)))
            if state is not None:
                inner = inner + dot(qf, state.astype(BF16), ((1,), (0,)))
            inner_ref[place, rows] = inner
            if start + CHUNK < tokens:
                new = dot(kf, vf, ((0,), (0,)))
                state = new if state is None else state + new


def inner_attention(quarters, queries, kept, conv_weight):
    tokens, width = queries.shape
    count = width // HDIM // GROUP * len(quarters)
    kfs, vfs, slots = zip(*(kept[j] for j in quarters))
    return pl.pallas_call(
        functools.partial(inner_kernel, quarters, slots),
        in_specs=[VMEM] * (2 + 2 * len(quarters)),
        out_specs=[VMEM] * 2,
        out_shape=[
            jax.ShapeDtypeStruct((count, tokens, HDIM), BF16),
            jax.ShapeDtypeStruct((count, tokens, HDIM), F32),
        ],
        compiler_params=pltpu.CompilerParams(vmem_limit_bytes=24 << 20),
        cost_estimate=pl.CostEstimate(
            flops=8 * count * tokens * HDIM * HDIM,
            bytes_accessed=12 * tokens * count * HDIM,
            transcendentals=tokens * count * HDIM,
        ),
        name="inner_attention",
    )(queries, conv_weight, *kfs, *vfs)


def finish_kernel(quarters, places, aliased, gain_ref, *refs):
    n = len(quarters)
    packets, qf_refs, inner_refs, refs = refs[0:n], refs[n : 2 * n], refs[2 * n : 3 * n], refs[3 * n + aliased :]
    out_hbm, out_buf, sem = refs
    per = packets[0].shape[0]
    tokens = out_buf.shape[1]
    part = tokens // PARTS
    there = rows_iota((FIX, HDIM)) < CONV - 1
    copies = []
    for i in range(n):
        quarter = member() ^ quarters[i]
        for c in range(PARTS):
            rows = slice(c * part, (c + 1) * part)
            for h in range(per):
                place = places[i] * per + h
                gain = gain_ref[:, pl.ds(pl.multiple_of((quarter * per + h) * HDIM, HDIM), HDIM)]
                o = inner_refs[i][place, rows] + dot(qf_refs[i][place, rows], packets[i][h, 0:HDIM], ((1,), (0,)))
                if c == 0:
                    fixed = packets[i][h, HDIM:].astype(F32)
                    o = jnp.concatenate([jnp.where(there, fixed, o[0:FIX]), o[FIX:]], axis=0)
                o = o * lax.rsqrt(jnp.mean(o * o, axis=1, keepdims=True) + 1e-06) * gain
                out_buf[i, rows, h * HDIM : (h + 1) * HDIM] = o.astype(BF16)
            cols = pl.ds(pl.multiple_of(quarter * per * HDIM, per * HDIM), per * HDIM)
            copies.append(pltpu.make_async_copy(out_buf.at[i, rows], out_hbm.at[rows, cols], sem.at[i, c]))
            copies[-1].start()
    for copy in copies:
        copy.wait()


def finish(quarters, prefixes, pieces, places, gain, begun=None):
    tokens = pieces[0][0].shape[1]
    width = gain.shape[1]
    n = len(quarters)
    others = [] if begun is None else [begun]
    return pl.pallas_call(
        functools.partial(finish_kernel, quarters, places, len(others)),
        in_specs=[VMEM] * (1 + 3 * n) + [HBM] * len(others),
        out_specs=HBM,
        out_shape=jax.ShapeDtypeStruct((tokens, width), BF16),
        input_output_aliases={1 + 3 * n: 0} if others else {},
        scratch_shapes=[
            pltpu.VMEM((n, tokens, width // GROUP), BF16),
            pltpu.SemaphoreType.DMA((n, PARTS)),
        ],
        compiler_params=pltpu.CompilerParams(vmem_limit_bytes=24 << 20),
        cost_estimate=pl.CostEstimate(
            flops=2 * n * tokens * width // GROUP * HDIM,
            bytes_accessed=8 * n * tokens * width // GROUP,
            transcendentals=n * tokens * width // GROUP // HDIM,
        ),
        name="finish",
    )(gain, *prefixes, *[p[0] for p in pieces], *[p[1] for p in pieces], *others)


def swapped(value, bits):
    count = lax.axis_size("ctx")
    return lax.ppermute(value, "ctx", [(s, s ^ bits) for s in range(count)])


def to_next_group(value):
    count = lax.axis_size("ctx")
    return lax.ppermute(value, "ctx", [(s, s + GROUP) for s in range(count - GROUP)])


def body(queries, key_rows, value_rows, conv_weight, head_gain):
    width = queries.shape[1]
    heads = width // GROUP // HDIM
    groups = lax.axis_size("ctx") // GROUP
    gain = head_gain.reshape(1, width)
    order = (3, 2, 1)
    kf, vf, early, k_rest, v_rest, queries, conv_weight = early_states(
        order + (0,), queries, key_rows, value_rows, conv_weight
    )
    kept = {j: (kf, vf, n) for n, j in enumerate(order)}
    sent = [swapped(early[n * heads : (n + 1) * heads], j) for n, j in enumerate(order)]
    kf, vf, own = own_states(k_rest, v_rest, queries, conv_weight)
    kept[0] = (kf, vf, 0)

    def beside(quarters, arrays):
        piece = inner_attention(quarters, queries, kept, conv_weight)
        return lax.optimization_barrier((arrays, piece))

    sent, piece_a = beside((0, 3), sent[::-1])
    packets = [own] + sent
    if groups == 2:
        incoming = swapped(group_total(packets, None, conv_weight), GROUP)
    else:
        last = jnp.stack(packets)[member() ^ (GROUP - 1)][:, HDIM:]
        tail = to_next_group(last)
        total = group_total(packets, tail, conv_weight)[:, 0:HDIM].astype(F32)
        tail = jnp.concatenate([tail[:, 21:24], tail[:, 3:16]], axis=1)
        prefix, passed = jnp.zeros_like(total), total
        for _ in range(groups - 1):
            prefix = to_next_group(passed)
            passed = prefix + total
        incoming = jnp.concatenate([prefix.astype(BF16), tail], axis=1)
    edges = member_edges(packets, conv_weight)
    (incoming, edges), piece_b = beside((2, 1), (incoming, edges))
    sends = member_prefixes(edges, incoming, conv_weight)
    far, near = swapped(sends[3], 3), [swapped(sends[j], j) for j in (2, 1)]
    out = finish((0, 3), [sends[0], far], [piece_a, piece_a], (0, 1), gain)
    return finish((2, 1), near, [piece_b, piece_b], (0, 1), gain, out)


def solution(mesh):
    return jax.shard_map(
        body,
        mesh=mesh,
        in_specs=(
            P(("mp", "ctx"), None),
            P(("mp", "ctx"), None),
            P(("mp", "ctx"), None),
            P("mp", None, None),
            P("mp"),
        ),
        out_specs=P(("mp", "ctx"), None),
        check_vma=False,
    )
```
